512 devices in a mesh: wide: 64 (over z_lo, y, core), narrow: 8 (over x, z_hi).
Axes of the slice: x: 4, y: 8, z: 8 (z_hi: 2, z_lo: 4; z = z_hi * 4 + z_lo), core: 2. Of those that a mesh axis runs over, the one named last changes fastest.
Arguments:
- grad: bfloat16 [4096, 16384], P('wide', 'narrow'), may hold values from -6 to 6
- left_codes: int32 [4096, 4096], P('wide', 'narrow'), may hold values from -8 to 7
- left_scales: int32 [4096, 32], P('wide', 'narrow'), may hold values from 2 to 6
- left_error: bfloat16 [4096, 4096], P('wide', 'narrow'), may hold values from -0.0029907227 to 0.0029907227
- right_codes: int32 [16, 1024, 1024], P('narrow', 'wide'), may hold values from -8 to 7
- right_scales: int32 [16, 1024, 8], P('narrow', 'wide'), may hold values from 3 to 7
- right_error: bfloat16 [16, 1024, 1024], P('narrow', 'wide'), may hold values from -0.0059814453 to 0.0059814453
- first_moment: float32 [8, 2048, 4096], P(None, 'wide', 'narrow'), may hold values from -6 to 6
- second_moment: float32 [8, 2048, 4096], P(None, 'wide', 'narrow'), may hold values from 0.5 to 4
Outputs:
- update: bfloat16 [4096, 16384], P('wide', 'narrow')
- new_first: float32 [8, 2048, 4096], P(None, 'wide', 'narrow')
- new_second: float32 [8, 2048, 4096], P(None, 'wide', 'narrow')
The draws below stay inside these ranges and needn't reach their ends.
All inputs are finite; a program needn't handle non-finite values.
Results may differ from the reference program's by a relative error of at most 0.007.
Values may be sent and summed in bfloat16 or wider, within the bound.
A program may use at most 64 MiB of HBM per device.

```python
import math
import jax
import jax.numpy as jnp

D = 4096
F = 16384
BLOCK = 1024
SCALE_GROUP = 128
SLAB = 2048
N_NARROW = 8


def place_ends(values, stream_key, smallest, top_value):
    dims = values.shape
    place = [jax.random.randint(jax.random.fold_in(stream_key, axis), (), 0, dims[axis]) for axis in range(len(dims))]
    values = values.at[tuple(place)].set(smallest)
    longest = dims.index(max(dims))
    place[longest] = (place[longest] + 1) % dims[longest]
    return values.at[tuple(place)].set(top_value)


def shard_levels(rng, dims, pieces, smallest, largest):
    factor_of, own = 1.0, jax.random.fold_in(rng, 6)
    for dim, blocks in pieces:
        draws = jnp.exp(jax.random.uniform(jax.random.fold_in(own, dim), (blocks,), jnp.float32, smallest / len(pieces), largest / len(pieces)))
        factor_of = factor_of * jnp.repeat(draws, dims[dim] // blocks).reshape([-1 if axis == dim else 1 for axis in range(len(dims))])
    return factor_of


def bell_draw(stream_key, dims, scale, bound, pieces=(), held_as=jnp.bfloat16):
    result = jax.random.normal(stream_key, dims, jnp.float32) * scale
    if len(pieces) > 0:
        result = shard_levels(stream_key, dims, pieces, -0.22, 0.18) * result
    return jnp.clip(result, min=-bound, max=bound).astype(held_as)


def setup_inputs(seed: int = 0) -> dict:
    keys = jax.random.split(jax.random.key(seed), 10)
    return {
        "grad": bell_draw(keys[0], (D, F), 1.0, 6.0, ((0, 64), (1, 8))),
        "left_codes": place_ends(jax.random.randint(keys[1], (D, D), -8, 8), jax.random.fold_in(keys[1], 1), -8, 7).astype(jnp.int32),
        "left_scales": place_ends(jax.random.randint(keys[2], (D, D // SCALE_GROUP), 2, 7), jax.random.fold_in(keys[2], 1), 2, 6).astype(jnp.int32),
        "left_error": jnp.clip(jax.random.uniform(keys[3], (D, D), jnp.float32, -0.0029907227, 0.0029907227) * shard_levels(keys[3], (D, D), ((0, 64), (1, 8)), -0.4, 0.0), -0.0029907227, 0.0029907227).astype(jnp.bfloat16),
        "right_codes": place_ends(jax.random.randint(keys[4], (F // BLOCK, BLOCK, BLOCK), -8, 8), jax.random.fold_in(keys[4], 1), -8, 7).astype(jnp.int32),
        "right_scales": place_ends(jax.random.randint(keys[5], (F // BLOCK, BLOCK, BLOCK // SCALE_GROUP), 3, 8), jax.random.fold_in(keys[5], 1), 3, 7).astype(jnp.int32),
        "right_error": jnp.clip(jax.random.uniform(keys[6], (F // BLOCK, BLOCK, BLOCK), jnp.float32, -0.0059814453, 0.0059814453) * shard_levels(keys[6], (F // BLOCK, BLOCK, BLOCK), ((0, 8), (1, 64)), -0.4, 0.0), -0.0059814453, 0.0059814453).astype(jnp.bfloat16),
        "first_moment": bell_draw(keys[7], (N_NARROW, SLAB, D), 1.0, 6.0, ((1, 64), (2, 8)), jnp.float32),
        "second_moment": jnp.clip(jnp.exp(math.log(4.0) - 2.0794415 * jax.random.uniform(keys[8], (N_NARROW, SLAB, D), jnp.float32) ** shard_levels(keys[8], (N_NARROW, SLAB, D), ((1, 64), (2, 8)), -0.2, 0.2)), 0.5, 4.0),
    }


BETA_ONE = 0.95
BETA_TWO = 0.95
EPSILON = 1e-08

def dequantize(code_array, scale_array, error_array, quantum):
    expanded = jnp.repeat(scale_array, SCALE_GROUP, axis=-1)
    values = code_array.astype(jnp.float32) * expanded.astype(jnp.float32) * quantum
    return (values + error_array.astype(jnp.float32)).astype(jnp.bfloat16)

def reference(grad, left_codes, left_scales, left_error, right_codes, right_scales, right_error, first_moment, second_moment):
    left_basis = dequantize(left_codes, left_scales, left_error, 1.0 / (16.0 * math.sqrt(D)))
    right_basis = dequantize(right_codes, right_scales, right_error, 1.0 / (16.0 * math.sqrt(BLOCK)))
    block_count = F // BLOCK
    blocked = grad.reshape(D, block_count, BLOCK).astype(jnp.float32)
    half_turned = jnp.einsum('rbk,bkj->rbj', blocked, right_basis.astype(jnp.float32))
    half_turned = half_turned.astype(jnp.bfloat16).reshape(D, F)
    rotated = jnp.dot(left_basis.T, half_turned, preferred_element_type=jnp.float32)
    rotated_slabs = rotated.T.reshape(N_NARROW, F // N_NARROW, D)
    new_first = BETA_ONE * first_moment + (1.0 - BETA_ONE) * rotated_slabs
    new_second = BETA_TWO * second_moment + (1.0 - BETA_TWO) * rotated_slabs * rotated_slabs
    direction = (new_first / (jnp.sqrt(new_second) + EPSILON)).astype(jnp.bfloat16)
    back_turned = jnp.dot(left_basis, direction.reshape(F, D).T, preferred_element_type=jnp.float32)
    back_turned = back_turned.astype(jnp.bfloat16).reshape(D, block_count, BLOCK).astype(jnp.float32)
    update = jnp.einsum('rbk,bjk->rbj', back_turned, right_basis.astype(jnp.float32))
    return (update.reshape(D, F).astype(jnp.bfloat16), new_first, new_second)
```

```python
import functools
import math

import jax
import jax.numpy as jnp
from jax import lax
from jax.experimental import pallas as pl
from jax.experimental.pallas import tpu as pltpu
from jax.sharding import PartitionSpec as P

MESH = pl.DeviceIdType.MESH
F32, BF16 = jnp.float32, jnp.bfloat16
BETA_ONE = 0.95
BETA_TWO = 0.95
EPSILON = 1e-08
GROUP = 128
NX = 4
NH = 2


def dequantized(codes, scales, error, first, width, quantum):
    step = min(width, GROUP)
    pieces = []
    for at in range(first, first + width, step):
        group = at // GROUP
        value = codes[:, at : at + step].astype(F32) * scales[:, group : group + 1].astype(F32) * quantum
        pieces.append((value + error[:, at : at + step].astype(F32)).astype(BF16))
    return pieces[0] if len(pieces) == 1 else jnp.concatenate(pieces, axis=1)


def kernel(
    nz,
    ny,
    grad,
    lcodes,
    lscales,
    lerror,
    rcodes,
    rscales,
    rerror,
    first,
    second,
    update,
    new_first,
    new_second,
    turned,
    right,
    left,
    rstage,
    lstage,
    outgoing,
    slabs,
    total,
    direction,
    partial,
    halfway,
    arrived,
    home,
    back,
    result,
    foreign,
    sib_s,
    sib_r,
    zr_s,
    zr_r,
    zl_s,
    zl_r,
    yr_s,
    yr_r,
    yl_s,
    yl_r,
    share_s,
    share_r,
    out_s,
    out_r,
    back_s,
    back_r,
    own_sem,
    ring_s,
    ring_r,
    sum_s,
    sum_r,
):
    nq = nz * ny
    block = 32 * nq
    order = 128 * nq
    span = lcodes.shape[1]
    half = span // 2
    wide, narrow = lax.axis_index("wide"), lax.axis_index("narrow")
    core, chip = lax.rem(wide, 2), wide // 2
    z, y = chip // ny, lax.rem(chip, ny)
    x, high = narrow // NH, lax.rem(narrow, NH)
    other = 1 - core
    side = wide // nq
    has_own = side == core

    def wide_at(zz, yy, cc):
        return (zz * ny + yy) * 2 + cc

    def copy(src, dst, send, recv, ww, nn):
        return pltpu.make_async_remote_copy(
            src_ref=src, dst_ref=dst, send_sem=send, recv_sem=recv, device_id=(ww, nn), device_id_type=MESH
        )

    sibling = wide + 1 - 2 * core
    y_up, y_down = lax.rem(y + 1, ny), lax.rem(y + ny - 1, ny)
    x_up, x_down = lax.rem(x + 1, NX), lax.rem(x + NX - 1, NX)
    x_far = lax.rem(x + 2, NX)
    n_up, n_down = x_up * NH + high, x_down * NH + high

    barrier = pltpu.get_barrier_semaphore()
    plane = 2 * nq * NH
    me = wide * NH + high

    def greet(i, carry):
        there = lax.rem(me + i, plane)
        pl.semaphore_signal(
            barrier, inc=1, device_id=(there // NH, x * NH + lax.rem(there, NH)), device_id_type=MESH
        )
        return carry

    lax.fori_loop(1, plane, greet, 0)
    for nn in (n_up, n_down):
        pl.semaphore_signal(barrier, inc=1, device_id=(wide, nn), device_id_type=MESH)

    quantum = 1.0 / (16.0 * math.sqrt(block))
    rows16 = pl.ds(pl.multiple_of(core * 16, 16), 16)
    rows64 = pl.ds(pl.multiple_of(core * 64, 64), 64)
    right[z, y, rows16, :] = dequantized(rcodes[core], rscales[core], rerror[core], 0, block, quantum)
    rstage[...] = dequantized(rcodes[other], rscales[other], rerror[other], 0, block, quantum)
    quantum = 1.0 / (16.0 * math.sqrt(order))
    for h in range(2):
        value = dequantized(lcodes[...], lscales[...], lerror[...], h * half, half, quantum)

        @pl.when(core == h)
        def _():
            left[h, z, y, rows64, :] = value
            turned[rows64, :] = grad[:, h * block : (h + 1) * block]

        @pl.when(core != h)
        def _():
            lstage[...] = value

    pl.semaphore_wait(barrier, plane - 1 + 2)

    sib = [
        copy(rstage, right.at[z, y, rows16, :], sib_s.at[0], sib_r.at[0], sibling, narrow),
        copy(lstage, left.at[other, z, y, rows64, :], sib_s.at[1], sib_r.at[1], sibling, narrow),
        copy(
            grad.at[:, pl.ds(pl.multiple_of(other * block, block), block)],
            turned.at[rows64, :],
            sib_s.at[2],
            sib_r.at[2],
            sibling,
            narrow,
        ),
    ]
    for c in sib:
        c.start()

    def along_z(ref, send, recv):
        return [
            copy(ref, ref, send.at[d - 1], recv.at[d - 1], wide_at(lax.rem(z + d, nz), y, core), narrow)
            for d in range(1, nz)
        ]

    zr = along_z(right.at[z, y], zr_s, zr_r)
    zl = along_z(left.at[core, z, y], zl_s, zl_r)
    sib[0].wait_recv()
    for c in zr:
        c.start()
    sib[1].wait_recv()

    def along_y(column, send, recv):
        steps = []
        for t in range(1, ny // 2 + 1):
            up = lax.rem(y + ny - (t - 1), ny)
            down = lax.rem(y + (t - 1), ny)
            zs = (pl.ds(0, nz), pl.ds(0, nz)) if t < ny // 2 else (pl.ds(0, nz // 2), pl.ds(nz // 2, nz // 2))
            a, b = column(zs[0], up), column(zs[1], down)
            steps.append(
                (
                    copy(a, a, send.at[t - 1, 0], recv.at[t - 1, 0], wide_at(z, y_up, core), narrow),
                    copy(b, b, send.at[t - 1, 1], recv.at[t - 1, 1], wide_at(z, y_down, core), narrow),
                )
            )
        return steps

    yr = along_y(lambda zs, yy: right.at[zs, yy], yr_s, yr_r)
    yl = along_y(lambda zs, yy: left.at[core, zs, yy], yl_s, yl_r)
    shares = []

    def share(zs, yy):
        ref = left.at[core, zs, yy]
        at = len(shares)
        c = copy(ref, ref, share_s.at[at], share_r.at[at], sibling, narrow)
        c.start()
        shares.append(c)

    def start(pair):
        for c in pair:
            c.start()

    def landed(pair):
        for c in pair:
            c.wait_recv()

    whole = pl.ds(0, nz)
    landed(zr)
    start(yr[0])
    for c in zl:
        c.start()
    for t in range(1, ny // 2):
        landed(yr[t - 1])
        start(yr[t])
    landed(zl)
    share(whole, y)
    landed(yr[ny // 2 - 1])
    start(yl[0])

    sib[2].wait_recv()
    wide_n = min(256, block)
    for at in range(0, block, wide_n):
        basis = right[:, :, :, at : at + wide_n].reshape(block, wide_n)
        value = jnp.dot(turned[...], basis, preferred_element_type=F32)
        outgoing[at // 32 : (at + wide_n) // 32] = value.T.astype(BF16).reshape(wide_n // 32, 32, 128)

    lands_at = narrow * nq + chip

    def send_out(t, carry):
        j = lax.rem(chip + t, nq)
        to = nq * core + j
        for extra in range(NH):
            nn = x * NH + lax.rem(high + extra, NH)
            c = copy(outgoing.at[j], slabs.at[lands_at], out_s, out_r, to, nn)
            if extra == 0:

                @pl.when(to != wide)
                def _():
                    c.start()

                @pl.when(to == wide)
                def _():
                    pltpu.make_async_copy(outgoing.at[j], slabs.at[lands_at], own_sem.at[0]).start()

            else:
                c.start()
        return carry

    lax.fori_loop(0, nq, send_out, 0)

    mine = x * NH * nq
    count = NH * nq

    def wait_all(ref, base, send, recv, sending):
        @pl.when(has_own)
        def _():
            part = ref.at[pl.ds(base, count - 1)]
            c = copy(part, part, send, recv, sibling, narrow)
            if sending:
                c.wait_send()
            else:
                c.wait_recv()

        @pl.when(jnp.logical_not(has_own))
        def _():
            part = ref.at[pl.ds(base, count)]
            c = copy(part, part, send, recv, sibling, narrow)
            if sending:
                c.wait_send()
            else:
                c.wait_recv()

    def columns_of(t):
        up, down = lax.rem(y + ny - t, ny), lax.rem(y + t, ny)
        return up, down

    def next_left(t):
        landed(yl[t - 1])
        if t < ny // 2:
            start(yl[t])
            for yy in columns_of(t):
                share(whole, yy)
        else:
            share(whole, columns_of(t)[0])

    next_left(1)
    wait_all(slabs, mine, out_s, out_r, False)

    @pl.when(has_own)
    def _():
        pltpu.make_async_copy(outgoing.at[0], slabs.at[lands_at], own_sem.at[0]).wait()

    own = slabs.at[pl.ds(mine, count)]
    from_down = slabs.at[pl.ds(x_down * count, nq)]
    from_up = slabs.at[pl.ds(x_up * count + nq, nq)]
    ring = [
        copy(own, own, ring_s.at[0], ring_r.at[0], wide, n_up),
        copy(own, own, ring_s.at[1], ring_r.at[1], wide, n_down),
        copy(from_down, from_down, ring_s.at[2], ring_r.at[2], wide, n_up),
        copy(from_up, from_up, ring_s.at[3], ring_r.at[3], wide, n_down),
    ]
    start(ring[:2])
    next_left(2)
    landed(ring[:2])
    start(ring[2:])
    for t in range(3, ny // 2 + 1):
        next_left(t)
    landed(ring[2:])
    landed(shares)

    rows = NX * NH * 32
    total[...] = jnp.zeros_like(total)
    deep = 4

    def rotate(i, carry):
        zz, yy = i // (ny // deep), lax.rem(i, ny // deep) * deep
        at = zz * ny + yy
        lhs = jnp.concatenate(
            [
                jnp.concatenate([slabs[s * nq + at + d] for s in range(NX * NH)], axis=0)
                for d in range(deep)
            ],
            axis=1,
        )
        for h in range(2):
            rhs = left[h, zz, pl.ds(yy, deep)].reshape(deep * 128, half)
            total[:, h * half : (h + 1) * half] += jnp.dot(lhs, rhs, preferred_element_type=F32)
        return carry

    lax.fori_loop(0, nq // deep, rotate, 0)

    def moments(s, carry):
        there = pl.ds(pl.multiple_of(s * 32, 32), 32)
        value = total[there, :]
        m = BETA_ONE * first[s] + (1.0 - BETA_ONE) * value
        v = BETA_TWO * second[s] + (1.0 - BETA_TWO) * value * value
        new_first[s] = m
        new_second[s] = v
        direction[there, :] = (m / (jnp.sqrt(v) + EPSILON)).astype(BF16)
        return carry

    lax.fori_loop(0, NX * NH, moments, 0)

    def rotate_back(i, carry):
        zz, yy = i // (ny // 2), lax.rem(i, ny // 2) * 2
        at = zz * ny + yy
        value = None
        for h in range(2):
            rhs = left[h, zz, pl.ds(yy, 2)].reshape(256, half)
            term = lax.dot_general(
                direction[:, h * half : (h + 1) * half],
                rhs,
                (((1,), (1,)), ((), ())),
                preferred_element_type=F32,
            )
            value = term if value is None else value + term
        value = value.astype(BF16)
        for s in range(NX * NH):
            for d in range(2):
                partial[s * nq + at + d] = value[s * 32 : (s + 1) * 32, d * 128 : (d + 1) * 128]
        return carry

    lax.fori_loop(0, nq // 2, rotate_back, 0)

    def part(xx, h):
        return partial.at[pl.ds(xx * count + h * nq, nq)]

    sums = [
        copy(part(x_far, 0), halfway.at[0], sum_s.at[0], sum_r.at[0], wide, n_up),
        copy(part(x_far, 1), halfway.at[1], sum_s.at[1], sum_r.at[1], wide, n_down),
        copy(part(x_up, 1), arrived.at[0, pl.ds(nq, nq)], sum_s.at[2], sum_r.at[2], wide, n_up),
        copy(part(x_down, 0), arrived.at[1, pl.ds(0, nq)], sum_s.at[3], sum_r.at[3], wide, n_down),
        copy(part(x_up, 0), arrived.at[0, pl.ds(0, nq)], sum_s.at[4], sum_r.at[4], wide, n_up),
        copy(part(x_down, 1), arrived.at[1, pl.ds(nq, nq)], sum_s.at[5], sum_r.at[5], wide, n_down),
    ]
    start(sums[:4])
    landed(sums[:2])
    few = min(8, nq)

    def pass_on(i, carry):
        at = i * few
        for h, base in ((0, x_up * count), (1, x_down * count + nq)):
            there = pl.ds(base + at, few)
            partial[there] = (partial[there].astype(F32) + halfway[h, pl.ds(at, few)].astype(F32)).astype(BF16)
        return carry

    lax.fori_loop(0, nq // few, pass_on, 0)
    start(sums[4:])
    landed(sums[2:])

    def add_up(i, carry):
        there = pl.ds(i * few, few)
        value = partial[pl.ds(mine + i * few, few)].astype(F32) + arrived[0, there].astype(F32)
        home[there] = (value + arrived[1, there].astype(F32)).astype(BF16)
        return carry

    lax.fori_loop(0, count // few, add_up, 0)

    goes_to = high * nq + lax.rem(wide, nq)

    def send_back(t, carry):
        qq = lax.rem(chip + t, nq)
        to = 2 * qq + side
        for extra in range(NH):
            hh = lax.rem(high + extra, NH)
            nn = x * NH + hh
            src = home.at[hh * nq + qq]
            c = copy(src, back.at[goes_to], back_s, back_r, to, nn)
            if extra == 0:

                @pl.when(to != wide)
                def _():
                    c.start()

                @pl.when(to == wide)
                def _():
                    pltpu.make_async_copy(src, back.at[goes_to], own_sem.at[1]).start()

            else:
                c.start()
        return carry

    lax.fori_loop(0, nq, send_back, 0)
    wait_all(back, 0, back_s, back_r, False)

    @pl.when(has_own)
    def _():
        pltpu.make_async_copy(home.at[0], back.at[goes_to], own_sem.at[1]).wait()

    turned_back = (back[0:nq].astype(F32) + back[nq : 2 * nq].astype(F32)).astype(BF16).reshape(block, 128)
    tall = ny * 32
    for zz in range(nz):
        value = jnp.dot(right[zz].reshape(tall, block), turned_back, preferred_element_type=F32)
        value = value.T.astype(BF16)
        result[0, :, zz * tall : (zz + 1) * tall] = value[0:64]
        result[1, :, zz * tall : (zz + 1) * tall] = value[64:128]
    last = copy(result.at[other], foreign, sib_s.at[3], sib_r.at[3], sibling, narrow)
    last.start()
    for h in range(2):

        @pl.when(core == h)
        def _():
            update[:, h * block : (h + 1) * block] = result[core]

    last.wait_recv()
    for h in range(2):

        @pl.when(core != h)
        def _():
            update[:, h * block : (h + 1) * block] = foreign[...]

    for c in sib + zr + zl + [c for pair in yr + yl for c in pair] + shares + ring + sums + [last]:
        c.wait_send()
    wait_all(slabs, mine, out_s, out_r, True)
    wait_all(back, 0, back_s, back_r, True)


def solution(mesh):
    nz, ny = 4, mesh.shape["wide"] // 8

    def step(*args):
        return body(nz, ny, *args)

    placed = (
        P("wide", "narrow"),
        P("wide", "narrow"),
        P("wide", "narrow"),
        P("wide", "narrow"),
        P("narrow", "wide", None),
        P("narrow", "wide", None),
        P("narrow", "wide", None),
        P(None, "wide", "narrow"),
        P(None, "wide", "narrow"),
    )
    return jax.shard_map(
        step,
        mesh=mesh,
        in_specs=placed,
        out_specs=(P("wide", "narrow"), P(None, "wide", "narrow"), P(None, "wide", "narrow")),
        check_vma=False,
    )


def body(nz, ny, *args):
    nq = nz * ny
    block, span = 32 * nq, args[1].shape[1]
    half = span // 2
    slabs = NX * NH
    dma = pltpu.SemaphoreType.DMA
    steps = ny // 2
    vmem = pl.BlockSpec(memory_space=pltpu.VMEM)
    return pl.pallas_call(
        functools.partial(kernel, nz, ny),
        out_shape=(
            jax.ShapeDtypeStruct(args[0].shape, BF16),
            jax.ShapeDtypeStruct(args[7].shape, F32),
            jax.ShapeDtypeStruct(args[8].shape, F32),
        ),
        in_specs=[vmem] * 9,
        out_specs=(vmem,) * 3,
        scratch_shapes=[
            pltpu.VMEM((128, block), BF16),
            pltpu.VMEM((nz, ny, 32, block), BF16),
            pltpu.VMEM((2, nz, ny, 128, half), BF16),
            pltpu.VMEM((16, block), BF16),
            pltpu.VMEM((64, half), BF16),
            pltpu.VMEM((nq, 32, 128), BF16),
            pltpu.VMEM((slabs * nq, 32, 128), BF16),
            pltpu.VMEM((slabs * 32, span), F32),
            pltpu.VMEM((slabs * 32, span), BF16),
            pltpu.VMEM((slabs * nq, 32, 128), BF16),
            pltpu.VMEM((2, nq, 32, 128), BF16),
            pltpu.VMEM((2, NH * nq, 32, 128), BF16),
            pltpu.VMEM((NH * nq, 32, 128), BF16),
            pltpu.VMEM((NH * nq, 32, 128), BF16),
            pltpu.VMEM((2, 64, block), BF16),
            pltpu.VMEM((64, block), BF16),
            dma((4,)),
            dma((4,)),
            dma((nz - 1,)),
            dma((nz - 1,)),
            dma((nz - 1,)),
            dma((nz - 1,)),
            dma((steps, 2)),
            dma((steps, 2)),
            dma((steps, 2)),
            dma((steps, 2)),
            dma((ny,)),
            dma((ny,)),
            dma,
            dma,
            dma,
            dma,
            dma((2,)),
            dma((4,)),
            dma((4,)),
            dma((6,)),
            dma((6,)),
        ],
        compiler_params=pltpu.CompilerParams(
            collective_id=0, has_side_effects=True, vmem_limit_bytes=48 * 1024 * 1024
        ),
        cost_estimate=pl.CostEstimate(flops=2_700_000_000, bytes_accessed=8_000_000, transcendentals=131072),
    )(*args)
```

```python
import functools
import math

import jax
import jax.numpy as jnp
from jax import lax
from jax.experimental import pallas as pl
from jax.experimental.pallas import tpu as pltpu
from jax.sharding import PartitionSpec as P

MESH = pl.DeviceIdType.MESH
F32, BF16 = jnp.float32, jnp.bfloat16
BETA_ONE = 0.95
BETA_TWO = 0.95
EPSILON = 1e-08
NX = 4
NH = 2


def dequantized(codes, scales, error, quantum):
    groups, columns = scales.shape[0], codes.shape[1]
    column = lax.broadcasted_iota(jnp.int32, (groups, columns), 1) // (columns // groups)
    spread = (column == lax.broadcasted_iota(jnp.int32, (groups, columns), 0)).astype(F32).astype(BF16)
    expanded = lax.dot_general(
        scales.astype(F32).astype(BF16), spread, (((0,), (0,)), ((), ())), preferred_element_type=F32
    )
    return (codes.astype(F32) * expanded * quantum + error.astype(F32)).astype(BF16)


def kernel(nz, ny, *refs):
    inputs, refs = refs[:9], refs[9:]
    outputs, fetched, held, refs = refs[:3], refs[3:12], refs[12:15], refs[15:]
    update, new_first, new_second = held
    grad, lcodes, lscales, lerror, rcodes, rscales, rerror, first, second = fetched
    (
        turned,
        right,
        left,
        rstage,
        lstage,
        outgoing,
        slabs,
        total,
        direction,
        partial,
        halfway,
        arrived,
        home,
        back,
        result,
        foreign,
    ) = refs[:16]
    (
        fetch_sem,
        sib_s,
        sib_r,
        zr_s,
        zr_r,
        za_s,
        za_r,
        zb_s,
        zb_r,
        yr_s,
        yr_r,
        ya_s,
        ya_r,
        yb_s,
        yb_r,
        share_s,
        share_r,
        out_s,
        out_r,
        back_s,
        back_r,
        own_sem,
        ring_s,
        ring_r,
        sum_s,
        sum_r,
    ) = refs[16:]
    nq = nz * ny
    block = 32 * nq
    order = 128 * nq
    span = lcodes.shape[1]
    half = span // 2
    wide, narrow = lax.axis_index("wide"), lax.axis_index("narrow")
    core, chip = lax.rem(wide, 2), wide // 2
    z, y = chip // ny, lax.rem(chip, ny)
    x, high = narrow // NH, lax.rem(narrow, NH)
    other = 1 - core
    side = wide // nq
    has_own = side == core

    fetches = [pltpu.make_async_copy(a, b, fetch_sem.at[i]) for i, (a, b) in enumerate(zip(inputs, fetched))]
    for i in (4, 5, 6, 1, 2, 3, 0, 7, 8):
        fetches[i].start()

    def wide_at(zz, yy, cc):
        return (zz * ny + yy) * 2 + cc

    def copy(src, dst, send, recv, ww, nn):
        return pltpu.make_async_remote_copy(
            src_ref=src, dst_ref=dst, send_sem=send, recv_sem=recv, device_id=(ww, nn), device_id_type=MESH
        )

    def start(copies):
        for c in copies:
            c.start()

    def landed(copies):
        for c in copies:
            c.wait_recv()

    sibling = wide + 1 - 2 * core
    y_up, y_down = lax.rem(y + 1, ny), lax.rem(y + ny - 1, ny)
    x_up, x_down = lax.rem(x + 1, NX), lax.rem(x + NX - 1, NX)
    x_far = lax.rem(x + 2, NX)
    n_up, n_down = x_up * NH + high, x_down * NH + high
    w_up, w_down = wide_at(z, y_up, core), wide_at(z, y_down, core)

    barrier = pltpu.get_barrier_semaphore()
    plane = 2 * nq * NH
    me = wide * NH + high

    def greet(i, carry):
        there = lax.rem(me + i, plane)
        pl.semaphore_signal(
            barrier, inc=1, device_id=(there // NH, x * NH + lax.rem(there, NH)), device_id_type=MESH
        )
        return carry

    lax.fori_loop(1, plane, greet, 0)
    for nn in (n_up, n_down):
        pl.semaphore_signal(barrier, inc=1, device_id=(wide, nn), device_id_type=MESH)

    rows16 = pl.ds(pl.multiple_of(core * 16, 16), 16)
    rows64 = pl.ds(pl.multiple_of(core * 64, 64), 64)
    quantum = 1.0 / (16.0 * math.sqrt(block))
    for i in (4, 5, 6):
        fetches[i].wait()
    rstage[...] = dequantized(rcodes[other], rscales[other], rerror[other], quantum)
    right[z, y, rows16, :] = dequantized(rcodes[core], rscales[core], rerror[core], quantum)
    pl.semaphore_wait(barrier, plane - 1 + 2)
    sib = [
        copy(rstage, right.at[z, y, rows16, :], sib_s.at[0], sib_r.at[0], sibling, narrow),
        copy(lstage, left.at[other, z, y, rows64, :], sib_s.at[1], sib_r.at[1], sibling, narrow),
        copy(
            grad.at[:, pl.ds(pl.multiple_of(other * block, block), block)],
            turned.at[rows64, :],
            sib_s.at[2],
            sib_r.at[2],
            sibling,
            narrow,
        ),
    ]
    sib[0].start()
    quantum = 1.0 / (16.0 * math.sqrt(order))
    for i in (1, 2, 3):
        fetches[i].wait()
    value = dequantized(lcodes[...], lscales[...], lerror[...], quantum)
    for h in range(2):

        @pl.when(core == h)
        def _():
            left[h, z, y, rows64, :] = value[:, h * half : (h + 1) * half]

        @pl.when(core != h)
        def _():
            lstage[...] = value[:, h * half : (h + 1) * half]

    sib[1].start()

    last = ny // 2

    def along_z(ref, send, recv):
        return [
            copy(ref, ref, send.at[d - 1], recv.at[d - 1], wide_at(lax.rem(z + d, nz), y, core), narrow)
            for d in range(1, nz)
        ]

    def passed(t):
        return lax.rem(y + ny - (t - 1), ny), lax.rem(y + (t - 1), ny)

    nearest = [0, 1, nz - 1][: min(nz, 3)] + list(range(2, nz - 1))
    if nz == 2:
        nearest = [0, 1]
    zr = along_z(right.at[z, y], zr_s, zr_r)

    def ring_right(t, e):
        zz = lax.rem(z + nz - e, nz)
        at = nearest.index(e)
        made = []
        for way, (yy, ww) in enumerate(zip(passed(t), (w_up, w_down))):
            if t < last or (at < nz // 2) == (way == 0):
                ref = right.at[zz, yy]
                made.append(copy(ref, ref, yr_s.at[t - 1, e, way], yr_r.at[t - 1, e, way], ww, narrow))
        return made

    yr = [[ring_right(t, e) for e in nearest] for t in range(1, last + 1)]

    def rows_a(zz, yy):
        return left.at[core, zz, yy, pl.ds(0, 64)]

    def rows_b(zz, yy, begin=0, size=64):
        return left.at[core, zz, yy, pl.ds(64 + begin, size)]

    za = along_z(rows_a(z, y), za_s, za_r)
    zb = along_z(rows_b(z, pl.ds(0, ny)), zb_s, zb_r)
    ya, yb = [], []
    for t in range(1, last + 1):
        up, down = passed(t)
        whole, low, upper = pl.ds(0, nz), pl.ds(0, nz // 2), pl.ds(nz // 2, nz // 2)
        a, b = (rows_a(whole, up), rows_a(whole, down)) if t < last else (rows_a(low, up), rows_a(upper, down))
        ya.append(
            [
                copy(a, a, ya_s.at[t - 1, 0], ya_r.at[t - 1, 0], w_up, narrow),
                copy(b, b, ya_s.at[t - 1, 1], ya_r.at[t - 1, 1], w_down, narrow),
            ]
        )
        a, b = (rows_b(z, up), rows_b(z, down)) if t < last else (rows_b(z, up, 0, 32), rows_b(z, down, 32, 32))
        yb.append(
            [
                copy(a, a, yb_s.at[t - 1, 0], yb_r.at[t - 1, 0], w_up, narrow),
                copy(b, b, yb_s.at[t - 1, 1], yb_r.at[t - 1, 1], w_down, narrow),
            ]
        )
    shares = []

    def share(ref):
        at = len(shares)
        c = copy(ref, ref, share_s.at[at], share_r.at[at], sibling, narrow)
        c.start()
        shares.append(c)

    sib[0].wait_recv()
    start(yr[0][0])
    start(zr)
    sib[1].wait_recv()
    start(yb[0])
    start(za)
    for at, e in enumerate(nearest):
        if at > 0:
            zr[e - 1].wait_recv()
            start(yr[0][at])
    fetches[0].wait()
    for h in range(2):

        @pl.when(core == h)
        def _():
            turned[rows64, :] = grad[:, h * block : (h + 1) * block]

    sib[2].start()
    b_step = 1

    def next_b(t):
        landed(yb[t - 1])
        if t < last:
            start(yb[t])
        else:
            start(zb)
            share(rows_b(z, pl.ds(0, ny)))

    for t in range(2, last + 1):
        for at in range(nz):
            landed(yr[t - 2][at])
            start(yr[t - 1][at])
            if at % 2 == 1 and b_step <= last and t < last:
                next_b(b_step)
                b_step += 1
    while b_step <= last:
        next_b(b_step)
        b_step += 1
    landed(za)
    share(rows_a(pl.ds(0, nz), y))
    for at in range(nz):
        landed(yr[last - 1][at])

    sib[2].wait_recv()
    wide_n = min(256, block)
    for at in range(0, block, wide_n):
        basis = right[:, :, :, at : at + wide_n].reshape(block, wide_n)
        value = jnp.dot(turned[...], basis, preferred_element_type=F32)
        outgoing[at // 32 : (at + wide_n) // 32] = value.T.astype(BF16).reshape(wide_n // 32, 32, 128)

    lands_at = narrow * nq + chip
    high_far = 1 - high
    n_far = x * NH + high_far

    def send_near(t, carry):
        j = lax.rem(chip + t, nq)
        to = nq * core + j

        @pl.when(to != wide)
        def _():
            copy(outgoing.at[j], slabs.at[lands_at], out_s.at[0], out_r.at[0], to, narrow).start()

        @pl.when(to == wide)
        def _():
            pltpu.make_async_copy(outgoing.at[j], slabs.at[lands_at], own_sem.at[0]).start()

        return carry

    def send_far(t, carry):
        j = lax.rem(chip + t, nq)
        copy(outgoing.at[j], slabs.at[lands_at], out_s.at[1], out_r.at[1], nq * core + j, n_far).start()
        return carry

    lax.fori_loop(0, nq, send_near, 0)
    lax.fori_loop(0, nq, send_far, 0)
    start(ya[0])

    def wait_near(ref, base, send, recv, sending):
        def wait(many):
            there = ref.at[pl.ds(base, many)]
            c = copy(there, there, send, recv, sibling, narrow)
            if sending:
                c.wait_send()
            else:
                c.wait_recv()

        @pl.when(has_own)
        def _():
            wait(nq - 1)

        @pl.when(jnp.logical_not(has_own))
        def _():
            wait(nq)

    def wait_far(ref, base, send, recv, sending):
        there = ref.at[pl.ds(base, nq)]
        c = copy(there, there, send, recv, sibling, narrow)
        if sending:
            c.wait_send()
        else:
            c.wait_recv()

    def next_a(t):
        landed(ya[t - 1])
        if t < last:
            start(ya[t])
            for yy in passed(t + 1):
                share(rows_a(pl.ds(0, nz), yy))
        else:
            share(rows_a(pl.ds(0, nz), lax.rem(y + last, ny)))

    hq = nq // 2

    def slab_at(xx, g):
        return (xx * NH + g) * nq

    def ring_x(g, at):
        own = slabs.at[pl.ds(slab_at(x, g), nq)]
        from_down = slabs.at[pl.ds(slab_at(x_down, g), hq)]
        from_up = slabs.at[pl.ds(slab_at(x_up, g) + hq, hq)]
        return [
            copy(own, own, ring_s.at[at, 0], ring_r.at[at, 0], wide, n_up),
            copy(own, own, ring_s.at[at, 1], ring_r.at[at, 1], wide, n_down),
            copy(from_down, from_down, ring_s.at[at, 2], ring_r.at[at, 2], wide, n_up),
            copy(from_up, from_up, ring_s.at[at, 3], ring_r.at[at, 3], wide, n_down),
        ]

    ring_near, ring_far = ring_x(high, 0), ring_x(high_far, 1)
    wait_near(slabs, slab_at(x, high), out_s.at[0], out_r.at[0], False)

    @pl.when(has_own)
    def _():
        pltpu.make_async_copy(outgoing.at[0], slabs.at[lands_at], own_sem.at[0]).wait()

    start(ring_near[:2])
    for t in range(1, last + 1):
        next_a(t)
        if t == last - 2 or (last == 2 and t == 1):
            landed(ring_near[:2])
            start(ring_near[2:])
            wait_far(slabs, slab_at(x, high_far), out_s.at[1], out_r.at[1], False)
            start(ring_far[:2])
    landed(zb)
    for d in range(1, nz):
        share(rows_b(lax.rem(z + nz - d, nz), pl.ds(0, ny)))
    landed(ring_far[:2])
    start(ring_far[2:])
    landed(ring_near[2:])
    landed(shares)
    landed(ring_far[2:])

    total[...] = jnp.zeros_like(total)
    deep = 4

    def rotate(i, carry):
        zz, yy = i // (ny // deep), lax.rem(i, ny // deep) * deep
        at = zz * ny + yy
        lhs = jnp.concatenate(
            [
                jnp.concatenate([slabs[s * nq + at + d] for s in range(NX * NH)], axis=0)
                for d in range(deep)
            ],
            axis=1,
        )
        for h in range(2):
            rhs = left[h, zz, pl.ds(yy, deep)].reshape(deep * 128, half)
            total[:, h * half : (h + 1) * half] += jnp.dot(lhs, rhs, preferred_element_type=F32)
        return carry

    lax.fori_loop(0, nq // deep, rotate, 0)
    fetches[7].wait()
    fetches[8].wait()

    def moments(s, carry):
        there = pl.ds(pl.multiple_of(s * 32, 32), 32)
        value = total[there, :]
        m = BETA_ONE * first[s] + (1.0 - BETA_ONE) * value
        v = BETA_TWO * second[s] + (1.0 - BETA_TWO) * value * value
        new_first[s] = m
        new_second[s] = v
        direction[there, :] = (m / (jnp.sqrt(v) + EPSILON)).astype(BF16)
        return carry

    lax.fori_loop(0, NX * NH, moments, 0)
    stores = [pltpu.make_async_copy(held[i], outputs[i], fetch_sem.at[9 + i]) for i in range(3)]
    stores[1].start()
    stores[2].start()

    def rotate_back(i, carry):
        zz, yy = i // (ny // 2), lax.rem(i, ny // 2) * 2
        at = zz * ny + yy
        value = None
        for h in range(2):
            rhs = left[h, zz, pl.ds(yy, 2)].reshape(256, half)
            term = lax.dot_general(
                direction[:, h * half : (h + 1) * half],
                rhs,
                (((1,), (1,)), ((), ())),
                preferred_element_type=F32,
            )
            value = term if value is None else value + term
        value = value.astype(BF16)
        for s in range(NX * NH):
            for d in range(2):
                partial[s * nq + at + d] = value[s * 32 : (s + 1) * 32, d * 128 : (d + 1) * 128]
        return carry

    def sums_of(g, at):
        def part(xx, h):
            return partial.at[pl.ds(slab_at(xx, g) + h * hq, hq)]

        lower, upper = pl.ds(0, hq), pl.ds(hq, hq)
        made = [
            (part(x_far, 0), halfway.at[at, 0], n_up),
            (part(x_far, 1), halfway.at[at, 1], n_down),
            (part(x_down, 0), arrived.at[at, 1, lower], n_down),
            (part(x_up, 1), arrived.at[at, 0, upper], n_up),
            (part(x_up, 0), arrived.at[at, 0, lower], n_up),
            (part(x_down, 1), arrived.at[at, 1, upper], n_down),
        ]
        return [copy(a, b, sum_s.at[at, i], sum_r.at[at, i], wide, nn) for i, (a, b, nn) in enumerate(made)]

    sums_far, sums_near = sums_of(high_far, 0), sums_of(high, 1)
    few = min(8, hq)

    def pass_on(g, at):
        def some(i, carry):
            for h, base in ((0, slab_at(x_up, g)), (1, slab_at(x_down, g) + hq)):
                there = pl.ds(base + i * few, few)
                held = halfway[at, h, pl.ds(i * few, few)]
                partial[there] = (partial[there].astype(F32) + held.astype(F32)).astype(BF16)
            return carry

        lax.fori_loop(0, hq // few, some, 0)

    def add_up(g, at):
        def some(i, carry):
            there = pl.ds(i * few, few)
            value = partial[pl.ds(slab_at(x, g) + i * few, few)].astype(F32) + arrived[at, 0, there].astype(F32)
            home[pl.ds(at * nq + i * few, few)] = (value + arrived[at, 1, there].astype(F32)).astype(BF16)
            return carry

        lax.fori_loop(0, nq // few, some, 0)

    lax.fori_loop(0, nq // 4, rotate_back, 0)
    start((sums_far[0], sums_far[2]))
    lax.fori_loop(nq // 4, nq // 2, rotate_back, 0)
    start((sums_far[1], sums_far[3]))
    start(sums_near[:2])
    landed(sums_far[:2])
    pass_on(high_far, 0)
    start(sums_far[4:])
    start(sums_near[2:4])
    landed(sums_near[:2])
    pass_on(high, 1)
    start(sums_near[4:])

    goes_to = high * nq + lax.rem(wide, nq)

    def back_far(t, carry):
        qq = lax.rem(chip + t, nq)
        copy(home.at[qq], back.at[goes_to], back_s.at[1], back_r.at[1], 2 * qq + side, n_far).start()
        return carry

    def back_near(t, carry):
        qq = lax.rem(chip + t, nq)
        to = 2 * qq + side
        src = home.at[nq + qq]

        @pl.when(to != wide)
        def _():
            copy(src, back.at[goes_to], back_s.at[0], back_r.at[0], to, narrow).start()

        @pl.when(to == wide)
        def _():
            pltpu.make_async_copy(src, back.at[goes_to], own_sem.at[1]).start()

        return carry

    landed(sums_far[2:])
    add_up(high_far, 0)
    lax.fori_loop(0, nq, back_far, 0)
    landed(sums_near[2:])
    add_up(high, 1)
    lax.fori_loop(0, nq, back_near, 0)
    wait_far(back, high_far * nq, back_s.at[1], back_r.at[1], False)
    wait_near(back, high * nq, back_s.at[0], back_r.at[0], False)

    @pl.when(has_own)
    def _():
        pltpu.make_async_copy(home.at[0], back.at[goes_to], own_sem.at[1]).wait()

    turned_back = (back[0:nq].astype(F32) + back[nq : 2 * nq].astype(F32)).astype(BF16).reshape(block, 128)
    tall = ny * 32
    for zz in range(nz):
        value = jnp.dot(right[zz].reshape(tall, block), turned_back, preferred_element_type=F32)
        value = value.T.astype(BF16)
        result[0, :, zz * tall : (zz + 1) * tall] = value[0:64]
        result[1, :, zz * tall : (zz + 1) * tall] = value[64:128]
    swap = copy(result.at[other], foreign, sib_s.at[3], sib_r.at[3], sibling, narrow)
    swap.start()
    for h in range(2):

        @pl.when(core == h)
        def _():
            update[:, h * block : (h + 1) * block] = result[core]

    swap.wait_recv()
    for h in range(2):

        @pl.when(core != h)
        def _():
            update[:, h * block : (h + 1) * block] = foreign[...]

    stores[0].start()

    sent = sib + zr + za + zb + [c for step in yr for pair in step for c in pair]
    sent += [c for pair in ya + yb for c in pair] + shares + ring_near + ring_far + sums_near + sums_far + [swap]
    for c in sent:
        c.wait_send()
    for c in stores:
        c.wait()
    wait_near(slabs, slab_at(x, high), out_s.at[0], out_r.at[0], True)
    wait_far(slabs, slab_at(x, high_far), out_s.at[1], out_r.at[1], True)
    wait_near(back, high * nq, back_s.at[0], back_r.at[0], True)
    wait_far(back, high_far * nq, back_s.at[1], back_r.at[1], True)


def solution(mesh):
    nz, ny = 4, mesh.shape["wide"] // 8

    def step(*args):
        return body(nz, ny, *args)

    placed = (
        P("wide", "narrow"),
        P("wide", "narrow"),
        P("wide", "narrow"),
        P("wide", "narrow"),
        P("narrow", "wide", None),
        P("narrow", "wide", None),
        P("narrow", "wide", None),
        P(None, "wide", "narrow"),
        P(None, "wide", "narrow"),
    )
    return jax.shard_map(
        step,
        mesh=mesh,
        in_specs=placed,
        out_specs=(P("wide", "narrow"), P(None, "wide", "narrow"), P(None, "wide", "narrow")),
        check_vma=False,
    )


def body(nz, ny, *args):
    nq = nz * ny
    block, span = 32 * nq, args[1].shape[1]
    half = span // 2
    slabs = NX * NH
    dma = pltpu.SemaphoreType.DMA
    steps = ny // 2
    anywhere = pl.BlockSpec(memory_space=pl.ANY)
    args = list(args)
    args[2] = args[2].T
    args[5] = jnp.swapaxes(args[5], 1, 2)
    return pl.pallas_call(
        functools.partial(kernel, nz, ny),
        out_shape=(
            jax.ShapeDtypeStruct(args[0].shape, BF16),
            jax.ShapeDtypeStruct(args[7].shape, F32),
            jax.ShapeDtypeStruct(args[8].shape, F32),
        ),
        in_specs=[anywhere] * 9,
        out_specs=(anywhere,) * 3,
        scratch_shapes=[pltpu.VMEM(a.shape, a.dtype) for a in args + [args[0], args[7], args[8]]]
        + [
            pltpu.VMEM((128, block), BF16),
            pltpu.VMEM((nz, ny, 32, block), BF16),
            pltpu.VMEM((2, nz, ny, 128, half), BF16),
            pltpu.VMEM((16, block), BF16),
            pltpu.VMEM((64, half), BF16),
            pltpu.VMEM((nq, 32, 128), BF16),
            pltpu.VMEM((slabs * nq, 32, 128), BF16),
            pltpu.VMEM((slabs * 32, span), F32),
            pltpu.VMEM((slabs * 32, span), BF16),
            pltpu.VMEM((slabs * nq, 32, 128), BF16),
            pltpu.VMEM((NH, 2, nq // 2, 32, 128), BF16),
            pltpu.VMEM((NH, 2, nq, 32, 128), BF16),
            pltpu.VMEM((NH * nq, 32, 128), BF16),
            pltpu.VMEM((NH * nq, 32, 128), BF16),
            pltpu.VMEM((2, 64, block), BF16),
            pltpu.VMEM((64, block), BF16),
            dma((12,)),
            dma((4,)),
            dma((4,)),
        ]
        + [dma((nz - 1,))] * 6
        + [dma((steps, nz, 2))] * 2
        + [dma((steps, 2))] * 4
        + [dma((ny + nz,))] * 2
        + [dma((2,))] * 5
        + [dma((2, 4))] * 2
        + [dma((2, 6))] * 2,
        compiler_params=pltpu.CompilerParams(
            collective_id=0, has_side_effects=True, vmem_limit_bytes=58 * 1024 * 1024
        ),
        cost_estimate=pl.CostEstimate(flops=2_700_000_000, bytes_accessed=8_000_000, transcendentals=131072),
    )(*args)
```

```python
import functools
import math

import jax
import jax.numpy as jnp
from jax import lax
from jax.experimental import pallas as pl
from jax.experimental.pallas import tpu as pltpu
from jax.sharding import PartitionSpec as P

MESH = pl.DeviceIdType.MESH
F32, BF16 = jnp.float32, jnp.bfloat16
BETA_ONE = 0.95
BETA_TWO = 0.95
EPSILON = 1e-08
NX = 4
NH = 2


def dequantized(codes, scales, error, quantum):
    groups, columns = scales.shape[0], codes.shape[1]
    column = lax.broadcasted_iota(jnp.int32, (groups, columns), 1) // (columns // groups)
    spread = (column == lax.broadcasted_iota(jnp.int32, (groups, columns), 0)).astype(F32).astype(BF16)
    expanded = lax.dot_general(
        scales.astype(F32).astype(BF16), spread, (((0,), (0,)), ((), ())), preferred_element_type=F32
    )
    return (codes.astype(F32) * expanded * quantum + error.astype(F32)).astype(BF16)


def kernel(nz, ny, *refs):
    inputs, refs = refs[:9], refs[9:]
    outputs, fetched, held, refs = refs[:3], refs[3:12], refs[12:15], refs[15:]
    update, new_first, new_second = held
    grad, lcodes, lscales, lerror, rcodes, rscales, rerror, first, second = fetched
    (
        turned,
        right,
        left,
        rstage,
        lstage,
        outgoing,
        slabs,
        total,
        direction,
        partial,
        halfway,
        arrived,
        home,
        back,
        result,
        foreign,
    ) = refs[:16]
    (
        fetch_sem,
        sib_s,
        sib_r,
        grad_s,
        grad_r,
        zr_s,
        zr_r,
        zl_s,
        zl_r,
        za_s,
        za_r,
        zb_s,
        zb_r,
        yr_s,
        yr_r,
        late_s,
        late_r,
        ya_s,
        ya_r,
        yb_s,
        yb_r,
        share_s,
        share_r,
        out_s,
        out_r,
        back_s,
        back_r,
        own_sem,
        ring_s,
        ring_r,
        sum_s,
        sum_r,
    ) = refs[16:]
    nq = nz * ny
    block = 32 * nq
    order = 128 * nq
    span = lcodes.shape[1]
    half = span // 2
    hb = block // 2
    wide, narrow = lax.axis_index("wide"), lax.axis_index("narrow")
    core, chip = lax.rem(wide, 2), wide // 2
    z, y = chip // ny, lax.rem(chip, ny)
    x, high = narrow // NH, lax.rem(narrow, NH)
    other = 1 - core
    pair, odd = z // 2, lax.rem(z, 2)
    place = (pair * ny + y) * 2 + odd
    side = wide // nq
    has_own = side == core
    sends_own = wide // (nq // 2) == 2 * core + odd

    fetches = [pltpu.make_async_copy(a, b, fetch_sem.at[i]) for i, (a, b) in enumerate(zip(inputs, fetched))]
    for i in (4, 5, 6, 1, 2, 3, 0, 7, 8):
        fetches[i].start()

    def wide_at(zz, yy, cc):
        return (zz * ny + yy) * 2 + cc

    def copy(src, dst, send, recv, ww, nn):
        return pltpu.make_async_remote_copy(
            src_ref=src, dst_ref=dst, send_sem=send, recv_sem=recv, device_id=(ww, nn), device_id_type=MESH
        )

    def start(copies):
        for c in copies:
            c.start()

    def landed(copies):
        for c in copies:
            c.wait_recv()

    sibling = wide + 1 - 2 * core
    y_up, y_down = lax.rem(y + 1, ny), lax.rem(y + ny - 1, ny)
    x_up, x_down = lax.rem(x + 1, NX), lax.rem(x + NX - 1, NX)
    x_far = lax.rem(x + 2, NX)
    n_up, n_down = x_up * NH + high, x_down * NH + high
    w_up, w_down = wide_at(z, y_up, core), wide_at(z, y_down, core)

    barrier = pltpu.get_barrier_semaphore()
    plane = 2 * nq * NH

    for extra in range(NH):
        nn = x * NH + lax.rem(high + extra, NH)

        def greet(i, carry):
            there = wide + i
            there = jnp.where(there >= 2 * nq, there - 2 * nq, there)
            pl.semaphore_signal(barrier, inc=1, device_id=(there, nn), device_id_type=MESH)
            return carry

        lax.fori_loop(1 if extra == 0 else 0, 2 * nq, greet, 0)
    for nn in (n_up, n_down):
        pl.semaphore_signal(barrier, inc=1, device_id=(wide, nn), device_id_type=MESH)

    rows16 = pl.ds(pl.multiple_of(core * 16, 16), 16)
    rows64 = pl.ds(pl.multiple_of(core * 64, 64), 64)
    quantum = 1.0 / (16.0 * math.sqrt(block))
    for i in (4, 5, 6):
        fetches[i].wait()
    for ref, which in ((rstage, other), (right.at[:, z, y, rows16, :], core)):
        value = dequantized(rcodes[which], rscales[which], rerror[which], quantum)
        for h in range(2):
            ref[h] = value[:, h * hb : (h + 1) * hb]
    pl.semaphore_wait(barrier, plane - 1 + 2)
    sib = [
        copy(rstage, right.at[:, z, y, rows16, :], sib_s.at[0], sib_r.at[0], sibling, narrow),
        copy(lstage, left.at[other, pair, y, odd, rows64, :], sib_s.at[1], sib_r.at[1], sibling, narrow),
    ]
    rows_g = pl.ds(pl.multiple_of(odd * 128 + core * 64, 64), 64)
    beside = wide_at(z + 1 - 2 * odd, y, core)
    own_block = grad.at[:, pl.ds(pl.multiple_of(core * block, block), block)]
    other_block = grad.at[:, pl.ds(pl.multiple_of(other * block, block), block)]
    rows_out = [
        copy(other_block, turned.at[rows_g, :], grad_s.at[0], grad_r.at[0], sibling, narrow),
        copy(own_block, turned.at[rows_g, :], grad_s.at[1], grad_r.at[1], beside, narrow),
        copy(other_block, turned.at[rows_g, :], grad_s.at[2], grad_r.at[2], beside + 1 - 2 * core, narrow),
    ]
    sib[0].start()
    quantum = 1.0 / (16.0 * math.sqrt(order))
    for i in (1, 2, 3):
        fetches[i].wait()
    value = dequantized(lcodes[...], lscales[...], lerror[...], quantum)
    for h in range(2):

        @pl.when(core == h)
        def _():
            left[h, pair, y, odd, rows64, :] = value[:, h * half : (h + 1) * half]

        @pl.when(core != h)
        def _():
            lstage[...] = value[:, h * half : (h + 1) * half]

    sib[1].start()

    last = ny // 2

    def along_z(ref_for, send, recv):
        made = []
        for d in range(1, nz):
            ref = ref_for(lax.rem(z + d, nz))
            made.append(copy(ref, ref, send.at[d - 1], recv.at[d - 1], wide_at(lax.rem(z + d, nz), y, core), narrow))
        return made

    def passed(t):
        return lax.rem(y + ny - (t - 1), ny), lax.rem(y + (t - 1), ny)

    nearest = [0, 1, nz - 1][: min(nz, 3)] + list(range(2, nz - 1))
    if nz == 2:
        nearest = [0, 1]
    zr = along_z(lambda zz: right.at[lax.rem(zz, 2), z, y], zr_s, zr_r)
    zlate = along_z(lambda zz: right.at[1 - lax.rem(zz, 2), z, y], zl_s, zl_r)

    def ring_right(t, e):
        zz = lax.rem(z + nz - e, nz)
        at = nearest.index(e)
        made = []
        for way, (yy, ww) in enumerate(zip(passed(t), (w_up, w_down))):
            if t < last or (at < nz // 2) == (way == 0):
                ref = right.at[odd, zz, yy]
                made.append(copy(ref, ref, yr_s.at[t - 1, e, way], yr_r.at[t - 1, e, way], ww, narrow))
        return made

    yr = [[ring_right(t, e) for e in nearest] for t in range(1, last + 1)]

    ra = 96
    rb = 128 - ra

    def rows_a(yy, zs=slice(None)):
        return left.at[core, :, yy, zs, pl.ds(0, ra)]

    def rows_b(yy, begin=0, size=rb):
        return left.at[core, pair, yy, odd, pl.ds(ra + begin, size)]

    own_a = left.at[core, pair, y, odd, pl.ds(0, ra)]
    za = along_z(lambda zz: own_a, za_s, za_r)
    zb = along_z(lambda zz: rows_b(pl.ds(0, ny)), zb_s, zb_r)
    ya, yb, late = [], [], []

    def both_ways(t, a, b, send, recv):
        return [
            copy(a, a, send.at[t - 1, 0], recv.at[t - 1, 0], w_up, narrow),
            copy(b, b, send.at[t - 1, 1], recv.at[t - 1, 1], w_down, narrow),
        ]

    for t in range(1, last + 1):
        up, down = passed(t)
        if t < last:
            a, b = rows_a(up), rows_a(down)
        else:
            a, b = rows_a(up, pl.ds(0, 1)), rows_a(down, pl.ds(1, 1))
        ya.append(both_ways(t, a, b, ya_s, ya_r))
        a, b = (rows_b(up), rows_b(down)) if t < last else (rows_b(up, 0, rb // 2), rows_b(down, rb // 2, rb // 2))
        yb.append(both_ways(t, a, b, yb_s, yb_r))
        zs = (pl.ds(0, nz), pl.ds(0, nz)) if t < last else (pl.ds(0, nz // 2), pl.ds(nz // 2, nz // 2))
        a, b = right.at[1 - odd, zs[0], up], right.at[1 - odd, zs[1], down]
        late.append(both_ways(t, a, b, late_s, late_r))
    shares = []

    def share(ref):
        at = len(shares)
        c = copy(ref, ref, share_s.at[at], share_r.at[at], sibling, narrow)
        c.start()
        shares.append(c)

    sib[0].wait_recv()
    start(yr[0][0])
    start(zr)
    fetches[0].wait()
    for h in range(2):

        @pl.when(core == h)
        def _():
            turned[rows_g, :] = grad[:, h * block : (h + 1) * block]

    start(rows_out)
    sib[1].wait_recv()
    start(yb[0])
    start(za)
    for at, e in enumerate(nearest):
        if at > 0:
            zr[e - 1].wait_recv()
            start(yr[0][at])
    start(zlate)
    b_step = 1

    def next_b(t):
        landed(yb[t - 1])
        if t < last:
            start(yb[t])
        else:
            start(zb)
            share(rows_b(pl.ds(0, ny)))

    for t in range(2, last + 1):
        for at in range(nz):
            landed(yr[t - 2][at])
            start(yr[t - 1][at])
            if at % 2 == 1 and b_step <= last and t < last:
                next_b(b_step)
                b_step += 1
    while b_step <= last:
        next_b(b_step)
        b_step += 1
    landed(za)
    share(rows_a(y))
    for at in range(nz):
        landed(yr[last - 1][at])

    landed(rows_out)
    wide_n = min(256, hb)
    for at in range(0, hb, wide_n):
        basis = right[odd, :, :, :, at : at + wide_n].reshape(block, wide_n)
        value = jnp.dot(turned[...], basis, preferred_element_type=F32).T.astype(BF16)
        for d in range(2):
            outgoing[at // 32 : (at + wide_n) // 32, d] = value[:, d * 128 : (d + 1) * 128].reshape(wide_n // 32, 32, 128)

    lands = slabs.at[pl.ds(narrow * nq + place - odd, 2)]
    high_far = 1 - high
    n_far = x * NH + high_far
    first_to = (nq // 2) * (2 * core + odd)

    def send_near(t, carry):
        j = lax.rem(2 * y + pair + t, nq // 2)
        to = first_to + j

        @pl.when(to != wide)
        def _():
            copy(outgoing.at[j], lands, out_s.at[0], out_r.at[0], to, narrow).start()

        @pl.when(to == wide)
        def _():
            pltpu.make_async_copy(outgoing.at[j], lands, own_sem.at[0]).start()

        return carry

    def send_far(t, carry):
        j = lax.rem(2 * y + pair + t, nq // 2)
        copy(outgoing.at[j], lands, out_s.at[1], out_r.at[1], first_to + j, n_far).start()
        return carry

    lax.fori_loop(0, nq // 2, send_near, 0)
    lax.fori_loop(0, nq // 2, send_far, 0)
    start(ya[0])

    def wait_near(ref, base, send, recv, sending, some_own=has_own, own_many=1):
        def wait(many):
            there = ref.at[pl.ds(base, many)]
            c = copy(there, there, send, recv, sibling, narrow)
            if sending:
                c.wait_send()
            else:
                c.wait_recv()

        @pl.when(some_own)
        def _():
            wait(nq - own_many)

        @pl.when(jnp.logical_not(some_own))
        def _():
            wait(nq)

    def wait_far(ref, base, send, recv, sending):
        there = ref.at[pl.ds(base, nq)]
        c = copy(there, there, send, recv, sibling, narrow)
        if sending:
            c.wait_send()
        else:
            c.wait_recv()

    def next_a(t):
        landed(ya[t - 1])
        if t < last:
            start(ya[t])
            for yy in passed(t + 1):
                share(rows_a(yy))
        else:
            share(rows_a(lax.rem(y + last, ny)))

    hq = nq // 2

    def slab_at(xx, g):
        return (xx * NH + g) * nq

    def ring_x(g, at):
        own = slabs.at[pl.ds(slab_at(x, g), nq)]
        from_down = slabs.at[pl.ds(slab_at(x_down, g), hq)]
        from_up = slabs.at[pl.ds(slab_at(x_up, g) + hq, hq)]
        return [
            copy(own, own, ring_s.at[at, 0], ring_r.at[at, 0], wide, n_up),
            copy(own, own, ring_s.at[at, 1], ring_r.at[at, 1], wide, n_down),
            copy(from_down, from_down, ring_s.at[at, 2], ring_r.at[at, 2], wide, n_up),
            copy(from_up, from_up, ring_s.at[at, 3], ring_r.at[at, 3], wide, n_down),
        ]

    ring_near, ring_far = ring_x(high, 0), ring_x(high_far, 1)
    wait_near(slabs, slab_at(x, high), out_s.at[0], out_r.at[0], False, sends_own, 2)

    @pl.when(sends_own)
    def _():
        pltpu.make_async_copy(outgoing.at[0], lands, own_sem.at[0]).wait()

    start(ring_near[:2])
    for t in range(1, last + 1):
        next_a(t)
        if t == last - 2 or (last == 2 and t == 1):
            landed(ring_near[:2])
            start(ring_near[2:])
            wait_far(slabs, slab_at(x, high_far), out_s.at[1], out_r.at[1], False)
            start(ring_far[:2])
    landed(zlate)
    start(late[0])
    landed(zb)
    for d in range(1, nz):
        zz = lax.rem(z + nz - d, nz)
        share(left.at[core, zz // 2, pl.ds(0, ny), lax.rem(zz, 2), pl.ds(ra, rb)])
    landed(ring_far[:2])
    start(ring_far[2:])
    landed(ring_near[2:])
    landed(shares)
    landed(ring_far[2:])

    total[...] = jnp.zeros_like(total)
    deep = 4

    def rotate(i, carry):
        at = i * deep
        zz, yy = i // (2 * ny // deep), lax.rem(i, 2 * ny // deep) * (deep // 2)
        lhs = jnp.concatenate(
            [
                jnp.concatenate([slabs[s * nq + at + d] for s in range(NX * NH)], axis=0)
                for d in range(deep)
            ],
            axis=1,
        )
        for h in range(2):
            rhs = left[h, zz, pl.ds(yy, deep // 2)].reshape(deep * 128, half)
            total[:, h * half : (h + 1) * half] += jnp.dot(lhs, rhs, preferred_element_type=F32)
        return carry

    def next_late(t):
        landed(late[t - 1])
        if t < last:
            start(late[t])

    lax.fori_loop(0, nq // deep, rotate, 0)
    next_late(1)
    fetches[7].wait()
    fetches[8].wait()

    def moments(s, carry):
        there = pl.ds(pl.multiple_of(s * 32, 32), 32)
        value = total[there, :]
        m = BETA_ONE * first[s] + (1.0 - BETA_ONE) * value
        v = BETA_TWO * second[s] + (1.0 - BETA_TWO) * value * value
        new_first[s] = m
        new_second[s] = v
        direction[there, :] = (m / (jnp.sqrt(v) + EPSILON)).astype(BF16)
        return carry

    lax.fori_loop(0, NX * NH, moments, 0)
    stores = [pltpu.make_async_copy(held[i], outputs[i], fetch_sem.at[9 + i]) for i in range(3)]
    stores[1].start()
    stores[2].start()

    def rotate_back(i, carry):
        at = i * 2
        zz, yy = i // ny, lax.rem(i, ny)
        value = None
        for h in range(2):
            rhs = left[h, zz, yy].reshape(256, half)
            term = lax.dot_general(
                direction[:, h * half : (h + 1) * half],
                rhs,
                (((1,), (1,)), ((), ())),
                preferred_element_type=F32,
            )
            value = term if value is None else value + term
        value = value.astype(BF16)
        for s in range(NX * NH):
            for d in range(2):
                partial[s * nq + at + d] = value[s * 32 : (s + 1) * 32, d * 128 : (d + 1) * 128]
        return carry

    def sums_of(g, at):
        def part(xx, h):
            return partial.at[pl.ds(slab_at(xx, g) + h * hq, hq)]

        lower, upper = pl.ds(0, hq), pl.ds(hq, hq)
        made = [
            (part(x_far, 0), halfway.at[at, 0], n_up),
            (part(x_far, 1), halfway.at[at, 1], n_down),
            (part(x_down, 0), arrived.at[at, 1, lower], n_down),
            (part(x_up, 1), arrived.at[at, 0, upper], n_up),
            (part(x_up, 0), arrived.at[at, 0, lower], n_up),
            (part(x_down, 1), arrived.at[at, 1, upper], n_down),
        ]
        return [copy(a, b, sum_s.at[at, i], sum_r.at[at, i], wide, nn) for i, (a, b, nn) in enumerate(made)]

    sums_far, sums_near = sums_of(high_far, 0), sums_of(high, 1)
    few = min(8, hq)

    def pass_on(g, at):
        def some(i, carry):
            for h, base in ((0, slab_at(x_up, g)), (1, slab_at(x_down, g) + hq)):
                there = pl.ds(base + i * few, few)
                held = halfway[at, h, pl.ds(i * few, few)]
                partial[there] = (partial[there].astype(F32) + held.astype(F32)).astype(BF16)
            return carry

        lax.fori_loop(0, hq // few, some, 0)

    def add_up(g, at):
        def some(i, carry):
            there = pl.ds(i * few, few)
            value = partial[pl.ds(slab_at(x, g) + i * few, few)].astype(F32) + arrived[at, 0, there].astype(F32)
            home[pl.ds(at * nq + i * few, few)] = (value + arrived[at, 1, there].astype(F32)).astype(BF16)
            return carry

        lax.fori_loop(0, nq // few, some, 0)

    lax.fori_loop(0, nq // 4, rotate_back, 0)
    start((sums_far[0], sums_far[2]))
    lax.fori_loop(nq // 4, nq // 2, rotate_back, 0)
    next_late(2)
    start((sums_far[1], sums_far[3]))
    start(sums_near[:2])
    landed(sums_far[:2])
    pass_on(high_far, 0)
    start(sums_far[4:])
    start(sums_near[2:4])
    landed(sums_near[:2])
    pass_on(high, 1)
    start(sums_near[4:])
    for t in range(3, last + 1):
        next_late(t)

    goes_to = high * nq + lax.rem(wide, nq)

    def owner(at):
        zz, yy = at // (2 * ny) * 2 + lax.rem(at, 2), lax.rem(at // 2, ny)
        return wide_at(zz, yy, side)

    def back_far(t, carry):
        at = lax.rem(place + t, nq)
        copy(home.at[at], back.at[goes_to], back_s.at[1], back_r.at[1], owner(at), n_far).start()
        return carry

    def back_near(t, carry):
        at = lax.rem(place + t, nq)
        to = owner(at)
        src = home.at[nq + at]

        @pl.when(to != wide)
        def _():
            copy(src, back.at[goes_to], back_s.at[0], back_r.at[0], to, narrow).start()

        @pl.when(to == wide)
        def _():
            pltpu.make_async_copy(src, back.at[goes_to], own_sem.at[1]).start()

        return carry

    landed(sums_far[2:])
    add_up(high_far, 0)
    lax.fori_loop(0, nq, back_far, 0)
    landed(sums_near[2:])
    add_up(high, 1)
    lax.fori_loop(0, nq, back_near, 0)
    wait_far(back, high_far * nq, back_s.at[1], back_r.at[1], False)
    wait_near(back, high * nq, back_s.at[0], back_r.at[0], False)

    @pl.when(has_own)
    def _():
        pltpu.make_async_copy(home.at[0], back.at[goes_to], own_sem.at[1]).wait()

    turned_back = (back[0:nq].astype(F32) + back[nq : 2 * nq].astype(F32)).astype(BF16).reshape(block, 128)
    tall = ny * 32
    for zz in range(nz):
        value = sum(
            jnp.dot(
                right[h, zz].reshape(tall, hb), turned_back[h * hb : (h + 1) * hb], preferred_element_type=F32
            )
            for h in range(2)
        )
        value = value.T.astype(BF16)
        result[0, :, zz * tall : (zz + 1) * tall] = value[0:64]
        result[1, :, zz * tall : (zz + 1) * tall] = value[64:128]
    swap = copy(result.at[other], foreign, sib_s.at[3], sib_r.at[3], sibling, narrow)
    swap.start()
    for h in range(2):

        @pl.when(core == h)
        def _():
            update[:, h * block : (h + 1) * block] = result[core]

    swap.wait_recv()
    for h in range(2):

        @pl.when(core != h)
        def _():
            update[:, h * block : (h + 1) * block] = foreign[...]

    stores[0].start()

    sent = sib + rows_out + zr + zlate + za + zb + [c for step in yr for part in step for c in part]
    sent += [c for part in ya + yb + late for c in part] + shares + ring_near + ring_far + sums_near + sums_far + [swap]
    for c in sent:
        c.wait_send()
    for c in stores:
        c.wait()
    wait_near(slabs, slab_at(x, high), out_s.at[0], out_r.at[0], True, sends_own, 2)
    wait_far(slabs, slab_at(x, high_far), out_s.at[1], out_r.at[1], True)
    wait_near(back, high * nq, back_s.at[0], back_r.at[0], True)
    wait_far(back, high_far * nq, back_s.at[1], back_r.at[1], True)


def solution(mesh):
    nz, ny = 4, mesh.shape["wide"] // 8

    def step(*args):
        return body(nz, ny, *args)

    placed = (
        P("wide", "narrow"),
        P("wide", "narrow"),
        P("wide", "narrow"),
        P("wide", "narrow"),
        P("narrow", "wide", None),
        P("narrow", "wide", None),
        P("narrow", "wide", None),
        P(None, "wide", "narrow"),
        P(None, "wide", "narrow"),
    )
    return jax.shard_map(
        step,
        mesh=mesh,
        in_specs=placed,
        out_specs=(P("wide", "narrow"), P(None, "wide", "narrow"), P(None, "wide", "narrow")),
        check_vma=False,
    )


def body(nz, ny, *args):
    nq = nz * ny
    block, span = 32 * nq, args[1].shape[1]
    half = span // 2
    slabs = NX * NH
    dma = pltpu.SemaphoreType.DMA
    steps = ny // 2
    anywhere = pl.BlockSpec(memory_space=pl.ANY)
    args = list(args)
    args[2] = args[2].T
    args[5] = jnp.swapaxes(args[5], 1, 2)
    return pl.pallas_call(
        functools.partial(kernel, nz, ny),
        out_shape=(
            jax.ShapeDtypeStruct(args[0].shape, BF16),
            jax.ShapeDtypeStruct(args[7].shape, F32),
            jax.ShapeDtypeStruct(args[8].shape, F32),
        ),
        in_specs=[anywhere] * 9,
        out_specs=(anywhere,) * 3,
        scratch_shapes=[pltpu.VMEM(a.shape, a.dtype) for a in args + [args[0], args[7], args[8]]]
        + [
            pltpu.VMEM((256, block), BF16),
            pltpu.VMEM((2, nz, ny, 32, block // 2), BF16),
            pltpu.VMEM((2, nz // 2, ny, 2, 128, half), BF16),
            pltpu.VMEM((2, 16, block // 2), BF16),
            pltpu.VMEM((64, half), BF16),
            pltpu.VMEM((nq // 2, 2, 32, 128), BF16),
            pltpu.VMEM((slabs * nq, 32, 128), BF16),
            pltpu.VMEM((slabs * 32, span), F32),
            pltpu.VMEM((slabs * 32, span), BF16),
            pltpu.VMEM((slabs * nq, 32, 128), BF16),
            pltpu.VMEM((NH, 2, nq // 2, 32, 128), BF16),
            pltpu.VMEM((NH, 2, nq, 32, 128), BF16),
            pltpu.VMEM((NH * nq, 32, 128), BF16),
            pltpu.VMEM((NH * nq, 32, 128), BF16),
            pltpu.VMEM((2, 64, block), BF16),
            pltpu.VMEM((64, block), BF16),
            dma((12,)),
            dma((4,)),
            dma((4,)),
            dma((3,)),
            dma((3,)),
        ]
        + [dma((nz - 1,))] * 8
        + [dma((steps, nz, 2))] * 2
        + [dma((steps, 2))] * 6
        + [dma((ny + nz,))] * 2
        + [dma((2,))] * 5
        + [dma((2, 4))] * 2
        + [dma((2, 6))] * 2,
        compiler_params=pltpu.CompilerParams(
            collective_id=0, has_side_effects=True, vmem_limit_bytes=58 * 1024 * 1024
        ),
        cost_estimate=pl.CostEstimate(flops=2_700_000_000, bytes_accessed=8_000_000, transcendentals=131072),
    )(*args)
```

```python
import functools
import math

import jax
import jax.numpy as jnp
from jax import lax
from jax.experimental import pallas as pl
from jax.experimental.pallas import tpu as pltpu
from jax.sharding import PartitionSpec as P

MESH = pl.DeviceIdType.MESH
F32, BF16 = jnp.float32, jnp.bfloat16
BETA_ONE = 0.95
BETA_TWO = 0.95
EPSILON = 1e-08
NX = 4
NH = 2


def dequantized(codes, scales, error, quantum):
    groups, columns = scales.shape[0], codes.shape[1]
    column = lax.broadcasted_iota(jnp.int32, (groups, columns), 1) // (columns // groups)
    spread = (column == lax.broadcasted_iota(jnp.int32, (groups, columns), 0)).astype(F32).astype(BF16)
    expanded = lax.dot_general(
        scales.astype(F32).astype(BF16), spread, (((0,), (0,)), ((), ())), preferred_element_type=F32
    )
    return (codes.astype(F32) * expanded * quantum + error.astype(F32)).astype(BF16)


def kernel(nz, ny, *refs):
    inputs, refs = refs[:9], refs[9:]
    outputs, fetched, held, refs = refs[:3], refs[3:12], refs[12:14], refs[14:]
    update, (new_first, new_second) = outputs[0], held
    grad, lcodes, lscales, lerror, rcodes, rscales, rerror, first, second = fetched
    (
        turned,
        right,
        left,
        rstage,
        lstage,
        outgoing,
        slabs,
        total,
        direction,
        partial,
        halfway,
        arrived,
        home,
        back,
        result,
    ) = refs[:15]
    (
        fetch_sem,
        sib_s,
        sib_r,
        swap_s,
        swap_r,
        grad_s,
        grad_r,
        zr_s,
        zr_r,
        zl_s,
        zl_r,
        za_s,
        za_r,
        zb_s,
        zb_r,
        yr_s,
        yr_r,
        late_s,
        late_r,
        ya_s,
        ya_r,
        yb_s,
        yb_r,
        share_s,
        share_r,
        out_s,
        out_r,
        back_s,
        back_r,
        own_sem,
        ring_s,
        ring_r,
        sum_s,
        sum_r,
    ) = refs[15:]
    nq = nz * ny
    block = 32 * nq
    order = 128 * nq
    span = lcodes.shape[1]
    half = span // 2
    hb = block // 2
    wide, narrow = lax.axis_index("wide"), lax.axis_index("narrow")
    core, chip = lax.rem(wide, 2), wide // 2
    z, y = chip // ny, lax.rem(chip, ny)
    x, high = narrow // NH, lax.rem(narrow, NH)
    other = 1 - core
    pair, odd = z // 2, lax.rem(z, 2)
    place = (pair * ny + y) * 2 + odd
    side = wide // nq
    has_own = side == core
    sends_own = wide // (nq // 2) == 2 * core + odd

    fetches = [pltpu.make_async_copy(a, b, fetch_sem.at[i]) for i, (a, b) in enumerate(zip(inputs, fetched))]
    for i in (4, 5, 6, 1, 2, 3, 0, 7, 8):
        fetches[i].start()

    def wide_at(zz, yy, cc):
        return (zz * ny + yy) * 2 + cc

    def copy(src, dst, send, recv, ww, nn):
        return pltpu.make_async_remote_copy(
            src_ref=src, dst_ref=dst, send_sem=send, recv_sem=recv, device_id=(ww, nn), device_id_type=MESH
        )

    def start(copies):
        for c in copies:
            c.start()

    def landed(copies):
        for c in copies:
            c.wait_recv()

    sibling = wide + 1 - 2 * core
    y_up, y_down = lax.rem(y + 1, ny), lax.rem(y + ny - 1, ny)
    x_up, x_down = lax.rem(x + 1, NX), lax.rem(x + NX - 1, NX)
    x_far = lax.rem(x + 2, NX)
    n_up, n_down = x_up * NH + high, x_down * NH + high
    w_up, w_down = wide_at(z, y_up, core), wide_at(z, y_down, core)

    barrier = pltpu.get_barrier_semaphore()
    plane = 2 * nq * NH

    for extra in range(NH):
        nn = x * NH + lax.rem(high + extra, NH)

        def greet(i, carry):
            there = wide + i
            there = jnp.where(there >= 2 * nq, there - 2 * nq, there)
            pl.semaphore_signal(barrier, inc=1, device_id=(there, nn), device_id_type=MESH)
            return carry

        lax.fori_loop(1 if extra == 0 else 0, 2 * nq, greet, 0)
    for nn in (n_up, n_down):
        pl.semaphore_signal(barrier, inc=1, device_id=(wide, nn), device_id_type=MESH)

    rows16 = pl.ds(pl.multiple_of(core * 16, 16), 16)
    rows64 = pl.ds(pl.multiple_of(core * 64, 64), 64)
    quantum = 1.0 / (16.0 * math.sqrt(block))
    for i in (4, 5, 6):
        fetches[i].wait()
    for ref, which in ((rstage, other), (right.at[:, z, y, rows16, :], core)):
        value = dequantized(rcodes[which], rscales[which], rerror[which], quantum)
        for h in range(2):
            ref[h] = value[:, h * hb : (h + 1) * hb]
    pl.semaphore_wait(barrier, plane - 1 + 2)
    sib = [
        copy(rstage, right.at[:, z, y, rows16, :], sib_s.at[0], sib_r.at[0], sibling, narrow),
        copy(lstage, left.at[other, pair, y, odd, rows64, :], sib_s.at[1], sib_r.at[1], sibling, narrow),
    ]
    rows_g = pl.ds(pl.multiple_of(odd * 128 + core * 64, 64), 64)
    beside = wide_at(z + 1 - 2 * odd, y, core)
    own_block = grad.at[:, pl.ds(pl.multiple_of(core * block, block), block)]
    other_block = grad.at[:, pl.ds(pl.multiple_of(other * block, block), block)]
    rows_out = [
        copy(other_block, turned.at[rows_g, :], grad_s.at[0], grad_r.at[0], sibling, narrow),
        copy(own_block, turned.at[rows_g, :], grad_s.at[1], grad_r.at[1], beside, narrow),
        copy(other_block, turned.at[rows_g, :], grad_s.at[2], grad_r.at[2], beside + 1 - 2 * core, narrow),
    ]
    sib[0].start()
    quantum = 1.0 / (16.0 * math.sqrt(order))
    for i in (1, 2, 3):
        fetches[i].wait()
    value = dequantized(lcodes[...], lscales[...], lerror[...], quantum)
    for h in range(2):

        @pl.when(core == h)
        def _():
            left[h, pair, y, odd, rows64, :] = value[:, h * half : (h + 1) * half]

        @pl.when(core != h)
        def _():
            lstage[...] = value[:, h * half : (h + 1) * half]

    sib[1].start()

    last = ny // 2

    def along_z(ref_for, send, recv):
        made = []
        for d in range(1, nz):
            ref = ref_for(lax.rem(z + d, nz))
            made.append(copy(ref, ref, send.at[d - 1], recv.at[d - 1], wide_at(lax.rem(z + d, nz), y, core), narrow))
        return made

    def passed(t):
        return lax.rem(y + ny - (t - 1), ny), lax.rem(y + (t - 1), ny)

    nearest = [0, 1, nz - 1][: min(nz, 3)] + list(range(2, nz - 1))
    if nz == 2:
        nearest = [0, 1]
    zr = along_z(lambda zz: right.at[lax.rem(zz, 2), z, y], zr_s, zr_r)
    zlate = along_z(lambda zz: right.at[1 - lax.rem(zz, 2), z, y], zl_s, zl_r)

    def ring_right(t, e):
        zz = lax.rem(z + nz - e, nz)
        at = nearest.index(e)
        made = []
        for way, (yy, ww) in enumerate(zip(passed(t), (w_up, w_down))):
            if t < last or (at < nz // 2) == (way == 0):
                ref = right.at[odd, zz, yy]
                made.append(copy(ref, ref, yr_s.at[t - 1, e, way], yr_r.at[t - 1, e, way], ww, narrow))
        return made

    yr = [[ring_right(t, e) for e in nearest] for t in range(1, last + 1)]

    ra = 96
    rb = 128 - ra

    def rows_a(yy, zs=slice(None)):
        return left.at[core, :, yy, zs, pl.ds(0, ra)]

    def rows_b(yy, begin=0, size=rb):
        return left.at[core, pair, yy, odd, pl.ds(ra + begin, size)]

    own_a = left.at[core, pair, y, odd, pl.ds(0, ra)]
    za = along_z(lambda zz: own_a, za_s, za_r)
    zb = along_z(lambda zz: rows_b(pl.ds(0, ny)), zb_s, zb_r)
    ya, yb, late = [], [], []

    def both_ways(t, a, b, send, recv):
        return [
            copy(a, a, send.at[t - 1, 0], recv.at[t - 1, 0], w_up, narrow),
            copy(b, b, send.at[t - 1, 1], recv.at[t - 1, 1], w_down, narrow),
        ]

    for t in range(1, last + 1):
        up, down = passed(t)
        if t < last:
            a, b = rows_a(up), rows_a(down)
        else:
            a, b = rows_a(up, pl.ds(0, 1)), rows_a(down, pl.ds(1, 1))
        ya.append(both_ways(t, a, b, ya_s, ya_r))
        a, b = (rows_b(up), rows_b(down)) if t < last else (rows_b(up, 0, rb // 2), rows_b(down, rb // 2, rb // 2))
        yb.append(both_ways(t, a, b, yb_s, yb_r))
        zs = (pl.ds(0, nz), pl.ds(0, nz)) if t < last else (pl.ds(0, nz // 2), pl.ds(nz // 2, nz // 2))
        a, b = right.at[1 - odd, zs[0], up], right.at[1 - odd, zs[1], down]
        late.append(both_ways(t, a, b, late_s, late_r))
    shares = []

    def share(ref):
        at = len(shares)
        c = copy(ref, ref, share_s.at[at], share_r.at[at], sibling, narrow)
        c.start()
        shares.append(c)

    sib[0].wait_recv()
    start(yr[0][0])
    start(zr)
    fetches[0].wait()
    for h in range(2):

        @pl.when(core == h)
        def _():
            turned[rows_g, :] = grad[:, h * block : (h + 1) * block]

    start(rows_out)
    sib[1].wait_recv()
    start(yb[0])
    start(za)
    for at, e in enumerate(nearest):
        if at > 0:
            zr[e - 1].wait_recv()
            start(yr[0][at])
    start(zlate)
    b_step = 1

    def next_b(t):
        landed(yb[t - 1])
        if t < last:
            start(yb[t])
        else:
            start(zb)
            share(rows_b(pl.ds(0, ny)))

    for t in range(2, last + 1):
        for at in range(nz):
            landed(yr[t - 2][at])
            start(yr[t - 1][at])
            if at % 2 == 1 and b_step <= last and t < last:
                next_b(b_step)
                b_step += 1
    while b_step <= last:
        next_b(b_step)
        b_step += 1
    landed(za)
    start(ya[0])
    share(rows_a(y))
    for at in range(nz):
        landed(yr[last - 1][at])

    landed(rows_out)
    lands = slabs.at[pl.ds(narrow * nq + place - odd, 2)]
    high_far = 1 - high
    n_far = x * NH + high_far
    first_to = (nq // 2) * (2 * core + odd)

    wide_n = min(256, hb)
    some = wide_n // 32

    def send_near(begin, t, carry):
        j = begin + lax.rem(2 * y + pair + t, some)
        to = first_to + j

        @pl.when(to != wide)
        def _():
            copy(outgoing.at[j], lands, out_s.at[0], out_r.at[0], to, narrow).start()

        @pl.when(to == wide)
        def _():
            pltpu.make_async_copy(outgoing.at[j], lands, own_sem.at[0]).start()

        return carry

    def send_far(t, carry):
        j = lax.rem(2 * y + pair + t, nq // 2)
        copy(outgoing.at[j], lands, out_s.at[1], out_r.at[1], first_to + j, n_far).start()
        return carry

    for at in range(0, hb, wide_n):
        basis = right[odd, :, :, :, at : at + wide_n].reshape(block, wide_n)
        value = jnp.dot(turned[...], basis, preferred_element_type=F32).T.astype(BF16)
        for d in range(2):
            outgoing[at // 32 : at // 32 + some, d] = value[:, d * 128 : (d + 1) * 128].reshape(some, 32, 128)
        lax.fori_loop(0, some, functools.partial(send_near, at // 32), 0)
    lax.fori_loop(0, nq // 2, send_far, 0)

    def wait_near(ref, base, send, recv, sending, some_own=has_own, own_many=1):
        def wait(many):
            there = ref.at[pl.ds(base, many)]
            c = copy(there, there, send, recv, sibling, narrow)
            if sending:
                c.wait_send()
            else:
                c.wait_recv()

        @pl.when(some_own)
        def _():
            wait(nq - own_many)

        @pl.when(jnp.logical_not(some_own))
        def _():
            wait(nq)

    def wait_far(ref, base, send, recv, sending):
        there = ref.at[pl.ds(base, nq)]
        c = copy(there, there, send, recv, sibling, narrow)
        if sending:
            c.wait_send()
        else:
            c.wait_recv()

    def next_a(t):
        landed(ya[t - 1])
        if t < last:
            start(ya[t])
            for yy in passed(t + 1):
                share(rows_a(yy))
        else:
            share(rows_a(lax.rem(y + last, ny)))

    hq = nq // 2

    def slab_at(xx, g):
        return (xx * NH + g) * nq

    def ring_x(g, at):
        own = [slabs.at[pl.ds(slab_at(x, g) + h * hq, hq)] for h in range(2)]
        from_down = slabs.at[pl.ds(slab_at(x_down, g), hq)]
        from_up = slabs.at[pl.ds(slab_at(x_up, g) + hq, hq)]
        made = [
            (own[0], n_up),
            (own[1], n_down),
            (own[1], n_up),
            (own[0], n_down),
            (from_down, n_up),
            (from_up, n_down),
        ]
        return [copy(a, a, ring_s.at[at, i], ring_r.at[at, i], wide, nn) for i, (a, nn) in enumerate(made)]

    ring_near, ring_far = ring_x(high, 0), ring_x(high_far, 1)
    next_a(1)
    wait_near(slabs, slab_at(x, high), out_s.at[0], out_r.at[0], False, sends_own, 2)

    @pl.when(sends_own)
    def _():
        pltpu.make_async_copy(outgoing.at[0], lands, own_sem.at[0]).wait()

    start(ring_near[:4])
    if last > 1:
        next_a(2)
    landed(ring_near[:2])
    start(ring_near[4:])
    if last > 2:
        next_a(3)
    wait_far(slabs, slab_at(x, high_far), out_s.at[1], out_r.at[1], False)
    start(ring_far[:4])
    for t in range(4, last + 1):
        next_a(t)
    landed(zb)
    for d in range(1, nz):
        zz = lax.rem(z + nz - d, nz)
        share(left.at[core, zz // 2, pl.ds(0, ny), lax.rem(zz, 2), pl.ds(ra, rb)])
    landed(ring_far[:2])
    start(ring_far[4:])
    landed(zlate)
    start(late[0])
    landed(ring_near[2:])
    landed(shares)
    landed(ring_far[2:])

    total[...] = jnp.zeros_like(total)
    deep = 4

    def rotate(i, carry):
        at = i * deep
        zz, yy = i // (2 * ny // deep), lax.rem(i, 2 * ny // deep) * (deep // 2)
        lhs = jnp.concatenate(
            [
                jnp.concatenate([slabs[s * nq + at + d] for s in range(NX * NH)], axis=0)
                for d in range(deep)
            ],
            axis=1,
        )
        for h in range(2):
            rhs = left[h, zz, pl.ds(yy, deep // 2)].reshape(deep * 128, half)
            total[:, h * half : (h + 1) * half] += jnp.dot(lhs, rhs, preferred_element_type=F32)
        return carry

    def next_late(t):
        landed(late[t - 1])
        if t < last:
            start(late[t])

    lax.fori_loop(0, nq // deep, rotate, 0)
    next_late(1)
    fetches[7].wait()
    fetches[8].wait()

    def moments(s, carry):
        there = pl.ds(pl.multiple_of(s * 32, 32), 32)
        value = total[there, :]
        m = BETA_ONE * first[s] + (1.0 - BETA_ONE) * value
        v = BETA_TWO * second[s] + (1.0 - BETA_TWO) * value * value
        new_first[s] = m
        new_second[s] = v
        direction[there, :] = (m / (jnp.sqrt(v) + EPSILON)).astype(BF16)
        return carry

    lax.fori_loop(0, NX * NH, moments, 0)
    stores = [pltpu.make_async_copy(held[i], outputs[1 + i], fetch_sem.at[9 + i]) for i in range(2)]
    for c in stores:
        c.start()

    def rotate_back(i, carry):
        at = i * 2
        zz, yy = i // ny, lax.rem(i, ny)
        value = None
        for h in range(2):
            rhs = left[h, zz, yy].reshape(256, half)
            term = lax.dot_general(
                direction[:, h * half : (h + 1) * half],
                rhs,
                (((1,), (1,)), ((), ())),
                preferred_element_type=F32,
            )
            value = term if value is None else value + term
        value = value.astype(BF16)
        for s in range(NX * NH):
            for d in range(2):
                partial[s * nq + at + d] = value[s * 32 : (s + 1) * 32, d * 128 : (d + 1) * 128]
        return carry

    def sums_of(g, at):
        def part(xx, h):
            return partial.at[pl.ds(slab_at(xx, g) + h * hq, hq)]

        lower, upper = pl.ds(0, hq), pl.ds(hq, hq)
        made = [
            (part(x_far, 0), halfway.at[at, 0], n_up),
            (part(x_far, 1), halfway.at[at, 1], n_down),
            (part(x_down, 0), arrived.at[at, 1, lower], n_down),
            (part(x_up, 1), arrived.at[at, 0, upper], n_up),
            (part(x_up, 0), arrived.at[at, 0, lower], n_up),
            (part(x_down, 1), arrived.at[at, 1, upper], n_down),
        ]
        return [copy(a, b, sum_s.at[at, i], sum_r.at[at, i], wide, nn) for i, (a, b, nn) in enumerate(made)]

    sums_far, sums_near = sums_of(high_far, 0), sums_of(high, 1)
    few = min(8, hq)

    def pass_on(g, at):
        def some(i, carry):
            for h, base in ((0, slab_at(x_up, g)), (1, slab_at(x_down, g) + hq)):
                there = pl.ds(base + i * few, few)
                held = halfway[at, h, pl.ds(i * few, few)]
                partial[there] = (partial[there].astype(F32) + held.astype(F32)).astype(BF16)
            return carry

        lax.fori_loop(0, hq // few, some, 0)

    def add_up(g, at):
        def some(i, carry):
            there = pl.ds(i * few, few)
            value = partial[pl.ds(slab_at(x, g) + i * few, few)].astype(F32) + arrived[at, 0, there].astype(F32)
            home[pl.ds(at * nq + i * few, few)] = (value + arrived[at, 1, there].astype(F32)).astype(BF16)
            return carry

        lax.fori_loop(0, nq // few, some, 0)

    lax.fori_loop(0, nq // 4, rotate_back, 0)
    start((sums_far[0], sums_far[2]))
    lax.fori_loop(nq // 4, nq // 2, rotate_back, 0)
    next_late(2)
    start((sums_far[1], sums_far[3]))
    start(sums_near[:2])
    landed(sums_far[:2])
    pass_on(high_far, 0)
    start(sums_far[4:])
    start(sums_near[2:4])
    landed(sums_near[:2])
    pass_on(high, 1)
    start(sums_near[4:])
    for t in range(3, last + 1):
        next_late(t)

    goes_to = high * nq + lax.rem(wide, nq)

    def owner(at):
        zz, yy = at // (2 * ny) * 2 + lax.rem(at, 2), lax.rem(at // 2, ny)
        return wide_at(zz, yy, side)

    def back_far(t, carry):
        at = lax.rem(place + t, nq)
        copy(home.at[at], back.at[goes_to], back_s.at[1], back_r.at[1], owner(at), n_far).start()
        return carry

    def back_near(t, carry):
        at = lax.rem(place + t, nq)
        to = owner(at)
        src = home.at[nq + at]

        @pl.when(to != wide)
        def _():
            copy(src, back.at[goes_to], back_s.at[0], back_r.at[0], to, narrow).start()

        @pl.when(to == wide)
        def _():
            pltpu.make_async_copy(src, back.at[goes_to], own_sem.at[1]).start()

        return carry

    landed(sums_far[2:])
    add_up(high_far, 0)
    lax.fori_loop(0, nq, back_far, 0)
    landed(sums_near[2:])
    add_up(high, 1)
    lax.fori_loop(0, nq, back_near, 0)
    wait_far(back, high_far * nq, back_s.at[1], back_r.at[1], False)
    wait_near(back, high * nq, back_s.at[0], back_r.at[0], False)

    @pl.when(has_own)
    def _():
        pltpu.make_async_copy(home.at[0], back.at[goes_to], own_sem.at[1]).wait()

    turned_back = (back[0:nq].astype(F32) + back[nq : 2 * nq].astype(F32)).astype(BF16).reshape(block, 128)
    tall = ny * 32
    swaps = []
    for zz in range(nz):
        value = sum(
            jnp.dot(
                right[h, zz].reshape(tall, hb), turned_back[h * hb : (h + 1) * hb], preferred_element_type=F32
            )
            for h in range(2)
        )
        value = value.T.astype(BF16)
        result[zz, 0] = value[0:64]
        result[zz, 1] = value[64:128]
        there = update.at[:, pl.ds(pl.multiple_of(core * block + zz * tall, tall), tall)]
        swap = copy(result.at[zz, other], there, swap_s.at[zz], swap_r.at[zz], sibling, narrow)
        swap.start()
        swaps.append(swap)
        store = pltpu.make_async_copy(result.at[zz, core], there, fetch_sem.at[11 + zz])
        store.start()
        stores.append(store)
    landed(swaps)

    sent = sib + rows_out + zr + zlate + za + zb + [c for step in yr for part in step for c in part]
    sent += [c for part in ya + yb + late for c in part] + shares + ring_near + ring_far + sums_near + sums_far + swaps
    for c in sent:
        c.wait_send()
    for c in stores:
        c.wait()
    wait_near(slabs, slab_at(x, high), out_s.at[0], out_r.at[0], True, sends_own, 2)
    wait_far(slabs, slab_at(x, high_far), out_s.at[1], out_r.at[1], True)
    wait_near(back, high * nq, back_s.at[0], back_r.at[0], True)
    wait_far(back, high_far * nq, back_s.at[1], back_r.at[1], True)


def solution(mesh):
    nz, ny = 4, mesh.shape["wide"] // 8

    def step(*args):
        return body(nz, ny, *args)

    placed = (
        P("wide", "narrow"),
        P("wide", "narrow"),
        P("wide", "narrow"),
        P("wide", "narrow"),
        P("narrow", "wide", None),
        P("narrow", "wide", None),
        P("narrow", "wide", None),
        P(None, "wide", "narrow"),
        P(None, "wide", "narrow"),
    )
    return jax.shard_map(
        step,
        mesh=mesh,
        in_specs=placed,
        out_specs=(P("wide", "narrow"), P(None, "wide", "narrow"), P(None, "wide", "narrow")),
        check_vma=False,
    )


def body(nz, ny, *args):
    nq = nz * ny
    block, span = 32 * nq, args[1].shape[1]
    half = span // 2
    slabs = NX * NH
    dma = pltpu.SemaphoreType.DMA
    steps = ny // 2
    anywhere = pl.BlockSpec(memory_space=pl.ANY)
    args = list(args)
    args[2] = args[2].T
    args[5] = jnp.swapaxes(args[5], 1, 2)
    return pl.pallas_call(
        functools.partial(kernel, nz, ny),
        out_shape=(
            jax.ShapeDtypeStruct(args[0].shape, BF16),
            jax.ShapeDtypeStruct(args[7].shape, F32),
            jax.ShapeDtypeStruct(args[8].shape, F32),
        ),
        in_specs=[anywhere] * 9,
        out_specs=(anywhere,) * 3,
        scratch_shapes=[pltpu.VMEM(a.shape, a.dtype) for a in args + args[7:9]]
        + [
            pltpu.VMEM((256, block), BF16),
            pltpu.VMEM((2, nz, ny, 32, block // 2), BF16),
            pltpu.VMEM((2, nz // 2, ny, 2, 128, half), BF16),
            pltpu.VMEM((2, 16, block // 2), BF16),
            pltpu.VMEM((64, half), BF16),
            pltpu.VMEM((nq // 2, 2, 32, 128), BF16),
            pltpu.VMEM((slabs * nq, 32, 128), BF16),
            pltpu.VMEM((slabs * 32, span), F32),
            pltpu.VMEM((slabs * 32, span), BF16),
            pltpu.VMEM((slabs * nq, 32, 128), BF16),
            pltpu.VMEM((NH, 2, nq // 2, 32, 128), BF16),
            pltpu.VMEM((NH, 2, nq, 32, 128), BF16),
            pltpu.VMEM((NH * nq, 32, 128), BF16),
            pltpu.VMEM((NH * nq, 32, 128), BF16),
            pltpu.VMEM((nz, 2, 64, ny * 32), BF16),
            dma((11 + nz,)),
            dma((2,)),
            dma((2,)),
            dma((nz,)),
            dma((nz,)),
            dma((3,)),
            dma((3,)),
        ]
        + [dma((nz - 1,))] * 8
        + [dma((steps, nz, 2))] * 2
        + [dma((steps, 2))] * 6
        + [dma((ny + nz,))] * 2
        + [dma((2,))] * 5
        + [dma((2, 6))] * 4,
        compiler_params=pltpu.CompilerParams(
            collective_id=0, has_side_effects=True, vmem_limit_bytes=58 * 1024 * 1024
        ),
        cost_estimate=pl.CostEstimate(flops=2_700_000_000, bytes_accessed=8_000_000, transcendentals=131072),
    )(*args)
```

```python
import functools
import math

import jax
import jax.numpy as jnp
from jax import lax
from jax.experimental import pallas as pl
from jax.experimental.pallas import tpu as pltpu
from jax.sharding import PartitionSpec as P

MESH = pl.DeviceIdType.MESH
F32, BF16 = jnp.float32, jnp.bfloat16
BETA_ONE = 0.95
BETA_TWO = 0.95
EPSILON = 1e-08
NX = 4
NH = 2


def dequantized(codes, scales, error, quantum):
    groups, columns = scales.shape[0], codes.shape[1]
    column = lax.broadcasted_iota(jnp.int32, (groups, columns), 1) // (columns // groups)
    spread = (column == lax.broadcasted_iota(jnp.int32, (groups, columns), 0)).astype(F32).astype(BF16)
    expanded = lax.dot_general(
        scales.astype(F32).astype(BF16), spread, (((0,), (0,)), ((), ())), preferred_element_type=F32
    )
    return (codes.astype(F32) * expanded * quantum + error.astype(F32)).astype(BF16)


def kernel(nz, ny, *refs):
    inputs, refs = refs[:9], refs[9:]
    outputs, fetched, held, refs = refs[:3], refs[3:12], refs[12:14], refs[14:]
    update, (new_first, new_second) = outputs[0], held
    grad, lcodes, lscales, lerror, rcodes, rscales, rerror, first, second = fetched
    (
        turned,
        right,
        left,
        rstage,
        lstage,
        outgoing,
        slabs,
        total,
        direction,
        partial,
        halfway,
        arrived,
        home,
        back,
        result,
    ) = refs[:15]
    (
        fetch_sem,
        sib_s,
        sib_r,
        swap_s,
        swap_r,
        grad_s,
        grad_r,
        zr_s,
        zr_r,
        zl_s,
        zl_r,
        za_s,
        za_r,
        zb_s,
        zb_r,
        yr_s,
        yr_r,
        late_s,
        late_r,
        ya_s,
        ya_r,
        yb_s,
        yb_r,
        share_s,
        share_r,
        out_s,
        out_r,
        back_s,
        back_r,
        own_sem,
        ring_s,
        ring_r,
        sum_s,
        sum_r,
    ) = refs[15:]
    nq = nz * ny
    block = 32 * nq
    order = 128 * nq
    span = lcodes.shape[1]
    half = span // 2
    hb = block // 2
    wide, narrow = lax.axis_index("wide"), lax.axis_index("narrow")
    core, chip = lax.rem(wide, 2), wide // 2
    z, y = chip // ny, lax.rem(chip, ny)
    x, high = narrow // NH, lax.rem(narrow, NH)
    other = 1 - core
    pair, odd = z // 2, lax.rem(z, 2)
    place = (pair * ny + y) * 2 + odd
    side = wide // nq
    has_own = side == core
    sends_own = wide // (nq // 2) == 2 * core + odd

    fetches = [pltpu.make_async_copy(a, b, fetch_sem.at[i]) for i, (a, b) in enumerate(zip(inputs, fetched))]
    for i in (4, 5, 6, 1, 2, 3, 0, 7, 8):
        fetches[i].start()

    def wide_at(zz, yy, cc):
        return (zz * ny + yy) * 2 + cc

    def copy(src, dst, send, recv, ww, nn):
        return pltpu.make_async_remote_copy(
            src_ref=src, dst_ref=dst, send_sem=send, recv_sem=recv, device_id=(ww, nn), device_id_type=MESH
        )

    def start(copies):
        for c in copies:
            c.start()

    def landed(copies):
        for c in copies:
            c.wait_recv()

    sibling = wide + 1 - 2 * core
    y_up, y_down = lax.rem(y + 1, ny), lax.rem(y + ny - 1, ny)
    x_up, x_down = lax.rem(x + 1, NX), lax.rem(x + NX - 1, NX)
    x_far = lax.rem(x + 2, NX)
    n_up, n_down = x_up * NH + high, x_down * NH + high
    w_up, w_down = wide_at(z, y_up, core), wide_at(z, y_down, core)

    barrier = pltpu.get_barrier_semaphore()
    plane = 2 * nq * NH

    for extra in range(NH):
        nn = x * NH + lax.rem(high + extra, NH)

        def greet(i, carry):
            there = wide + i
            there = jnp.where(there >= 2 * nq, there - 2 * nq, there)
            pl.semaphore_signal(barrier, inc=1, device_id=(there, nn), device_id_type=MESH)
            return carry

        lax.fori_loop(1 if extra == 0 else 0, 2 * nq, greet, 0)
    for nn in (n_up, n_down):
        pl.semaphore_signal(barrier, inc=1, device_id=(wide, nn), device_id_type=MESH)

    rows16 = pl.ds(pl.multiple_of(core * 16, 16), 16)
    rows64 = pl.ds(pl.multiple_of(core * 64, 64), 64)
    quantum = 1.0 / (16.0 * math.sqrt(block))
    for i in (4, 5, 6):
        fetches[i].wait()
    for ref, which in ((rstage, other), (right.at[:, z, y, rows16, :], core)):
        value = dequantized(rcodes[which], rscales[which], rerror[which], quantum)
        for h in range(2):
            ref[h] = value[:, h * hb : (h + 1) * hb]
    pl.semaphore_wait(barrier, plane - 1 + 2)
    sib = [
        copy(rstage, right.at[:, z, y, rows16, :], sib_s.at[0], sib_r.at[0], sibling, narrow),
        copy(lstage, left.at[other, pair, y, odd, rows64, :], sib_s.at[1], sib_r.at[1], sibling, narrow),
    ]
    rows_g = pl.ds(pl.multiple_of(odd * 128 + core * 64, 64), 64)
    beside = wide_at(z + 1 - 2 * odd, y, core)
    own_block = grad.at[:, pl.ds(pl.multiple_of(core * block, block), block)]
    other_block = grad.at[:, pl.ds(pl.multiple_of(other * block, block), block)]
    rows_out = [
        copy(other_block, turned.at[rows_g, :], grad_s.at[0], grad_r.at[0], sibling, narrow),
        copy(own_block, turned.at[rows_g, :], grad_s.at[1], grad_r.at[1], beside, narrow),
        copy(other_block, turned.at[rows_g, :], grad_s.at[2], grad_r.at[2], beside + 1 - 2 * core, narrow),
    ]
    sib[0].start()
    quantum = 1.0 / (16.0 * math.sqrt(order))
    for i in (1, 2, 3):
        fetches[i].wait()
    value = dequantized(lcodes[...], lscales[...], lerror[...], quantum)
    for h in range(2):

        @pl.when(core == h)
        def _():
            left[h, pair, y, odd, rows64, :] = value[:, h * half : (h + 1) * half]

        @pl.when(core != h)
        def _():
            lstage[...] = value[:, h * half : (h + 1) * half]

    sib[1].start()

    last = ny // 2

    def along_z(ref_for, send, recv):
        made = []
        for d in range(1, nz):
            ref = ref_for(lax.rem(z + d, nz))
            made.append(copy(ref, ref, send.at[d - 1], recv.at[d - 1], wide_at(lax.rem(z + d, nz), y, core), narrow))
        return made

    def passed(t):
        return lax.rem(y + ny - (t - 1), ny), lax.rem(y + (t - 1), ny)

    nearest = [0, 1, nz - 1][: min(nz, 3)] + list(range(2, nz - 1))
    if nz == 2:
        nearest = [0, 1]
    zr = along_z(lambda zz: right.at[lax.rem(zz, 2), z, y], zr_s, zr_r)
    zlate = along_z(lambda zz: right.at[1 - lax.rem(zz, 2), z, y], zl_s, zl_r)

    def ring_right(t, e):
        zz = lax.rem(z + nz - e, nz)
        at = nearest.index(e)
        made = []
        for way, (yy, ww) in enumerate(zip(passed(t), (w_up, w_down))):
            if t < last or (at < nz // 2) == (way == 0):
                ref = right.at[odd, zz, yy]
                made.append(copy(ref, ref, yr_s.at[t - 1, e, way], yr_r.at[t - 1, e, way], ww, narrow))
        return made

    yr = [[ring_right(t, e) for e in nearest] for t in range(1, last + 1)]

    ra = 96
    rb = 128 - ra

    def rows_a(yy, zs=slice(None)):
        return left.at[core, :, yy, zs, pl.ds(0, ra)]

    def rows_b(yy, begin=0, size=rb):
        return left.at[core, pair, yy, odd, pl.ds(ra + begin, size)]

    own_a = left.at[core, pair, y, odd, pl.ds(0, ra)]
    za = along_z(lambda zz: own_a, za_s, za_r)
    zb = along_z(lambda zz: rows_b(pl.ds(0, ny)), zb_s, zb_r)
    ya, yb, late = [], [], []

    def both_ways(t, a, b, send, recv):
        return [
            copy(a, a, send.at[t - 1, 0], recv.at[t - 1, 0], w_up, narrow),
            copy(b, b, send.at[t - 1, 1], recv.at[t - 1, 1], w_down, narrow),
        ]

    for t in range(1, last + 1):
        up, down = passed(t)
        if t < last:
            a, b = rows_a(up), rows_a(down)
        else:
            a, b = rows_a(up, pl.ds(0, 1)), rows_a(down, pl.ds(1, 1))
        ya.append(both_ways(t, a, b, ya_s, ya_r))
        a, b = (rows_b(up), rows_b(down)) if t < last else (rows_b(up, 0, rb // 2), rows_b(down, rb // 2, rb // 2))
        yb.append(both_ways(t, a, b, yb_s, yb_r))
        zs = (pl.ds(0, nz), pl.ds(0, nz)) if t < last else (pl.ds(0, nz // 2), pl.ds(nz // 2, nz // 2))
        a, b = right.at[1 - odd, zs[0], up], right.at[1 - odd, zs[1], down]
        late.append(both_ways(t, a, b, late_s, late_r))
    shares = []

    def share(ref):
        at = len(shares)
        c = copy(ref, ref, share_s.at[at], share_r.at[at], sibling, narrow)
        c.start()
        shares.append(c)

    sib[0].wait_recv()
    start(yr[0][0])
    start(zr)
    fetches[0].wait()
    for h in range(2):

        @pl.when(core == h)
        def _():
            turned[rows_g, :] = grad[:, h * block : (h + 1) * block]

    start(rows_out)
    sib[1].wait_recv()
    start(yb[0])
    start(za)
    for at, e in enumerate(nearest):
        if at > 0:
            zr[e - 1].wait_recv()
            start(yr[0][at])
    start(zlate)
    b_step = 1

    def next_b(t):
        landed(yb[t - 1])
        if t < last:
            start(yb[t])
        else:
            start(zb)
            share(rows_b(pl.ds(0, ny)))

    for t in range(2, last + 1):
        for at in range(nz):
            landed(yr[t - 2][at])
            start(yr[t - 1][at])
            if at == nz - 1 and b_step < last:
                next_b(b_step)
                b_step += 1
    landed(za)
    start(ya[0])
    for at in range(nz):
        landed(yr[last - 1][at])
    while b_step <= last:
        next_b(b_step)
        b_step += 1
    share(rows_a(y))

    landed(rows_out)
    lands = slabs.at[pl.ds(narrow * nq + place - odd, 2)]
    high_far = 1 - high
    n_far = x * NH + high_far
    first_to = (nq // 2) * (2 * core + odd)

    wide_n = min(256, hb)
    some = wide_n // 32

    def send_near(begin, t, carry):
        j = begin + lax.rem(2 * y + pair + t, some)
        to = first_to + j

        @pl.when(to != wide)
        def _():
            copy(outgoing.at[j], lands, out_s.at[0], out_r.at[0], to, narrow).start()

        @pl.when(to == wide)
        def _():
            pltpu.make_async_copy(outgoing.at[j], lands, own_sem.at[0]).start()

        return carry

    def send_far(t, carry):
        j = lax.rem(2 * y + pair + t, nq // 2)
        copy(outgoing.at[j], lands, out_s.at[1], out_r.at[1], first_to + j, n_far).start()
        return carry

    for at in range(0, hb, wide_n):
        basis = right[odd, :, :, :, at : at + wide_n].reshape(block, wide_n)
        value = jnp.dot(turned[...], basis, preferred_element_type=F32).T.astype(BF16)
        for d in range(2):
            outgoing[at // 32 : at // 32 + some, d] = value[:, d * 128 : (d + 1) * 128].reshape(some, 32, 128)
        lax.fori_loop(0, some, functools.partial(send_near, at // 32), 0)
    lax.fori_loop(0, nq // 2, send_far, 0)

    def wait_near(ref, base, send, recv, sending, some_own=has_own, own_many=1):
        def wait(many):
            there = ref.at[pl.ds(base, many)]
            c = copy(there, there, send, recv, sibling, narrow)
            if sending:
                c.wait_send()
            else:
                c.wait_recv()

        @pl.when(some_own)
        def _():
            wait(nq - own_many)

        @pl.when(jnp.logical_not(some_own))
        def _():
            wait(nq)

    def wait_far(ref, base, send, recv, sending):
        there = ref.at[pl.ds(base, nq)]
        c = copy(there, there, send, recv, sibling, narrow)
        if sending:
            c.wait_send()
        else:
            c.wait_recv()

    def next_a(t):
        landed(ya[t - 1])
        if t < last:
            start(ya[t])
            for yy in passed(t + 1):
                share(rows_a(yy))
        else:
            share(rows_a(lax.rem(y + last, ny)))

    hq = nq // 2

    def slab_at(xx, g):
        return (xx * NH + g) * nq

    def ring_x(g, at):
        own = [slabs.at[pl.ds(slab_at(x, g) + h * hq, hq)] for h in range(2)]
        from_down = slabs.at[pl.ds(slab_at(x_down, g), hq)]
        from_up = slabs.at[pl.ds(slab_at(x_up, g) + hq, hq)]
        made = [
            (own[0], n_up),
            (own[1], n_down),
            (own[1], n_up),
            (own[0], n_down),
            (from_down, n_up),
            (from_up, n_down),
        ]
        return [copy(a, a, ring_s.at[at, i], ring_r.at[at, i], wide, nn) for i, (a, nn) in enumerate(made)]

    ring_near, ring_far = ring_x(high, 0), ring_x(high_far, 1)
    wait_near(slabs, slab_at(x, high), out_s.at[0], out_r.at[0], False, sends_own, 2)

    @pl.when(sends_own)
    def _():
        pltpu.make_async_copy(outgoing.at[0], lands, own_sem.at[0]).wait()

    start(ring_near[:4])
    next_a(1)
    landed(ring_near[:2])
    start(ring_near[4:])
    wait_far(slabs, slab_at(x, high_far), out_s.at[1], out_r.at[1], False)
    start(ring_far[:4])
    for t in range(2, last):
        next_a(t)
    landed(ring_far[:2])
    start(ring_far[4:])
    if last > 1:
        next_a(last)
    landed(zb)
    for d in range(1, nz):
        zz = lax.rem(z + nz - d, nz)
        share(left.at[core, zz // 2, pl.ds(0, ny), lax.rem(zz, 2), pl.ds(ra, rb)])
    landed(zlate)
    start(late[0])
    landed(ring_near[2:])
    landed(shares)
    landed(ring_far[2:])

    total[...] = jnp.zeros_like(total)
    deep = 4

    def rotate(i, carry):
        at = i * deep
        zz, yy = i // (2 * ny // deep), lax.rem(i, 2 * ny // deep) * (deep // 2)
        lhs = jnp.concatenate(
            [
                jnp.concatenate([slabs[s * nq + at + d] for s in range(NX * NH)], axis=0)
                for d in range(deep)
            ],
            axis=1,
        )
        for h in range(2):
            rhs = left[h, zz, pl.ds(yy, deep // 2)].reshape(deep * 128, half)
            total[:, h * half : (h + 1) * half] += jnp.dot(lhs, rhs, preferred_element_type=F32)
        return carry

    def next_late(t):
        landed(late[t - 1])
        if t < last:
            start(late[t])

    lax.fori_loop(0, nq // deep, rotate, 0)
    next_late(1)
    fetches[7].wait()
    fetches[8].wait()

    def moments(s, carry):
        there = pl.ds(pl.multiple_of(s * 32, 32), 32)
        value = total[there, :]
        m = BETA_ONE * first[s] + (1.0 - BETA_ONE) * value
        v = BETA_TWO * second[s] + (1.0 - BETA_TWO) * value * value
        new_first[s] = m
        new_second[s] = v
        direction[there, :] = (m / (jnp.sqrt(v) + EPSILON)).astype(BF16)
        return carry

    lax.fori_loop(0, NX * NH, moments, 0)
    stores = [pltpu.make_async_copy(held[i], outputs[1 + i], fetch_sem.at[9 + i]) for i in range(2)]
    for c in stores:
        c.start()

    def rotate_back(i, carry):
        at = i * 2
        zz, yy = i // ny, lax.rem(i, ny)
        value = None
        for h in range(2):
            rhs = left[h, zz, yy].reshape(256, half)
            term = lax.dot_general(
                direction[:, h * half : (h + 1) * half],
                rhs,
                (((1,), (1,)), ((), ())),
                preferred_element_type=F32,
            )
            value = term if value is None else value + term
        value = value.astype(BF16)
        for s in range(NX * NH):
            for d in range(2):
                partial[s * nq + at + d] = value[s * 32 : (s + 1) * 32, d * 128 : (d + 1) * 128]
        return carry

    def sums_of(g, at):
        def part(xx, h):
            return partial.at[pl.ds(slab_at(xx, g) + h * hq, hq)]

        lower, upper = pl.ds(0, hq), pl.ds(hq, hq)
        made = [
            (part(x_far, 0), halfway.at[at, 0], n_up),
            (part(x_far, 1), halfway.at[at, 1], n_down),
            (part(x_down, 0), arrived.at[at, 1, lower], n_down),
            (part(x_up, 1), arrived.at[at, 0, upper], n_up),
            (part(x_up, 0), arrived.at[at, 0, lower], n_up),
            (part(x_down, 1), arrived.at[at, 1, upper], n_down),
        ]
        return [copy(a, b, sum_s.at[at, i], sum_r.at[at, i], wide, nn) for i, (a, b, nn) in enumerate(made)]

    sums_far, sums_near = sums_of(high_far, 0), sums_of(high, 1)
    few = min(8, hq)

    def pass_on(g, at):
        def some(i, carry):
            for h, base in ((0, slab_at(x_up, g)), (1, slab_at(x_down, g) + hq)):
                there = pl.ds(base + i * few, few)
                held = halfway[at, h, pl.ds(i * few, few)]
                partial[there] = (partial[there].astype(F32) + held.astype(F32)).astype(BF16)
            return carry

        lax.fori_loop(0, hq // few, some, 0)

    def add_up(g, at):
        def some(i, carry):
            there = pl.ds(i * few, few)
            value = partial[pl.ds(slab_at(x, g) + i * few, few)].astype(F32) + arrived[at, 0, there].astype(F32)
            home[pl.ds(at * nq + i * few, few)] = (value + arrived[at, 1, there].astype(F32)).astype(BF16)
            return carry

        lax.fori_loop(0, nq // few, some, 0)

    lax.fori_loop(0, nq // 4, rotate_back, 0)
    start((sums_far[0], sums_far[2]))
    lax.fori_loop(nq // 4, nq // 2, rotate_back, 0)
    next_late(2)
    start((sums_far[1], sums_far[3]))
    start(sums_near[:2])
    landed(sums_far[:2])
    pass_on(high_far, 0)
    start(sums_far[4:])
    start(sums_near[2:4])
    landed(sums_near[:2])
    pass_on(high, 1)
    start(sums_near[4:])
    for t in range(3, last + 1):
        next_late(t)

    goes_to = high * nq + lax.rem(wide, nq)

    def owner(at):
        zz, yy = at // (2 * ny) * 2 + lax.rem(at, 2), lax.rem(at // 2, ny)
        return wide_at(zz, yy, side)

    def back_far(t, carry):
        at = lax.rem(place + t, nq)
        copy(home.at[at], back.at[goes_to], back_s.at[1], back_r.at[1], owner(at), n_far).start()
        return carry

    def back_near(t, carry):
        at = lax.rem(place + t, nq)
        to = owner(at)
        src = home.at[nq + at]

        @pl.when(to != wide)
        def _():
            copy(src, back.at[goes_to], back_s.at[0], back_r.at[0], to, narrow).start()

        @pl.when(to == wide)
        def _():
            pltpu.make_async_copy(src, back.at[goes_to], own_sem.at[1]).start()

        return carry

    landed(sums_far[2:])
    add_up(high_far, 0)
    lax.fori_loop(0, nq, back_far, 0)
    landed(sums_near[2:])
    add_up(high, 1)
    lax.fori_loop(0, nq, back_near, 0)
    wait_far(back, high_far * nq, back_s.at[1], back_r.at[1], False)
    wait_near(back, high * nq, back_s.at[0], back_r.at[0], False)

    @pl.when(has_own)
    def _():
        pltpu.make_async_copy(home.at[0], back.at[goes_to], own_sem.at[1]).wait()

    turned_back = (back[0:nq].astype(F32) + back[nq : 2 * nq].astype(F32)).astype(BF16).reshape(block, 128)
    tall = ny * 32
    swaps = []
    for zz in range(nz):
        value = sum(
            jnp.dot(
                right[h, zz].reshape(tall, hb), turned_back[h * hb : (h + 1) * hb], preferred_element_type=F32
            )
            for h in range(2)
        )
        value = value.T.astype(BF16)
        result[zz, 0] = value[0:64]
        result[zz, 1] = value[64:128]
        there = update.at[:, pl.ds(pl.multiple_of(core * block + zz * tall, tall), tall)]
        swap = copy(result.at[zz, other], there, swap_s.at[zz], swap_r.at[zz], sibling, narrow)
        swap.start()
        swaps.append(swap)
        store = pltpu.make_async_copy(result.at[zz, core], there, fetch_sem.at[11 + zz])
        store.start()
        stores.append(store)
    landed(swaps)

    sent = sib + rows_out + zr + zlate + za + zb + [c for step in yr for part in step for c in part]
    sent += [c for part in ya + yb + late for c in part] + shares + ring_near + ring_far + sums_near + sums_far + swaps
    for c in sent:
        c.wait_send()
    for c in stores:
        c.wait()
    wait_near(slabs, slab_at(x, high), out_s.at[0], out_r.at[0], True, sends_own, 2)
    wait_far(slabs, slab_at(x, high_far), out_s.at[1], out_r.at[1], True)
    wait_near(back, high * nq, back_s.at[0], back_r.at[0], True)
    wait_far(back, high_far * nq, back_s.at[1], back_r.at[1], True)


def solution(mesh):
    nz, ny = 4, mesh.shape["wide"] // 8

    def step(*args):
        return body(nz, ny, *args)

    placed = (
        P("wide", "narrow"),
        P("wide", "narrow"),
        P("wide", "narrow"),
        P("wide", "narrow"),
        P("narrow", "wide", None),
        P("narrow", "wide", None),
        P("narrow", "wide", None),
        P(None, "wide", "narrow"),
        P(None, "wide", "narrow"),
    )
    return jax.shard_map(
        step,
        mesh=mesh,
        in_specs=placed,
        out_specs=(P("wide", "narrow"), P(None, "wide", "narrow"), P(None, "wide", "narrow")),
        check_vma=False,
    )


def body(nz, ny, *args):
    nq = nz * ny
    block, span = 32 * nq, args[1].shape[1]
    half = span // 2
    slabs = NX * NH
    dma = pltpu.SemaphoreType.DMA
    steps = ny // 2
    anywhere = pl.BlockSpec(memory_space=pl.ANY)
    args = list(args)
    args[2] = args[2].T
    args[5] = jnp.swapaxes(args[5], 1, 2)
    return pl.pallas_call(
        functools.partial(kernel, nz, ny),
        out_shape=(
            jax.ShapeDtypeStruct(args[0].shape, BF16),
            jax.ShapeDtypeStruct(args[7].shape, F32),
            jax.ShapeDtypeStruct(args[8].shape, F32),
        ),
        in_specs=[anywhere] * 9,
        out_specs=(anywhere,) * 3,
        scratch_shapes=[pltpu.VMEM(a.shape, a.dtype) for a in args + args[7:9]]
        + [
            pltpu.VMEM((256, block), BF16),
            pltpu.VMEM((2, nz, ny, 32, block // 2), BF16),
            pltpu.VMEM((2, nz // 2, ny, 2, 128, half), BF16),
            pltpu.VMEM((2, 16, block // 2), BF16),
            pltpu.VMEM((64, half), BF16),
            pltpu.VMEM((nq // 2, 2, 32, 128), BF16),
            pltpu.VMEM((slabs * nq, 32, 128), BF16),
            pltpu.VMEM((slabs * 32, span), F32),
            pltpu.VMEM((slabs * 32, span), BF16),
            pltpu.VMEM((slabs * nq, 32, 128), BF16),
            pltpu.VMEM((NH, 2, nq // 2, 32, 128), BF16),
            pltpu.VMEM((NH, 2, nq, 32, 128), BF16),
            pltpu.VMEM((NH * nq, 32, 128), BF16),
            pltpu.VMEM((NH * nq, 32, 128), BF16),
            pltpu.VMEM((nz, 2, 64, ny * 32), BF16),
            dma((11 + nz,)),
            dma((2,)),
            dma((2,)),
            dma((nz,)),
            dma((nz,)),
            dma((3,)),
            dma((3,)),
        ]
        + [dma((nz - 1,))] * 8
        + [dma((steps, nz, 2))] * 2
        + [dma((steps, 2))] * 6
        + [dma((ny + nz,))] * 2
        + [dma((2,))] * 5
        + [dma((2, 6))] * 4,
        compiler_params=pltpu.CompilerParams(
            collective_id=0, has_side_effects=True, vmem_limit_bytes=58 * 1024 * 1024
        ),
        cost_estimate=pl.CostEstimate(flops=2_700_000_000, bytes_accessed=8_000_000, transcendentals=131072),
    )(*args)
```

```python
import functools
import math

import jax
import jax.numpy as jnp
from jax import lax
from jax.experimental import pallas as pl
from jax.experimental.pallas import tpu as pltpu
from jax.sharding import PartitionSpec as P

MESH = pl.DeviceIdType.MESH
F32, BF16 = jnp.float32, jnp.bfloat16
BETA_ONE = 0.95
BETA_TWO = 0.95
EPSILON = 1e-08
NX = 4
NH = 2


def dequantized(codes, scales, error, quantum):
    groups, columns = scales.shape[0], codes.shape[1]
    column = lax.broadcasted_iota(jnp.int32, (groups, columns), 1) // (columns // groups)
    spread = (column == lax.broadcasted_iota(jnp.int32, (groups, columns), 0)).astype(F32).astype(BF16)
    expanded = lax.dot_general(
        scales.astype(F32).astype(BF16), spread, (((0,), (0,)), ((), ())), preferred_element_type=F32
    )
    return (codes.astype(F32) * expanded * quantum + error.astype(F32)).astype(BF16)


def kernel(nz, ny, *refs):
    inputs, refs = refs[:9], refs[9:]
    outputs, fetched, held, refs = refs[:3], refs[3:12], refs[12:14], refs[14:]
    update, (new_first, new_second) = outputs[0], held
    grad, lcodes, lscales, lerror, rcodes, rscales, rerror, first, second = fetched
    (
        turned,
        right,
        left,
        rstage,
        lstage,
        outgoing,
        slabs,
        total,
        direction,
        partial,
        halfway,
        arrived,
        home,
        back,
        result,
    ) = refs[:15]
    (
        fetch_sem,
        sib_s,
        sib_r,
        swap_s,
        swap_r,
        grad_s,
        grad_r,
        zr_s,
        zr_r,
        zl_s,
        zl_r,
        za_s,
        za_r,
        zb_s,
        zb_r,
        yr_s,
        yr_r,
        late_s,
        late_r,
        ya_s,
        ya_r,
        yb_s,
        yb_r,
        share_s,
        share_r,
        out_s,
        out_r,
        back_s,
        back_r,
        own_sem,
        ring_s,
        ring_r,
        sum_s,
        sum_r,
    ) = refs[15:]
    nq = nz * ny
    block = 32 * nq
    order = 128 * nq
    span = lcodes.shape[1]
    half = span // 2
    hb = block // 2
    wide, narrow = lax.axis_index("wide"), lax.axis_index("narrow")
    core, chip = lax.rem(wide, 2), wide // 2
    z, y = chip // ny, lax.rem(chip, ny)
    x, high = narrow // NH, lax.rem(narrow, NH)
    other = 1 - core
    pair, odd = z // 2, lax.rem(z, 2)
    place = (pair * ny + y) * 2 + odd
    side = wide // nq
    has_own = side == core
    sends_own = wide // (nq // 2) == 2 * core + odd

    fetches = [pltpu.make_async_copy(a, b, fetch_sem.at[i]) for i, (a, b) in enumerate(zip(inputs, fetched))]
    for i in (4, 5, 6, 1, 2, 3, 0, 7, 8):
        fetches[i].start()

    def wide_at(zz, yy, cc):
        return (zz * ny + yy) * 2 + cc

    def copy(src, dst, send, recv, ww, nn):
        return pltpu.make_async_remote_copy(
            src_ref=src, dst_ref=dst, send_sem=send, recv_sem=recv, device_id=(ww, nn), device_id_type=MESH
        )

    def start(copies):
        for c in copies:
            c.start()

    def landed(copies):
        for c in copies:
            c.wait_recv()

    sibling = wide + 1 - 2 * core
    y_up, y_down = lax.rem(y + 1, ny), lax.rem(y + ny - 1, ny)
    x_up, x_down = lax.rem(x + 1, NX), lax.rem(x + NX - 1, NX)
    x_far = lax.rem(x + 2, NX)
    n_up, n_down = x_up * NH + high, x_down * NH + high
    w_up, w_down = wide_at(z, y_up, core), wide_at(z, y_down, core)

    barrier = pltpu.get_barrier_semaphore()
    plane = 2 * nq * NH

    for extra in range(NH):
        nn = x * NH + lax.rem(high + extra, NH)

        def greet(i, carry):
            there = wide + i
            there = jnp.where(there >= 2 * nq, there - 2 * nq, there)
            pl.semaphore_signal(barrier, inc=1, device_id=(there, nn), device_id_type=MESH)
            return carry

        lax.fori_loop(1 if extra == 0 else 0, 2 * nq, greet, 0)
    for nn in (n_up, n_down):
        pl.semaphore_signal(barrier, inc=1, device_id=(wide, nn), device_id_type=MESH)

    rows16 = pl.ds(pl.multiple_of(core * 16, 16), 16)
    rows64 = pl.ds(pl.multiple_of(core * 64, 64), 64)
    quantum = 1.0 / (16.0 * math.sqrt(block))
    for i in (4, 5, 6):
        fetches[i].wait()
    for ref, which in ((rstage, other), (right.at[:, z, y, rows16, :], core)):
        value = dequantized(rcodes[which], rscales[which], rerror[which], quantum)
        for h in range(2):
            ref[h] = value[:, h * hb : (h + 1) * hb]
    pl.semaphore_wait(barrier, plane - 1 + 2)
    sib = [
        copy(rstage, right.at[:, z, y, rows16, :], sib_s.at[0], sib_r.at[0], sibling, narrow),
        copy(lstage, left.at[other, pair, y, odd, rows64, :], sib_s.at[1], sib_r.at[1], sibling, narrow),
    ]
    rows_g = pl.ds(pl.multiple_of(odd * 128 + core * 64, 64), 64)
    beside = wide_at(z + 1 - 2 * odd, y, core)
    own_block = grad.at[:, pl.ds(pl.multiple_of(core * block, block), block)]
    other_block = grad.at[:, pl.ds(pl.multiple_of(other * block, block), block)]
    rows_out = [
        copy(other_block, turned.at[rows_g, :], grad_s.at[0], grad_r.at[0], sibling, narrow),
        copy(own_block, turned.at[rows_g, :], grad_s.at[1], grad_r.at[1], beside, narrow),
        copy(other_block, turned.at[rows_g, :], grad_s.at[2], grad_r.at[2], beside + 1 - 2 * core, narrow),
    ]
    last = ny // 2

    def along_z(ref_for, send, recv):
        made = []
        for d in range(1, nz):
            ref = ref_for(lax.rem(z + d, nz))
            made.append(copy(ref, ref, send.at[d - 1], recv.at[d - 1], wide_at(lax.rem(z + d, nz), y, core), narrow))
        return made

    def passed(t):
        return lax.rem(y + ny - (t - 1), ny), lax.rem(y + (t - 1), ny)

    nearest = [0, 1, nz - 1][: min(nz, 3)] + list(range(2, nz - 1))
    if nz == 2:
        nearest = [0, 1]
    def rows_to_line(which, send, recv):
        made = []
        for d in range(1, nz):
            zz = lax.rem(z + d, nz)
            h = lax.rem(zz + which, 2)
            dst = right.at[h, z, y, rows16, :]
            both = ((dst, core), (rstage.at[h], other))
            made.append(
                [
                    copy(src, dst, send.at[d - 1, i], recv.at[d - 1, i], wide_at(zz, y, cc), narrow)
                    for i, (src, cc) in enumerate(both)
                ]
            )
        return made

    zr = rows_to_line(0, zr_s, zr_r)
    zlate = rows_to_line(1, zl_s, zl_r)

    sib[0].start()
    for e in nearest[1:]:
        start(zr[e - 1])
    quantum = 1.0 / (16.0 * math.sqrt(order))
    for i in (1, 2, 3):
        fetches[i].wait()
    value = dequantized(lcodes[...], lscales[...], lerror[...], quantum)
    for h in range(2):

        @pl.when(core == h)
        def _():
            left[h, pair, y, odd, rows64, :] = value[:, h * half : (h + 1) * half]

        @pl.when(core != h)
        def _():
            lstage[...] = value[:, h * half : (h + 1) * half]

    sib[1].start()

    def ring_right(t, e):
        zz = lax.rem(z + nz - e, nz)
        at = nearest.index(e)
        made = []
        for way, (yy, ww) in enumerate(zip(passed(t), (w_up, w_down))):
            if t < last or (at < nz // 2) == (way == 0):
                ref = right.at[odd, zz, yy]
                made.append(copy(ref, ref, yr_s.at[t - 1, e, way], yr_r.at[t - 1, e, way], ww, narrow))
        return made

    yr = [[ring_right(t, e) for e in nearest] for t in range(1, last + 1)]

    ra = 96
    rb = 128 - ra

    def rows_a(yy, zs=slice(None)):
        return left.at[core, :, yy, zs, pl.ds(0, ra)]

    def rows_b(yy, begin=0, size=rb):
        return left.at[core, pair, yy, odd, pl.ds(ra + begin, size)]

    own_a = left.at[core, pair, y, odd, pl.ds(0, ra)]
    za = along_z(lambda zz: own_a, za_s, za_r)
    zb = along_z(lambda zz: rows_b(pl.ds(0, ny)), zb_s, zb_r)
    ya, yb, late = [], [], []

    def both_ways(t, a, b, send, recv):
        return [
            copy(a, a, send.at[t - 1, 0], recv.at[t - 1, 0], w_up, narrow),
            copy(b, b, send.at[t - 1, 1], recv.at[t - 1, 1], w_down, narrow),
        ]

    for t in range(1, last + 1):
        up, down = passed(t)
        if t < last:
            a, b = rows_a(up), rows_a(down)
        else:
            a, b = rows_a(up, pl.ds(0, 1)), rows_a(down, pl.ds(1, 1))
        ya.append(both_ways(t, a, b, ya_s, ya_r))
        a, b = (rows_b(up), rows_b(down)) if t < last else (rows_b(up, 0, rb // 2), rows_b(down, rb // 2, rb // 2))
        yb.append(both_ways(t, a, b, yb_s, yb_r))
        zs = (pl.ds(0, nz), pl.ds(0, nz)) if t < last else (pl.ds(0, nz // 2), pl.ds(nz // 2, nz // 2))
        a, b = right.at[1 - odd, zs[0], up], right.at[1 - odd, zs[1], down]
        late.append(both_ways(t, a, b, late_s, late_r))
    shares = []

    def share(ref):
        at = len(shares)
        c = copy(ref, ref, share_s.at[at], share_r.at[at], sibling, narrow)
        c.start()
        shares.append(c)

    sib[0].wait_recv()
    start(yr[0][0])
    fetches[0].wait()
    for h in range(2):

        @pl.when(core == h)
        def _():
            turned[rows_g, :] = grad[:, h * block : (h + 1) * block]

    start(rows_out)
    sib[1].wait_recv()
    start(yb[0])
    start(za)
    for at, e in enumerate(nearest):
        if at > 0:
            landed(zr[e - 1])
            start(yr[0][at])
    for part in zlate:
        start(part)
    b_step = 1

    def next_b(t):
        landed(yb[t - 1])
        if t < last:
            start(yb[t])
        else:
            start(zb)
            share(rows_b(pl.ds(0, ny)))

    for t in range(2, last + 1):
        for at in range(nz):
            landed(yr[t - 2][at])
            start(yr[t - 1][at])
            if at % 2 == 1 and b_step <= last and t < last:
                next_b(b_step)
                b_step += 1
    while b_step <= last:
        next_b(b_step)
        b_step += 1
    landed(za)
    start(ya[0])
    share(rows_a(y))
    for at in range(nz):
        landed(yr[last - 1][at])

    landed(rows_out)
    lands = slabs.at[pl.ds(narrow * nq + place - odd, 2)]
    high_far = 1 - high
    n_far = x * NH + high_far
    first_to = (nq // 2) * (2 * core + odd)

    wide_n = min(256, hb)
    some = wide_n // 32

    def send_near(begin, t, carry):
        j = begin + lax.rem(2 * y + pair + t, some)
        to = first_to + j

        @pl.when(to != wide)
        def _():
            copy(outgoing.at[j], lands, out_s.at[0], out_r.at[0], to, narrow).start()

        @pl.when(to == wide)
        def _():
            pltpu.make_async_copy(outgoing.at[j], lands, own_sem.at[0]).start()

        return carry

    def send_far(t, carry):
        j = lax.rem(2 * y + pair + t, nq // 2)
        copy(outgoing.at[j], lands, out_s.at[1], out_r.at[1], first_to + j, n_far).start()
        return carry

    for at in range(0, hb, wide_n):
        basis = right[odd, :, :, :, at : at + wide_n].reshape(block, wide_n)
        value = jnp.dot(turned[...], basis, preferred_element_type=F32).T.astype(BF16)
        for d in range(2):
            outgoing[at // 32 : at // 32 + some, d] = value[:, d * 128 : (d + 1) * 128].reshape(some, 32, 128)
        lax.fori_loop(0, some, functools.partial(send_near, at // 32), 0)
    lax.fori_loop(0, nq // 2, send_far, 0)

    def wait_near(ref, base, send, recv, sending, some_own=has_own, own_many=1):
        def wait(many):
            there = ref.at[pl.ds(base, many)]
            c = copy(there, there, send, recv, sibling, narrow)
            if sending:
                c.wait_send()
            else:
                c.wait_recv()

        @pl.when(some_own)
        def _():
            wait(nq - own_many)

        @pl.when(jnp.logical_not(some_own))
        def _():
            wait(nq)

    def wait_far(ref, base, send, recv, sending):
        there = ref.at[pl.ds(base, nq)]
        c = copy(there, there, send, recv, sibling, narrow)
        if sending:
            c.wait_send()
        else:
            c.wait_recv()

    def next_a(t):
        landed(ya[t - 1])
        if t < last:
            start(ya[t])
            for yy in passed(t + 1):
                share(rows_a(yy))
        else:
            share(rows_a(lax.rem(y + last, ny)))

    hq = nq // 2

    def slab_at(xx, g):
        return (xx * NH + g) * nq

    def ring_x(g, at):
        own = [slabs.at[pl.ds(slab_at(x, g) + h * hq, hq)] for h in range(2)]
        from_down = slabs.at[pl.ds(slab_at(x_down, g), hq)]
        from_up = slabs.at[pl.ds(slab_at(x_up, g) + hq, hq)]
        made = [
            (own[0], n_up),
            (own[1], n_down),
            (own[1], n_up),
            (own[0], n_down),
            (from_down, n_up),
            (from_up, n_down),
        ]
        return [copy(a, a, ring_s.at[at, i], ring_r.at[at, i], wide, nn) for i, (a, nn) in enumerate(made)]

    ring_near, ring_far = ring_x(high, 0), ring_x(high_far, 1)
    next_a(1)
    wait_near(slabs, slab_at(x, high), out_s.at[0], out_r.at[0], False, sends_own, 2)

    @pl.when(sends_own)
    def _():
        pltpu.make_async_copy(outgoing.at[0], lands, own_sem.at[0]).wait()

    start(ring_near[:4])
    if last > 1:
        next_a(2)
    landed(ring_near[:2])
    start(ring_near[4:])
    if last > 2:
        next_a(3)
    wait_far(slabs, slab_at(x, high_far), out_s.at[1], out_r.at[1], False)
    start(ring_far[:4])
    for t in range(4, last + 1):
        next_a(t)
    landed(zb)
    for d in range(1, nz):
        zz = lax.rem(z + nz - d, nz)
        share(left.at[core, zz // 2, pl.ds(0, ny), lax.rem(zz, 2), pl.ds(ra, rb)])
    landed(ring_far[:2])
    start(ring_far[4:])
    for part in zlate:
        landed(part)
    start(late[0])
    landed(ring_near[2:])
    landed(shares)
    landed(ring_far[2:])

    total[...] = jnp.zeros_like(total)
    deep = 4

    def rotate(i, carry):
        at = i * deep
        zz, yy = i // (2 * ny // deep), lax.rem(i, 2 * ny // deep) * (deep // 2)
        lhs = jnp.concatenate(
            [
                jnp.concatenate([slabs[s * nq + at + d] for s in range(NX * NH)], axis=0)
                for d in range(deep)
            ],
            axis=1,
        )
        for h in range(2):
            rhs = left[h, zz, pl.ds(yy, deep // 2)].reshape(deep * 128, half)
            total[:, h * half : (h + 1) * half] += jnp.dot(lhs, rhs, preferred_element_type=F32)
        return carry

    def next_late(t):
        landed(late[t - 1])
        if t < last:
            start(late[t])

    lax.fori_loop(0, nq // deep, rotate, 0)
    fetches[7].wait()
    fetches[8].wait()

    def moments(s, carry):
        there = pl.ds(pl.multiple_of(s * 32, 32), 32)
        value = total[there, :]
        m = BETA_ONE * first[s] + (1.0 - BETA_ONE) * value
        v = BETA_TWO * second[s] + (1.0 - BETA_TWO) * value * value
        new_first[s] = m
        new_second[s] = v
        direction[there, :] = (m / (jnp.sqrt(v) + EPSILON)).astype(BF16)
        return carry

    lax.fori_loop(0, NX * NH, moments, 0)
    stores = [pltpu.make_async_copy(held[i], outputs[1 + i], fetch_sem.at[9 + i]) for i in range(2)]
    for c in stores:
        c.start()

    def rotate_back(i, carry):
        at = i * 2
        zz, yy = i // ny, lax.rem(i, ny)
        value = None
        for h in range(2):
            rhs = left[h, zz, yy].reshape(256, half)
            term = lax.dot_general(
                direction[:, h * half : (h + 1) * half],
                rhs,
                (((1,), (1,)), ((), ())),
                preferred_element_type=F32,
            )
            value = term if value is None else value + term
        value = value.astype(BF16)
        for s in range(NX * NH):
            for d in range(2):
                partial[s * nq + at + d] = value[s * 32 : (s + 1) * 32, d * 128 : (d + 1) * 128]
        return carry

    def sums_of(g, at):
        def part(xx, h):
            return partial.at[pl.ds(slab_at(xx, g) + h * hq, hq)]

        lower, upper = pl.ds(0, hq), pl.ds(hq, hq)
        made = [
            (part(x_far, 0), halfway.at[at, 0], n_up),
            (part(x_far, 1), halfway.at[at, 1], n_down),
            (part(x_down, 0), arrived.at[at, 1, lower], n_down),
            (part(x_up, 1), arrived.at[at, 0, upper], n_up),
            (part(x_up, 0), arrived.at[at, 0, lower], n_up),
            (part(x_down, 1), arrived.at[at, 1, upper], n_down),
        ]
        return [copy(a, b, sum_s.at[at, i], sum_r.at[at, i], wide, nn) for i, (a, b, nn) in enumerate(made)]

    sums_far, sums_near = sums_of(high_far, 0), sums_of(high, 1)
    few = min(8, hq)

    def pass_on(g, at):
        def some(i, carry):
            for h, base in ((0, slab_at(x_up, g)), (1, slab_at(x_down, g) + hq)):
                there = pl.ds(base + i * few, few)
                held = halfway[at, h, pl.ds(i * few, few)]
                partial[there] = (partial[there].astype(F32) + held.astype(F32)).astype(BF16)
            return carry

        lax.fori_loop(0, hq // few, some, 0)

    def add_up(g, at):
        def some(i, carry):
            there = pl.ds(i * few, few)
            value = partial[pl.ds(slab_at(x, g) + i * few, few)].astype(F32) + arrived[at, 0, there].astype(F32)
            home[pl.ds(at * nq + i * few, few)] = (value + arrived[at, 1, there].astype(F32)).astype(BF16)
            return carry

        lax.fori_loop(0, nq // few, some, 0)

    lax.fori_loop(0, nq // 4, rotate_back, 0)
    start((sums_far[0], sums_far[2]))
    lax.fori_loop(nq // 4, nq // 2, rotate_back, 0)
    start((sums_far[1], sums_far[3]))
    start(sums_near[:2])
    next_late(1)
    landed(sums_far[:2])
    pass_on(high_far, 0)
    start(sums_far[4:])
    start(sums_near[2:4])
    if last > 1:
        next_late(2)
    landed(sums_near[:2])
    pass_on(high, 1)
    start(sums_near[4:])
    for t in range(3, last):
        next_late(t)

    goes_to = high * nq + lax.rem(wide, nq)

    def owner(at):
        zz, yy = at // (2 * ny) * 2 + lax.rem(at, 2), lax.rem(at // 2, ny)
        return wide_at(zz, yy, side)

    def back_far(t, carry):
        at = lax.rem(place + t, nq)
        copy(home.at[at], back.at[goes_to], back_s.at[1], back_r.at[1], owner(at), n_far).start()
        return carry

    def back_near(t, carry):
        at = lax.rem(place + t, nq)
        to = owner(at)
        src = home.at[nq + at]

        @pl.when(to != wide)
        def _():
            copy(src, back.at[goes_to], back_s.at[0], back_r.at[0], to, narrow).start()

        @pl.when(to == wide)
        def _():
            pltpu.make_async_copy(src, back.at[goes_to], own_sem.at[1]).start()

        return carry

    landed(sums_far[2:])
    add_up(high_far, 0)
    lax.fori_loop(0, nq, back_far, 0)
    landed(sums_near[2:])
    add_up(high, 1)
    lax.fori_loop(0, nq, back_near, 0)
    if last > 2:
        next_late(last)
    wait_far(back, high_far * nq, back_s.at[1], back_r.at[1], False)
    wait_near(back, high * nq, back_s.at[0], back_r.at[0], False)

    @pl.when(has_own)
    def _():
        pltpu.make_async_copy(home.at[0], back.at[goes_to], own_sem.at[1]).wait()

    turned_back = (back[0:nq].astype(F32) + back[nq : 2 * nq].astype(F32)).astype(BF16).reshape(block, 128)
    tall = ny * 32
    swaps = []
    for zz in range(nz):
        value = sum(
            jnp.dot(
                right[h, zz].reshape(tall, hb), turned_back[h * hb : (h + 1) * hb], preferred_element_type=F32
            )
            for h in range(2)
        )
        value = value.T.astype(BF16)
        result[zz, 0] = value[0:64]
        result[zz, 1] = value[64:128]
        there = update.at[:, pl.ds(pl.multiple_of(core * block + zz * tall, tall), tall)]
        swap = copy(result.at[zz, other], there, swap_s.at[zz], swap_r.at[zz], sibling, narrow)
        swap.start()
        swaps.append(swap)
        store = pltpu.make_async_copy(result.at[zz, core], there, fetch_sem.at[11 + zz])
        store.start()
        stores.append(store)
    landed(swaps)

    sent = sib + rows_out + za + zb + [c for part in zr + zlate for c in part] + [c for step in yr for part in step for c in part]
    sent += [c for part in ya + yb + late for c in part] + shares + ring_near + ring_far + sums_near + sums_far + swaps
    for c in sent:
        c.wait_send()
    for c in stores:
        c.wait()
    wait_near(slabs, slab_at(x, high), out_s.at[0], out_r.at[0], True, sends_own, 2)
    wait_far(slabs, slab_at(x, high_far), out_s.at[1], out_r.at[1], True)
    wait_near(back, high * nq, back_s.at[0], back_r.at[0], True)
    wait_far(back, high_far * nq, back_s.at[1], back_r.at[1], True)


def solution(mesh):
    nz, ny = 4, mesh.shape["wide"] // 8

    def step(*args):
        return body(nz, ny, *args)

    placed = (
        P("wide", "narrow"),
        P("wide", "narrow"),
        P("wide", "narrow"),
        P("wide", "narrow"),
        P("narrow", "wide", None),
        P("narrow", "wide", None),
        P("narrow", "wide", None),
        P(None, "wide", "narrow"),
        P(None, "wide", "narrow"),
    )
    return jax.shard_map(
        step,
        mesh=mesh,
        in_specs=placed,
        out_specs=(P("wide", "narrow"), P(None, "wide", "narrow"), P(None, "wide", "narrow")),
        check_vma=False,
    )


def body(nz, ny, *args):
    nq = nz * ny
    block, span = 32 * nq, args[1].shape[1]
    half = span // 2
    slabs = NX * NH
    dma = pltpu.SemaphoreType.DMA
    steps = ny // 2
    anywhere = pl.BlockSpec(memory_space=pl.ANY)
    args = list(args)
    args[2] = args[2].T
    args[5] = jnp.swapaxes(args[5], 1, 2)
    return pl.pallas_call(
        functools.partial(kernel, nz, ny),
        out_shape=(
            jax.ShapeDtypeStruct(args[0].shape, BF16),
            jax.ShapeDtypeStruct(args[7].shape, F32),
            jax.ShapeDtypeStruct(args[8].shape, F32),
        ),
        in_specs=[anywhere] * 9,
        out_specs=(anywhere,) * 3,
        scratch_shapes=[pltpu.VMEM(a.shape, a.dtype) for a in args + args[7:9]]
        + [
            pltpu.VMEM((256, block), BF16),
            pltpu.VMEM((2, nz, ny, 32, block // 2), BF16),
            pltpu.VMEM((2, nz // 2, ny, 2, 128, half), BF16),
            pltpu.VMEM((2, 16, block // 2), BF16),
            pltpu.VMEM((64, half), BF16),
            pltpu.VMEM((nq // 2, 2, 32, 128), BF16),
            pltpu.VMEM((slabs * nq, 32, 128), BF16),
            pltpu.VMEM((slabs * 32, span), F32),
            pltpu.VMEM((slabs * 32, span), BF16),
            pltpu.VMEM((slabs * nq, 32, 128), BF16),
            pltpu.VMEM((NH, 2, nq // 2, 32, 128), BF16),
            pltpu.VMEM((NH, 2, nq, 32, 128), BF16),
            pltpu.VMEM((NH * nq, 32, 128), BF16),
            pltpu.VMEM((NH * nq, 32, 128), BF16),
            pltpu.VMEM((nz, 2, 64, ny * 32), BF16),
            dma((11 + nz,)),
            dma((2,)),
            dma((2,)),
            dma((nz,)),
            dma((nz,)),
            dma((3,)),
            dma((3,)),
        ]
        + [dma((nz - 1, 2))] * 4
        + [dma((nz - 1,))] * 4
        + [dma((steps, nz, 2))] * 2
        + [dma((steps, 2))] * 6
        + [dma((ny + nz,))] * 2
        + [dma((2,))] * 5
        + [dma((2, 6))] * 4,
        compiler_params=pltpu.CompilerParams(
            collective_id=0, has_side_effects=True, vmem_limit_bytes=58 * 1024 * 1024
        ),
        cost_estimate=pl.CostEstimate(flops=2_700_000_000, bytes_accessed=8_000_000, transcendentals=131072),
    )(*args)
```

```python
import functools
import math

import jax
import jax.numpy as jnp
from jax import lax
from jax.experimental import pallas as pl
from jax.experimental.pallas import tpu as pltpu
from jax.sharding import PartitionSpec as P

MESH = pl.DeviceIdType.MESH
F32, BF16 = jnp.float32, jnp.bfloat16
BETA_ONE = 0.95
BETA_TWO = 0.95
EPSILON = 1e-08
NX = 4
NH = 2


def dequantized(codes, scales, error, quantum):
    groups, columns = scales.shape[0], codes.shape[1]
    column = lax.broadcasted_iota(jnp.int32, (groups, columns), 1) // (columns // groups)
    spread = (column == lax.broadcasted_iota(jnp.int32, (groups, columns), 0)).astype(F32).astype(BF16)
    expanded = lax.dot_general(
        scales.astype(F32).astype(BF16), spread, (((0,), (0,)), ((), ())), preferred_element_type=F32
    )
    return (codes.astype(F32) * expanded * quantum + error.astype(F32)).astype(BF16)


def kernel(nz, ny, *refs):
    inputs, refs = refs[:9], refs[9:]
    outputs, fetched, held, refs = refs[:3], refs[3:12], refs[12:14], refs[14:]
    update, (new_first, new_second) = outputs[0], held
    grad, lcodes, lscales, lerror, rcodes, rscales, rerror, first, second = fetched
    (
        turned,
        right,
        left,
        rstage,
        lstage,
        outgoing,
        slabs,
        total,
        direction,
        partial,
        halfway,
        arrived,
        home,
        back,
        result,
    ) = refs[:15]
    (
        fetch_sem,
        sib_s,
        sib_r,
        swap_s,
        swap_r,
        grad_s,
        grad_r,
        zr_s,
        zr_r,
        zl_s,
        zl_r,
        za_s,
        za_r,
        zb_s,
        zb_r,
        yr_s,
        yr_r,
        late_s,
        late_r,
        ya_s,
        ya_r,
        yb_s,
        yb_r,
        share_s,
        share_r,
        out_s,
        out_r,
        back_s,
        back_r,
        own_sem,
        ring_s,
        ring_r,
        sum_s,
        sum_r,
    ) = refs[15:]
    nq = nz * ny
    block = 32 * nq
    order = 128 * nq
    span = lcodes.shape[1]
    half = span // 2
    hb = block // 2
    wide, narrow = lax.axis_index("wide"), lax.axis_index("narrow")
    core, chip = lax.rem(wide, 2), wide // 2
    z, y = chip // ny, lax.rem(chip, ny)
    x, high = narrow // NH, lax.rem(narrow, NH)
    other = 1 - core
    pair, odd = z // 2, lax.rem(z, 2)
    mine_half = 1 - odd
    place = (pair * ny + y) * 2 + odd
    side = wide // nq
    has_own = side == core
    sends_own = wide // (nq // 2) == 2 * core + mine_half

    fetches = [pltpu.make_async_copy(a, b, fetch_sem.at[i]) for i, (a, b) in enumerate(zip(inputs, fetched))]
    for i in (4, 5, 6, 1, 2, 3, 0, 7, 8):
        fetches[i].start()

    def wide_at(zz, yy, cc):
        return (zz * ny + yy) * 2 + cc

    def copy(src, dst, send, recv, ww, nn):
        return pltpu.make_async_remote_copy(
            src_ref=src, dst_ref=dst, send_sem=send, recv_sem=recv, device_id=(ww, nn), device_id_type=MESH
        )

    def start(copies):
        for c in copies:
            c.start()

    def landed(copies):
        for c in copies:
            c.wait_recv()

    sibling = wide + 1 - 2 * core
    y_up, y_down = lax.rem(y + 1, ny), lax.rem(y + ny - 1, ny)
    x_up, x_down = lax.rem(x + 1, NX), lax.rem(x + NX - 1, NX)
    x_far = lax.rem(x + 2, NX)
    n_up, n_down = x_up * NH + high, x_down * NH + high
    w_up, w_down = wide_at(z, y_up, core), wide_at(z, y_down, core)

    barrier = pltpu.get_barrier_semaphore()
    plane = 2 * nq * NH

    for extra in range(NH):
        nn = x * NH + lax.rem(high + extra, NH)

        def greet(i, carry):
            there = wide + i
            there = jnp.where(there >= 2 * nq, there - 2 * nq, there)
            pl.semaphore_signal(barrier, inc=1, device_id=(there, nn), device_id_type=MESH)
            return carry

        lax.fori_loop(1 if extra == 0 else 0, 2 * nq, greet, 0)
    for nn in (n_up, n_down):
        pl.semaphore_signal(barrier, inc=1, device_id=(wide, nn), device_id_type=MESH)

    rows16 = pl.ds(pl.multiple_of(core * 16, 16), 16)
    rows64 = pl.ds(pl.multiple_of(core * 64, 64), 64)
    quantum = 1.0 / (16.0 * math.sqrt(block))
    for i in (4, 5, 6):
        fetches[i].wait()
    for ref, which in ((rstage, other), (right.at[:, z, y, rows16, :], core)):
        value = dequantized(rcodes[which], rscales[which], rerror[which], quantum)
        for h in range(2):
            ref[h] = value[:, h * hb : (h + 1) * hb]
    pl.semaphore_wait(barrier, plane - 1 + 2)
    sib = [
        copy(rstage, right.at[:, z, y, rows16, :], sib_s.at[0], sib_r.at[0], sibling, narrow),
        copy(lstage, left.at[other, pair, y, odd, rows64, :], sib_s.at[1], sib_r.at[1], sibling, narrow),
    ]
    rows_g = pl.ds(pl.multiple_of(odd * 128 + core * 64, 64), 64)
    beside = wide_at(z + 1 - 2 * odd, y, core)
    own_block = grad.at[:, pl.ds(pl.multiple_of(core * block, block), block)]
    other_block = grad.at[:, pl.ds(pl.multiple_of(other * block, block), block)]
    rows_out = [
        copy(other_block, turned.at[rows_g, :], grad_s.at[0], grad_r.at[0], sibling, narrow),
        copy(own_block, turned.at[rows_g, :], grad_s.at[1], grad_r.at[1], beside, narrow),
        copy(other_block, turned.at[rows_g, :], grad_s.at[2], grad_r.at[2], beside + 1 - 2 * core, narrow),
    ]
    last = ny // 2

    def along_z(ref_for, send, recv):
        made = []
        for d in range(1, nz):
            ref = ref_for(lax.rem(z + d, nz))
            made.append(copy(ref, ref, send.at[d - 1], recv.at[d - 1], wide_at(lax.rem(z + d, nz), y, core), narrow))
        return made

    def passed(t):
        return lax.rem(y + ny - (t - 1), ny), lax.rem(y + (t - 1), ny)

    nearest = [0, 1, nz - 1][: min(nz, 3)] + list(range(2, nz - 1))
    if nz == 2:
        nearest = [0, 1]
    def rows_to_line(which, send, recv):
        made = []
        for d in range(1, nz):
            zz = lax.rem(z + d, nz)
            h = lax.rem(zz + which, 2)
            dst = right.at[h, z, y, rows16, :]
            both = ((dst, core), (rstage.at[h], other))
            made.append(
                [
                    copy(src, dst, send.at[d - 1, i], recv.at[d - 1, i], wide_at(zz, y, cc), narrow)
                    for i, (src, cc) in enumerate(both)
                ]
            )
        return made

    zr = rows_to_line(1, zr_s, zr_r)
    zlate = rows_to_line(0, zl_s, zl_r)

    sib[0].start()
    for e in nearest[1:]:
        start(zr[e - 1])
    quantum = 1.0 / (16.0 * math.sqrt(order))
    for i in (1, 2, 3):
        fetches[i].wait()
    value = dequantized(lcodes[...], lscales[...], lerror[...], quantum)
    for h in range(2):

        @pl.when(core == h)
        def _():
            left[h, pair, y, odd, rows64, :] = value[:, h * half : (h + 1) * half]

        @pl.when(core != h)
        def _():
            lstage[...] = value[:, h * half : (h + 1) * half]

    sib[1].start()

    def ring_right(t, e):
        zz = lax.rem(z + nz - e, nz)
        at = nearest.index(e)
        made = []
        for way, (yy, ww) in enumerate(zip(passed(t), (w_up, w_down))):
            if t < last or (at < nz // 2) == (way == 0):
                ref = right.at[mine_half, zz, yy]
                made.append(copy(ref, ref, yr_s.at[t - 1, e, way], yr_r.at[t - 1, e, way], ww, narrow))
        return made

    yr = [[ring_right(t, e) for e in nearest] for t in range(1, last + 1)]

    ra = 96
    rb = 128 - ra

    def rows_a(yy, zs=slice(None)):
        return left.at[core, :, yy, zs, pl.ds(0, ra)]

    def rows_b(yy, begin=0, size=rb):
        return left.at[core, pair, yy, odd, pl.ds(ra + begin, size)]

    own_a = left.at[core, pair, y, odd, pl.ds(0, ra)]
    za = along_z(lambda zz: own_a, za_s, za_r)
    zb = along_z(lambda zz: rows_b(pl.ds(0, ny)), zb_s, zb_r)
    ya, yb, late = [], [], []

    def both_ways(t, a, b, send, recv):
        return [
            copy(a, a, send.at[t - 1, 0], recv.at[t - 1, 0], w_up, narrow),
            copy(b, b, send.at[t - 1, 1], recv.at[t - 1, 1], w_down, narrow),
        ]

    for t in range(1, last + 1):
        up, down = passed(t)
        if t < last:
            a, b = rows_a(up), rows_a(down)
        else:
            a, b = rows_a(up, pl.ds(0, 1)), rows_a(down, pl.ds(1, 1))
        ya.append(both_ways(t, a, b, ya_s, ya_r))
        a, b = (rows_b(up), rows_b(down)) if t < last else (rows_b(up, 0, rb // 2), rows_b(down, rb // 2, rb // 2))
        yb.append(both_ways(t, a, b, yb_s, yb_r))
        zs = (pl.ds(0, nz), pl.ds(0, nz)) if t < last else (pl.ds(0, nz // 2), pl.ds(nz // 2, nz // 2))
        a, b = right.at[odd, zs[0], up], right.at[odd, zs[1], down]
        late.append(both_ways(t, a, b, late_s, late_r))
    shares = []

    def share(ref):
        at = len(shares)
        c = copy(ref, ref, share_s.at[at], share_r.at[at], sibling, narrow)
        c.start()
        shares.append(c)

    sib[0].wait_recv()
    start(yr[0][0])
    fetches[0].wait()
    for h in range(2):

        @pl.when(core == h)
        def _():
            turned[rows_g, :] = grad[:, h * block : (h + 1) * block]

    start(rows_out)
    sib[1].wait_recv()
    start(yb[0])
    start(za)
    for at, e in enumerate(nearest):
        if at > 0:
            landed(zr[e - 1])
            start(yr[0][at])
    for part in zlate:
        start(part)
    b_step = 1

    def next_b(t):
        landed(yb[t - 1])
        if t < last:
            start(yb[t])
        else:
            start(zb)
            share(rows_b(pl.ds(0, ny)))

    for t in range(2, last + 1):
        for at in range(nz):
            landed(yr[t - 2][at])
            start(yr[t - 1][at])
            if at % 2 == 1 and b_step <= last and t < last:
                next_b(b_step)
                b_step += 1
    while b_step <= last:
        next_b(b_step)
        b_step += 1
    landed(za)
    start(ya[0])
    share(rows_a(y))
    for at in range(nz):
        landed(yr[last - 1][at])

    landed(rows_out)
    lands = slabs.at[pl.ds(narrow * nq + place - odd, 2)]
    high_far = 1 - high
    n_far = x * NH + high_far
    first_to = (nq // 2) * (2 * core + mine_half)

    wide_n = min(256, hb)
    some = wide_n // 32

    def send_near(begin, t, carry):
        j = begin + lax.rem(2 * y + pair + t, some)
        to = first_to + j

        @pl.when(to != wide)
        def _():
            copy(outgoing.at[j], lands, out_s.at[0], out_r.at[0], to, narrow).start()

        @pl.when(to == wide)
        def _():
            pltpu.make_async_copy(outgoing.at[j], lands, own_sem.at[0]).start()

        return carry

    def send_far(t, carry):
        j = lax.rem(2 * y + pair + t, nq // 2)
        copy(outgoing.at[j], lands, out_s.at[1], out_r.at[1], first_to + j, n_far).start()
        return carry

    for at in range(0, hb, wide_n):
        basis = right[mine_half, :, :, :, at : at + wide_n].reshape(block, wide_n)
        value = jnp.dot(turned[...], basis, preferred_element_type=F32).T.astype(BF16)
        for d in range(2):
            outgoing[at // 32 : at // 32 + some, d] = value[:, d * 128 : (d + 1) * 128].reshape(some, 32, 128)
        lax.fori_loop(0, some, functools.partial(send_near, at // 32), 0)
    lax.fori_loop(0, nq // 2, send_far, 0)

    def wait_near(ref, base, send, recv, sending, some_own=has_own, own_many=1):
        def wait(many):
            there = ref.at[pl.ds(base, many)]
            c = copy(there, there, send, recv, sibling, narrow)
            if sending:
                c.wait_send()
            else:
                c.wait_recv()

        @pl.when(some_own)
        def _():
            wait(nq - own_many)

        @pl.when(jnp.logical_not(some_own))
        def _():
            wait(nq)

    def wait_far(ref, base, send, recv, sending):
        there = ref.at[pl.ds(base, nq)]
        c = copy(there, there, send, recv, sibling, narrow)
        if sending:
            c.wait_send()
        else:
            c.wait_recv()

    def next_a(t):
        landed(ya[t - 1])
        if t < last:
            start(ya[t])
            for yy in passed(t + 1):
                share(rows_a(yy))
        else:
            share(rows_a(lax.rem(y + last, ny)))

    hq = nq // 2

    def slab_at(xx, g):
        return (xx * NH + g) * nq

    def ring_x(g, at):
        own = [slabs.at[pl.ds(slab_at(x, g) + h * hq, hq)] for h in range(2)]
        from_down = slabs.at[pl.ds(slab_at(x_down, g), hq)]
        from_up = slabs.at[pl.ds(slab_at(x_up, g) + hq, hq)]
        made = [
            (own[0], n_up),
            (own[1], n_down),
            (own[1], n_up),
            (own[0], n_down),
            (from_down, n_up),
            (from_up, n_down),
        ]
        return [copy(a, a, ring_s.at[at, i], ring_r.at[at, i], wide, nn) for i, (a, nn) in enumerate(made)]

    ring_near, ring_far = ring_x(high, 0), ring_x(high_far, 1)
    next_a(1)
    wait_near(slabs, slab_at(x, high), out_s.at[0], out_r.at[0], False, sends_own, 2)

    @pl.when(sends_own)
    def _():
        pltpu.make_async_copy(outgoing.at[0], lands, own_sem.at[0]).wait()

    start(ring_near[:4])
    if last > 1:
        next_a(2)
    if last > 2:
        next_a(3)
    landed(ring_near[:2])
    start(ring_near[4:])
    wait_far(slabs, slab_at(x, high_far), out_s.at[1], out_r.at[1], False)
    start(ring_far[:4])
    for t in range(4, last + 1):
        next_a(t)
    landed(zb)
    for d in range(1, nz):
        zz = lax.rem(z + nz - d, nz)
        share(left.at[core, zz // 2, pl.ds(0, ny), lax.rem(zz, 2), pl.ds(ra, rb)])
    landed(ring_far[:2])
    start(ring_far[4:])
    for part in zlate:
        landed(part)
    start(late[0])
    landed(ring_near[2:])
    landed(shares)
    landed(ring_far[2:])

    total[...] = jnp.zeros_like(total)
    deep = 4

    def rotate(i, carry):
        at = i * deep
        zz, yy = i // (2 * ny // deep), lax.rem(i, 2 * ny // deep) * (deep // 2)
        lhs = jnp.concatenate(
            [
                jnp.concatenate([slabs[s * nq + at + d] for s in range(NX * NH)], axis=0)
                for d in range(deep)
            ],
            axis=1,
        )
        for h in range(2):
            rhs = left[h, zz, pl.ds(yy, deep // 2)].reshape(deep * 128, half)
            total[:, h * half : (h + 1) * half] += jnp.dot(lhs, rhs, preferred_element_type=F32)
        return carry

    def next_late(t):
        landed(late[t - 1])
        if t < last:
            start(late[t])

    lax.fori_loop(0, nq // deep, rotate, 0)
    fetches[7].wait()
    fetches[8].wait()

    def moments(s, carry):
        there = pl.ds(pl.multiple_of(s * 32, 32), 32)
        value = total[there, :]
        m = BETA_ONE * first[s] + (1.0 - BETA_ONE) * value
        v = BETA_TWO * second[s] + (1.0 - BETA_TWO) * value * value
        new_first[s] = m
        new_second[s] = v
        direction[there, :] = (m / (jnp.sqrt(v) + EPSILON)).astype(BF16)
        return carry

    lax.fori_loop(0, NX * NH, moments, 0)
    stores = [pltpu.make_async_copy(held[i], outputs[1 + i], fetch_sem.at[9 + i]) for i in range(2)]
    for c in stores:
        c.start()

    def rotate_back(i, carry):
        at = i * 2
        zz, yy = i // ny, lax.rem(i, ny)
        value = None
        for h in range(2):
            rhs = left[h, zz, yy].reshape(256, half)
            term = lax.dot_general(
                direction[:, h * half : (h + 1) * half],
                rhs,
                (((1,), (1,)), ((), ())),
                preferred_element_type=F32,
            )
            value = term if value is None else value + term
        value = value.astype(BF16)
        for s in range(NX * NH):
            for d in range(2):
                partial[s * nq + at + d] = value[s * 32 : (s + 1) * 32, d * 128 : (d + 1) * 128]
        return carry

    def sums_of(g, at):
        def part(xx, h):
            return partial.at[pl.ds(slab_at(xx, g) + h * hq, hq)]

        lower, upper = pl.ds(0, hq), pl.ds(hq, hq)
        made = [
            (part(x_far, 0), halfway.at[at, 0], n_up),
            (part(x_far, 1), halfway.at[at, 1], n_down),
            (part(x_down, 0), arrived.at[at, 1, lower], n_down),
            (part(x_up, 1), arrived.at[at, 0, upper], n_up),
            (part(x_up, 0), arrived.at[at, 0, lower], n_up),
            (part(x_down, 1), arrived.at[at, 1, upper], n_down),
        ]
        return [copy(a, b, sum_s.at[at, i], sum_r.at[at, i], wide, nn) for i, (a, b, nn) in enumerate(made)]

    sums_far, sums_near = sums_of(high_far, 0), sums_of(high, 1)
    few = min(8, hq)

    def pass_on(g, at):
        def some(i, carry):
            for h, base in ((0, slab_at(x_up, g)), (1, slab_at(x_down, g) + hq)):
                there = pl.ds(base + i * few, few)
                held = halfway[at, h, pl.ds(i * few, few)]
                partial[there] = (partial[there].astype(F32) + held.astype(F32)).astype(BF16)
            return carry

        lax.fori_loop(0, hq // few, some, 0)

    def add_up(g, at):
        def some(i, carry):
            there = pl.ds(i * few, few)
            value = partial[pl.ds(slab_at(x, g) + i * few, few)].astype(F32) + arrived[at, 0, there].astype(F32)
            home[pl.ds(at * nq + i * few, few)] = (value + arrived[at, 1, there].astype(F32)).astype(BF16)
            return carry

        lax.fori_loop(0, nq // few, some, 0)

    lax.fori_loop(0, nq // 4, rotate_back, 0)
    start((sums_far[0], sums_far[2]))
    lax.fori_loop(nq // 4, nq // 2, rotate_back, 0)
    start((sums_far[1], sums_far[3]))
    start(sums_near[:2])
    next_late(1)
    landed(sums_far[:2])
    pass_on(high_far, 0)
    start(sums_far[4:])
    start(sums_near[2:4])
    if last > 1:
        next_late(2)
    landed(sums_near[:2])
    pass_on(high, 1)
    start(sums_near[4:])
    for t in range(3, last):
        next_late(t)

    goes_to = high * nq + lax.rem(wide, nq)

    def owner(at):
        zz, yy = at // (2 * ny) * 2 + lax.rem(at, 2), lax.rem(at // 2, ny)
        return wide_at(zz, yy, side)

    def back_far(t, carry):
        at = lax.rem(place + t, nq)
        copy(home.at[at], back.at[goes_to], back_s.at[1], back_r.at[1], owner(at), n_far).start()
        return carry

    def back_near(t, carry):
        at = lax.rem(place + t, nq)
        to = owner(at)
        src = home.at[nq + at]

        @pl.when(to != wide)
        def _():
            copy(src, back.at[goes_to], back_s.at[0], back_r.at[0], to, narrow).start()

        @pl.when(to == wide)
        def _():
            pltpu.make_async_copy(src, back.at[goes_to], own_sem.at[1]).start()

        return carry

    landed(sums_far[2:])
    add_up(high_far, 0)
    lax.fori_loop(0, nq, back_far, 0)
    landed(sums_near[2:])
    add_up(high, 1)
    lax.fori_loop(0, nq, back_near, 0)
    if last > 2:
        next_late(last)
    wait_far(back, high_far * nq, back_s.at[1], back_r.at[1], False)
    wait_near(back, high * nq, back_s.at[0], back_r.at[0], False)

    @pl.when(has_own)
    def _():
        pltpu.make_async_copy(home.at[0], back.at[goes_to], own_sem.at[1]).wait()

    turned_back = (back[0:nq].astype(F32) + back[nq : 2 * nq].astype(F32)).astype(BF16).reshape(block, 128)
    tall = ny * 32
    swaps = []
    for zz in range(nz):
        value = sum(
            jnp.dot(
                right[h, zz].reshape(tall, hb), turned_back[h * hb : (h + 1) * hb], preferred_element_type=F32
            )
            for h in range(2)
        )
        value = value.T.astype(BF16)
        result[zz, 0] = value[0:64]
        result[zz, 1] = value[64:128]
        there = update.at[:, pl.ds(pl.multiple_of(core * block + zz * tall, tall), tall)]
        swap = copy(result.at[zz, other], there, swap_s.at[zz], swap_r.at[zz], sibling, narrow)
        swap.start()
        swaps.append(swap)
        store = pltpu.make_async_copy(result.at[zz, core], there, fetch_sem.at[11 + zz])
        store.start()
        stores.append(store)
    landed(swaps)

    sent = sib + rows_out + za + zb + [c for part in zr + zlate for c in part] + [c for step in yr for part in step for c in part]
    sent += [c for part in ya + yb + late for c in part] + shares + ring_near + ring_far + sums_near + sums_far + swaps
    for c in sent:
        c.wait_send()
    for c in stores:
        c.wait()
    wait_near(slabs, slab_at(x, high), out_s.at[0], out_r.at[0], True, sends_own, 2)
    wait_far(slabs, slab_at(x, high_far), out_s.at[1], out_r.at[1], True)
    wait_near(back, high * nq, back_s.at[0], back_r.at[0], True)
    wait_far(back, high_far * nq, back_s.at[1], back_r.at[1], True)


def solution(mesh):
    nz, ny = 4, mesh.shape["wide"] // 8

    def step(*args):
        return body(nz, ny, *args)

    placed = (
        P("wide", "narrow"),
        P("wide", "narrow"),
        P("wide", "narrow"),
        P("wide", "narrow"),
        P("narrow", "wide", None),
        P("narrow", "wide", None),
        P("narrow", "wide", None),
        P(None, "wide", "narrow"),
        P(None, "wide", "narrow"),
    )
    return jax.shard_map(
        step,
        mesh=mesh,
        in_specs=placed,
        out_specs=(P("wide", "narrow"), P(None, "wide", "narrow"), P(None, "wide", "narrow")),
        check_vma=False,
    )


def body(nz, ny, *args):
    nq = nz * ny
    block, span = 32 * nq, args[1].shape[1]
    half = span // 2
    slabs = NX * NH
    dma = pltpu.SemaphoreType.DMA
    steps = ny // 2
    anywhere = pl.BlockSpec(memory_space=pl.ANY)
    args = list(args)
    args[2] = args[2].T
    args[5] = jnp.swapaxes(args[5], 1, 2)
    return pl.pallas_call(
        functools.partial(kernel, nz, ny),
        out_shape=(
            jax.ShapeDtypeStruct(args[0].shape, BF16),
            jax.ShapeDtypeStruct(args[7].shape, F32),
            jax.ShapeDtypeStruct(args[8].shape, F32),
        ),
        in_specs=[anywhere] * 9,
        out_specs=(anywhere,) * 3,
        scratch_shapes=[pltpu.VMEM(a.shape, a.dtype) for a in args + args[7:9]]
        + [
            pltpu.VMEM((256, block), BF16),
            pltpu.VMEM((2, nz, ny, 32, block // 2), BF16),
            pltpu.VMEM((2, nz // 2, ny, 2, 128, half), BF16),
            pltpu.VMEM((2, 16, block // 2), BF16),
            pltpu.VMEM((64, half), BF16),
            pltpu.VMEM((nq // 2, 2, 32, 128), BF16),
            pltpu.VMEM((slabs * nq, 32, 128), BF16),
            pltpu.VMEM((slabs * 32, span), F32),
            pltpu.VMEM((slabs * 32, span), BF16),
            pltpu.VMEM((slabs * nq, 32, 128), BF16),
            pltpu.VMEM((NH, 2, nq // 2, 32, 128), BF16),
            pltpu.VMEM((NH, 2, nq, 32, 128), BF16),
            pltpu.VMEM((NH * nq, 32, 128), BF16),
            pltpu.VMEM((NH * nq, 32, 128), BF16),
            pltpu.VMEM((nz, 2, 64, ny * 32), BF16),
            dma((11 + nz,)),
            dma((2,)),
            dma((2,)),
            dma((nz,)),
            dma((nz,)),
            dma((3,)),
            dma((3,)),
        ]
        + [dma((nz - 1, 2))] * 4
        + [dma((nz - 1,))] * 4
        + [dma((steps, nz, 2))] * 2
        + [dma((steps, 2))] * 6
        + [dma((ny + nz,))] * 2
        + [dma((2,))] * 5
        + [dma((2, 6))] * 4,
        compiler_params=pltpu.CompilerParams(
            collective_id=0, has_side_effects=True, vmem_limit_bytes=58 * 1024 * 1024
        ),
        cost_estimate=pl.CostEstimate(flops=2_700_000_000, bytes_accessed=8_000_000, transcendentals=131072),
    )(*args)
```

```python
import functools
import math

import jax
import jax.numpy as jnp
from jax import lax
from jax.experimental import pallas as pl
from jax.experimental.pallas import tpu as pltpu
from jax.sharding import PartitionSpec as P

MESH = pl.DeviceIdType.MESH
F32, BF16 = jnp.float32, jnp.bfloat16
BETA_ONE = 0.95
BETA_TWO = 0.95
EPSILON = 1e-08
NX = 4
NH = 2


def dequantized(codes, scales, error, quantum):
    groups, columns = scales.shape[0], codes.shape[1]
    column = lax.broadcasted_iota(jnp.int32, (groups, columns), 1) // (columns // groups)
    spread = (column == lax.broadcasted_iota(jnp.int32, (groups, columns), 0)).astype(F32).astype(BF16)
    expanded = lax.dot_general(
        scales.astype(F32).astype(BF16), spread, (((0,), (0,)), ((), ())), preferred_element_type=F32
    )
    return (codes.astype(F32) * expanded * quantum + error.astype(F32)).astype(BF16)


def kernel(nz, ny, *refs):
    inputs, refs = refs[:9], refs[9:]
    outputs, fetched, held, refs = refs[:3], refs[3:12], refs[12:14], refs[14:]
    update, (new_first, new_second) = outputs[0], held
    grad, lcodes, lscales, lerror, rcodes, rscales, rerror, first, second = fetched
    (
        turned,
        right,
        left,
        rstage,
        lstage,
        outgoing,
        slabs,
        total,
        direction,
        partial,
        halfway,
        arrived,
        home,
        back,
        result,
    ) = refs[:15]
    (
        fetch_sem,
        sib_s,
        sib_r,
        swap_s,
        swap_r,
        grad_s,
        grad_r,
        zr_s,
        zr_r,
        zl_s,
        zl_r,
        za_s,
        za_r,
        zb_s,
        zb_r,
        yr_s,
        yr_r,
        late_s,
        late_r,
        ya_s,
        ya_r,
        yb_s,
        yb_r,
        share_s,
        share_r,
        out_s,
        out_r,
        back_s,
        back_r,
        own_sem,
        ring_s,
        ring_r,
        sum_s,
        sum_r,
    ) = refs[15:]
    nq = nz * ny
    block = 32 * nq
    order = 128 * nq
    span = lcodes.shape[1]
    half = span // 2
    hb = block // 2
    wide, narrow = lax.axis_index("wide"), lax.axis_index("narrow")
    core, chip = lax.rem(wide, 2), wide // 2
    z, y = chip // ny, lax.rem(chip, ny)
    x, high = narrow // NH, lax.rem(narrow, NH)
    other = 1 - core
    pair, odd = z // 2, lax.rem(z, 2)
    mine_half = 1 - odd
    place = (pair * ny + y) * 2 + odd
    side = wide // nq
    has_own = side == core
    sends_own = wide // (nq // 2) == 2 * core + mine_half

    fetches = [pltpu.make_async_copy(a, b, fetch_sem.at[i]) for i, (a, b) in enumerate(zip(inputs, fetched))]
    for i in (4, 5, 6, 1, 2, 3, 0, 7, 8):
        fetches[i].start()

    def wide_at(zz, yy, cc):
        return (zz * ny + yy) * 2 + cc

    def copy(src, dst, send, recv, ww, nn):
        return pltpu.make_async_remote_copy(
            src_ref=src, dst_ref=dst, send_sem=send, recv_sem=recv, device_id=(ww, nn), device_id_type=MESH
        )

    def start(copies):
        for c in copies:
            c.start()

    def landed(copies):
        for c in copies:
            c.wait_recv()

    sibling = wide + 1 - 2 * core
    y_up, y_down = lax.rem(y + 1, ny), lax.rem(y + ny - 1, ny)
    x_up, x_down = lax.rem(x + 1, NX), lax.rem(x + NX - 1, NX)
    x_far = lax.rem(x + 2, NX)
    n_up, n_down = x_up * NH + high, x_down * NH + high
    w_up, w_down = wide_at(z, y_up, core), wide_at(z, y_down, core)

    barrier = pltpu.get_barrier_semaphore()
    plane = 2 * nq * NH

    for extra in range(NH):
        nn = x * NH + lax.rem(high + extra, NH)

        def greet(i, carry):
            there = wide + i
            there = jnp.where(there >= 2 * nq, there - 2 * nq, there)
            pl.semaphore_signal(barrier, inc=1, device_id=(there, nn), device_id_type=MESH)
            return carry

        lax.fori_loop(1 if extra == 0 else 0, 2 * nq, greet, 0)
    for nn in (n_up, n_down):
        pl.semaphore_signal(barrier, inc=1, device_id=(wide, nn), device_id_type=MESH)

    rows16 = pl.ds(pl.multiple_of(core * 16, 16), 16)
    rows64 = pl.ds(pl.multiple_of(core * 64, 64), 64)
    quantum = 1.0 / (16.0 * math.sqrt(block))
    for i in (4, 5, 6):
        fetches[i].wait()
    for ref, which in ((rstage, other), (right.at[:, z, y, rows16, :], core)):
        value = dequantized(rcodes[which], rscales[which], rerror[which], quantum)
        for h in range(2):
            ref[h] = value[:, h * hb : (h + 1) * hb]
    pl.semaphore_wait(barrier, plane - 1 + 2)
    sib = [
        copy(rstage, right.at[:, z, y, rows16, :], sib_s.at[0], sib_r.at[0], sibling, narrow),
        copy(lstage, left.at[other, pair, y, odd, rows64, :], sib_s.at[1], sib_r.at[1], sibling, narrow),
    ]
    rows_g = pl.ds(pl.multiple_of(odd * 128 + core * 64, 64), 64)
    beside = wide_at(z + 1 - 2 * odd, y, core)
    own_block = grad.at[:, pl.ds(pl.multiple_of(core * block, block), block)]
    other_block = grad.at[:, pl.ds(pl.multiple_of(other * block, block), block)]
    rows_out = [
        copy(other_block, turned.at[rows_g, :], grad_s.at[0], grad_r.at[0], sibling, narrow),
        copy(own_block, turned.at[rows_g, :], grad_s.at[1], grad_r.at[1], beside, narrow),
        copy(other_block, turned.at[rows_g, :], grad_s.at[2], grad_r.at[2], beside + 1 - 2 * core, narrow),
    ]
    last = ny // 2

    def along_z(ref_for, send, recv):
        made = []
        for d in range(1, nz):
            ref = ref_for(lax.rem(z + d, nz))
            made.append(copy(ref, ref, send.at[d - 1], recv.at[d - 1], wide_at(lax.rem(z + d, nz), y, core), narrow))
        return made

    def passed(t):
        return lax.rem(y + ny - (t - 1), ny), lax.rem(y + (t - 1), ny)

    nearest = [0, 1, nz - 1][: min(nz, 3)] + list(range(2, nz - 1))
    if nz == 2:
        nearest = [0, 1]
    def rows_to_line(which, send, recv):
        made = []
        for d in range(1, nz):
            zz = lax.rem(z + d, nz)
            h = lax.rem(zz + which, 2)
            dst = right.at[h, z, y, rows16, :]
            both = ((dst, core), (rstage.at[h], other))
            made.append(
                [
                    copy(src, dst, send.at[d - 1, i], recv.at[d - 1, i], wide_at(zz, y, cc), narrow)
                    for i, (src, cc) in enumerate(both)
                ]
            )
        return made

    zr = rows_to_line(1, zr_s, zr_r)
    zlate = rows_to_line(0, zl_s, zl_r)

    sib[0].start()
    for e in nearest[1:]:
        start(zr[e - 1])
    quantum = 1.0 / (16.0 * math.sqrt(order))
    for i in (1, 2, 3):
        fetches[i].wait()
    value = dequantized(lcodes[...], lscales[...], lerror[...], quantum)
    for h in range(2):

        @pl.when(core == h)
        def _():
            left[h, pair, y, odd, rows64, :] = value[:, h * half : (h + 1) * half]

        @pl.when(core != h)
        def _():
            lstage[...] = value[:, h * half : (h + 1) * half]

    sib[1].start()

    def ring_right(t, e):
        zz = lax.rem(z + nz - e, nz)
        at = nearest.index(e)
        made = []
        for way, (yy, ww) in enumerate(zip(passed(t), (w_up, w_down))):
            if t < last or (at < nz // 2) == (way == 0):
                ref = right.at[mine_half, zz, yy]
                made.append(copy(ref, ref, yr_s.at[t - 1, e, way], yr_r.at[t - 1, e, way], ww, narrow))
        return made

    yr = [[ring_right(t, e) for e in nearest] for t in range(1, last + 1)]

    ra, rb = 80, 48
    rb_up = 32

    def rows_a(yy, zs=slice(None)):
        return left.at[core, :, yy, zs, pl.ds(0, ra)]

    def rows_b(yy, begin=0, size=rb):
        return left.at[core, pair, yy, odd, pl.ds(ra + begin, size)]

    own_a = left.at[core, pair, y, odd, pl.ds(0, ra)]
    za = along_z(lambda zz: own_a, za_s, za_r)
    zb = along_z(lambda zz: rows_b(pl.ds(0, ny)), zb_s, zb_r)
    ya, yb, late = [], [], []

    def both_ways(t, a, b, send, recv):
        return [
            copy(a, a, send.at[t - 1, 0], recv.at[t - 1, 0], w_up, narrow),
            copy(b, b, send.at[t - 1, 1], recv.at[t - 1, 1], w_down, narrow),
        ]

    for t in range(1, last + 1):
        up, down = passed(t)
        if t < last:
            a, b = rows_a(up), rows_a(down)
        else:
            a, b = rows_a(up, pl.ds(0, 1)), rows_a(down, pl.ds(1, 1))
        ya.append(both_ways(t, a, b, ya_s, ya_r))
        a, b = (rows_b(up), rows_b(down)) if t < last else (rows_b(up, 0, rb_up), rows_b(down, rb_up, rb - rb_up))
        yb.append(both_ways(t, a, b, yb_s, yb_r))
        zs = (pl.ds(0, nz), pl.ds(0, nz)) if t < last else (pl.ds(0, nz // 2), pl.ds(nz // 2, nz // 2))
        a, b = right.at[odd, zs[0], up], right.at[odd, zs[1], down]
        late.append(both_ways(t, a, b, late_s, late_r))
    shares = []

    def share(ref):
        at = len(shares)
        c = copy(ref, ref, share_s.at[at], share_r.at[at], sibling, narrow)
        c.start()
        shares.append(c)

    sib[0].wait_recv()
    start(yr[0][0])
    fetches[0].wait()
    for h in range(2):

        @pl.when(core == h)
        def _():
            turned[rows_g, :] = grad[:, h * block : (h + 1) * block]

    start(rows_out)
    sib[1].wait_recv()
    start(yb[0])
    start(za)
    for at, e in enumerate(nearest):
        if at > 0:
            landed(zr[e - 1])
            start(yr[0][at])
    for part in zlate:
        start(part)
    b_step = 1

    def next_b(t):
        landed(yb[t - 1])
        if t < last:
            start(yb[t])
        else:
            start(zb)
            share(rows_b(pl.ds(0, ny)))

    for t in range(2, last + 1):
        if t == last:
            landed(za)
            start(ya[0])
        for at in range(nz):
            landed(yr[t - 2][at])
            start(yr[t - 1][at])
            if at % 2 == 1 and b_step <= last and t < last:
                next_b(b_step)
                b_step += 1
    while b_step <= last:
        next_b(b_step)
        b_step += 1
    share(rows_a(y))
    for at in range(nz):
        landed(yr[last - 1][at])

    landed(rows_out)
    lands = slabs.at[pl.ds(narrow * nq + place - odd, 2)]
    high_far = 1 - high
    n_far = x * NH + high_far
    first_to = (nq // 2) * (2 * core + mine_half)

    def next_a(t):
        landed(ya[t - 1])
        if t < last:
            start(ya[t])
            for yy in passed(t + 1):
                share(rows_a(yy))
        else:
            share(rows_a(lax.rem(y + last, ny)))

    wide_n = min(256, hb)
    some = wide_n // 32

    def send_near(begin, t, carry):
        j = begin + lax.rem(2 * y + pair + t, some)
        to = first_to + j

        @pl.when(to != wide)
        def _():
            copy(outgoing.at[j], lands, out_s.at[0], out_r.at[0], to, narrow).start()

        @pl.when(to == wide)
        def _():
            pltpu.make_async_copy(outgoing.at[j], lands, own_sem.at[0]).start()

        return carry

    def send_far(t, carry):
        j = lax.rem(2 * y + pair + t, nq // 2)
        copy(outgoing.at[j], lands, out_s.at[1], out_r.at[1], first_to + j, n_far).start()
        return carry

    for at in range(0, hb, wide_n):
        basis = right[mine_half, :, :, :, at : at + wide_n].reshape(block, wide_n)
        value = jnp.dot(turned[...], basis, preferred_element_type=F32).T.astype(BF16)
        for d in range(2):
            outgoing[at // 32 : at // 32 + some, d] = value[:, d * 128 : (d + 1) * 128].reshape(some, 32, 128)
        lax.fori_loop(0, some, functools.partial(send_near, at // 32), 0)
        if at == 0:
            next_a(1)
    lax.fori_loop(0, nq // 2, send_far, 0)

    def wait_near(ref, base, send, recv, sending, some_own=has_own, own_many=1):
        def wait(many):
            there = ref.at[pl.ds(base, many)]
            c = copy(there, there, send, recv, sibling, narrow)
            if sending:
                c.wait_send()
            else:
                c.wait_recv()

        @pl.when(some_own)
        def _():
            wait(nq - own_many)

        @pl.when(jnp.logical_not(some_own))
        def _():
            wait(nq)

    def wait_far(ref, base, send, recv, sending):
        there = ref.at[pl.ds(base, nq)]
        c = copy(there, there, send, recv, sibling, narrow)
        if sending:
            c.wait_send()
        else:
            c.wait_recv()

    hq = nq // 2

    def slab_at(xx, g):
        return (xx * NH + g) * nq

    def ring_x(g, at):
        own = [slabs.at[pl.ds(slab_at(x, g) + h * hq, hq)] for h in range(2)]
        from_down = slabs.at[pl.ds(slab_at(x_down, g), hq)]
        from_up = slabs.at[pl.ds(slab_at(x_up, g) + hq, hq)]
        made = [
            (own[0], n_up),
            (own[1], n_down),
            (own[1], n_up),
            (own[0], n_down),
            (from_down, n_up),
            (from_up, n_down),
        ]
        return [copy(a, a, ring_s.at[at, i], ring_r.at[at, i], wide, nn) for i, (a, nn) in enumerate(made)]

    ring_near, ring_far = ring_x(high, 0), ring_x(high_far, 1)
    wait_near(slabs, slab_at(x, high), out_s.at[0], out_r.at[0], False, sends_own, 2)

    @pl.when(sends_own)
    def _():
        pltpu.make_async_copy(outgoing.at[0], lands, own_sem.at[0]).wait()

    start(ring_near[:4])
    if last > 1:
        next_a(2)
    if last > 2:
        next_a(3)
    landed(ring_near[:2])
    start(ring_near[4:])
    wait_far(slabs, slab_at(x, high_far), out_s.at[1], out_r.at[1], False)
    start(ring_far[:4])
    for t in range(4, last + 1):
        next_a(t)
    landed(zb)
    for d in range(1, nz):
        zz = lax.rem(z + nz - d, nz)
        share(left.at[core, zz // 2, pl.ds(0, ny), lax.rem(zz, 2), pl.ds(ra, rb)])
    landed(ring_far[:2])
    start(ring_far[4:])
    for part in zlate:
        landed(part)
    start(late[0])
    landed(ring_near[2:])
    landed(shares)
    landed(ring_far[2:])

    total[...] = jnp.zeros_like(total)
    deep = 4

    def rotate(i, carry):
        at = i * deep
        zz, yy = i // (2 * ny // deep), lax.rem(i, 2 * ny // deep) * (deep // 2)
        lhs = jnp.concatenate(
            [
                jnp.concatenate([slabs[s * nq + at + d] for s in range(NX * NH)], axis=0)
                for d in range(deep)
            ],
            axis=1,
        )
        for h in range(2):
            rhs = left[h, zz, pl.ds(yy, deep // 2)].reshape(deep * 128, half)
            total[:, h * half : (h + 1) * half] += jnp.dot(lhs, rhs, preferred_element_type=F32)
        return carry

    def next_late(t):
        landed(late[t - 1])
        if t < last:
            start(late[t])

    lax.fori_loop(0, nq // deep, rotate, 0)
    fetches[7].wait()
    fetches[8].wait()

    def moments(s, carry):
        there = pl.ds(pl.multiple_of(s * 32, 32), 32)
        value = total[there, :]
        m = BETA_ONE * first[s] + (1.0 - BETA_ONE) * value
        v = BETA_TWO * second[s] + (1.0 - BETA_TWO) * value * value
        new_first[s] = m
        new_second[s] = v
        direction[there, :] = (m / (jnp.sqrt(v) + EPSILON)).astype(BF16)
        return carry

    lax.fori_loop(0, NX * NH, moments, 0)
    stores = [pltpu.make_async_copy(held[i], outputs[1 + i], fetch_sem.at[9 + i]) for i in range(2)]
    for c in stores:
        c.start()

    def rotate_back(i, carry):
        at = i * 2
        zz, yy = i // ny, lax.rem(i, ny)
        value = None
        for h in range(2):
            rhs = left[h, zz, yy].reshape(256, half)
            term = lax.dot_general(
                direction[:, h * half : (h + 1) * half],
                rhs,
                (((1,), (1,)), ((), ())),
                preferred_element_type=F32,
            )
            value = term if value is None else value + term
        value = value.astype(BF16)
        for s in range(NX * NH):
            for d in range(2):
                partial[s * nq + at + d] = value[s * 32 : (s + 1) * 32, d * 128 : (d + 1) * 128]
        return carry

    def sums_of(g, at):
        def part(xx, h):
            return partial.at[pl.ds(slab_at(xx, g) + h * hq, hq)]

        lower, upper = pl.ds(0, hq), pl.ds(hq, hq)
        made = [
            (part(x_far, 0), halfway.at[at, 0], n_up),
            (part(x_far, 1), halfway.at[at, 1], n_down),
            (part(x_down, 0), arrived.at[at, 1, lower], n_down),
            (part(x_up, 1), arrived.at[at, 0, upper], n_up),
            (part(x_up, 0), arrived.at[at, 0, lower], n_up),
            (part(x_down, 1), arrived.at[at, 1, upper], n_down),
        ]
        return [copy(a, b, sum_s.at[at, i], sum_r.at[at, i], wide, nn) for i, (a, b, nn) in enumerate(made)]

    sums_far, sums_near = sums_of(high_far, 0), sums_of(high, 1)
    few = min(8, hq)

    def pass_on(g, at):
        def some(i, carry):
            for h, base in ((0, slab_at(x_up, g)), (1, slab_at(x_down, g) + hq)):
                there = pl.ds(base + i * few, few)
                held = halfway[at, h, pl.ds(i * few, few)]
                partial[there] = (partial[there].astype(F32) + held.astype(F32)).astype(BF16)
            return carry

        lax.fori_loop(0, hq // few, some, 0)

    def add_up(g, at):
        def some(i, carry):
            there = pl.ds(i * few, few)
            value = partial[pl.ds(slab_at(x, g) + i * few, few)].astype(F32) + arrived[at, 0, there].astype(F32)
            home[pl.ds(at * nq + i * few, few)] = (value + arrived[at, 1, there].astype(F32)).astype(BF16)
            return carry

        lax.fori_loop(0, nq // few, some, 0)

    lax.fori_loop(0, nq // 4, rotate_back, 0)
    start((sums_far[0], sums_far[2]))
    lax.fori_loop(nq // 4, nq // 2, rotate_back, 0)
    start((sums_far[1], sums_far[3]))
    start(sums_near[:2])
    next_late(1)
    landed(sums_far[:2])
    pass_on(high_far, 0)
    start(sums_far[4:])
    start(sums_near[2:4])
    if last > 1:
        next_late(2)
    landed(sums_near[:2])
    pass_on(high, 1)
    start(sums_near[4:])
    for t in range(3, last):
        next_late(t)

    goes_to = high * nq + lax.rem(wide, nq)

    def owner(at):
        zz, yy = at // (2 * ny) * 2 + lax.rem(at, 2), lax.rem(at // 2, ny)
        return wide_at(zz, yy, side)

    def back_far(t, carry):
        at = lax.rem(place + t, nq)
        copy(home.at[at], back.at[goes_to], back_s.at[1], back_r.at[1], owner(at), n_far).start()
        return carry

    def back_near(t, carry):
        at = lax.rem(place + t, nq)
        to = owner(at)
        src = home.at[nq + at]

        @pl.when(to != wide)
        def _():
            copy(src, back.at[goes_to], back_s.at[0], back_r.at[0], to, narrow).start()

        @pl.when(to == wide)
        def _():
            pltpu.make_async_copy(src, back.at[goes_to], own_sem.at[1]).start()

        return carry

    landed(sums_far[2:])
    add_up(high_far, 0)
    lax.fori_loop(0, nq, back_far, 0)
    landed(sums_near[2:])
    add_up(high, 1)
    lax.fori_loop(0, nq, back_near, 0)
    if last > 2:
        next_late(last)
    wait_far(back, high_far * nq, back_s.at[1], back_r.at[1], False)
    wait_near(back, high * nq, back_s.at[0], back_r.at[0], False)

    @pl.when(has_own)
    def _():
        pltpu.make_async_copy(home.at[0], back.at[goes_to], own_sem.at[1]).wait()

    turned_back = (back[0:nq].astype(F32) + back[nq : 2 * nq].astype(F32)).astype(BF16).reshape(block, 128)
    tall = ny * 32
    swaps = []
    for zz in range(nz):
        value = sum(
            jnp.dot(
                right[h, zz].reshape(tall, hb), turned_back[h * hb : (h + 1) * hb], preferred_element_type=F32
            )
            for h in range(2)
        )
        value = value.T.astype(BF16)
        result[zz, 0] = value[0:64]
        result[zz, 1] = value[64:128]
        there = update.at[:, pl.ds(pl.multiple_of(core * block + zz * tall, tall), tall)]
        swap = copy(result.at[zz, other], there, swap_s.at[zz], swap_r.at[zz], sibling, narrow)
        swap.start()
        swaps.append(swap)
        store = pltpu.make_async_copy(result.at[zz, core], there, fetch_sem.at[11 + zz])
        store.start()
        stores.append(store)
    landed(swaps)

    sent = sib + rows_out + za + zb + [c for part in zr + zlate for c in part] + [c for step in yr for part in step for c in part]
    sent += [c for part in ya + yb + late for c in part] + shares + ring_near + ring_far + sums_near + sums_far + swaps
    for c in sent:
        c.wait_send()
    for c in stores:
        c.wait()
    wait_near(slabs, slab_at(x, high), out_s.at[0], out_r.at[0], True, sends_own, 2)
    wait_far(slabs, slab_at(x, high_far), out_s.at[1], out_r.at[1], True)
    wait_near(back, high * nq, back_s.at[0], back_r.at[0], True)
    wait_far(back, high_far * nq, back_s.at[1], back_r.at[1], True)


def solution(mesh):
    nz, ny = 4, mesh.shape["wide"] // 8

    def step(*args):
        return body(nz, ny, *args)

    placed = (
        P("wide", "narrow"),
        P("wide", "narrow"),
        P("wide", "narrow"),
        P("wide", "narrow"),
        P("narrow", "wide", None),
        P("narrow", "wide", None),
        P("narrow", "wide", None),
        P(None, "wide", "narrow"),
        P(None, "wide", "narrow"),
    )
    return jax.shard_map(
        step,
        mesh=mesh,
        in_specs=placed,
        out_specs=(P("wide", "narrow"), P(None, "wide", "narrow"), P(None, "wide", "narrow")),
        check_vma=False,
    )


def body(nz, ny, *args):
    nq = nz * ny
    block, span = 32 * nq, args[1].shape[1]
    half = span // 2
    slabs = NX * NH
    dma = pltpu.SemaphoreType.DMA
    steps = ny // 2
    anywhere = pl.BlockSpec(memory_space=pl.ANY)
    args = list(args)
    args[2] = args[2].T
    args[5] = jnp.swapaxes(args[5], 1, 2)
    return pl.pallas_call(
        functools.partial(kernel, nz, ny),
        out_shape=(
            jax.ShapeDtypeStruct(args[0].shape, BF16),
            jax.ShapeDtypeStruct(args[7].shape, F32),
            jax.ShapeDtypeStruct(args[8].shape, F32),
        ),
        in_specs=[anywhere] * 9,
        out_specs=(anywhere,) * 3,
        scratch_shapes=[pltpu.VMEM(a.shape, a.dtype) for a in args + args[7:9]]
        + [
            pltpu.VMEM((256, block), BF16),
            pltpu.VMEM((2, nz, ny, 32, block // 2), BF16),
            pltpu.VMEM((2, nz // 2, ny, 2, 128, half), BF16),
            pltpu.VMEM((2, 16, block // 2), BF16),
            pltpu.VMEM((64, half), BF16),
            pltpu.VMEM((nq // 2, 2, 32, 128), BF16),
            pltpu.VMEM((slabs * nq, 32, 128), BF16),
            pltpu.VMEM((slabs * 32, span), F32),
            pltpu.VMEM((slabs * 32, span), BF16),
            pltpu.VMEM((slabs * nq, 32, 128), BF16),
            pltpu.VMEM((NH, 2, nq // 2, 32, 128), BF16),
            pltpu.VMEM((NH, 2, nq, 32, 128), BF16),
            pltpu.VMEM((NH * nq, 32, 128), BF16),
            pltpu.VMEM((NH * nq, 32, 128), BF16),
            pltpu.VMEM((nz, 2, 64, ny * 32), BF16),
            dma((11 + nz,)),
            dma((2,)),
            dma((2,)),
            dma((nz,)),
            dma((nz,)),
            dma((3,)),
            dma((3,)),
        ]
        + [dma((nz - 1, 2))] * 4
        + [dma((nz - 1,))] * 4
        + [dma((steps, nz, 2))] * 2
        + [dma((steps, 2))] * 6
        + [dma((ny + nz,))] * 2
        + [dma((2,))] * 5
        + [dma((2, 6))] * 4,
        compiler_params=pltpu.CompilerParams(
            collective_id=0, has_side_effects=True, vmem_limit_bytes=58 * 1024 * 1024
        ),
        cost_estimate=pl.CostEstimate(flops=2_700_000_000, bytes_accessed=8_000_000, transcendentals=131072),
    )(*args)
```

```python
import functools
import math

import jax
import jax.numpy as jnp
from jax import lax
from jax.experimental import pallas as pl
from jax.experimental.pallas import tpu as pltpu
from jax.sharding import PartitionSpec as P

MESH = pl.DeviceIdType.MESH
F32, BF16 = jnp.float32, jnp.bfloat16
BETA_ONE = 0.95
BETA_TWO = 0.95
EPSILON = 1e-08
NX = 4
NH = 2


def dequantized(codes, scales, error, quantum):
    groups, columns = scales.shape[0], codes.shape[1]
    column = lax.broadcasted_iota(jnp.int32, (groups, columns), 1) // (columns // groups)
    spread = (column == lax.broadcasted_iota(jnp.int32, (groups, columns), 0)).astype(F32).astype(BF16)
    expanded = lax.dot_general(
        scales.astype(F32).astype(BF16), spread, (((0,), (0,)), ((), ())), preferred_element_type=F32
    )
    return (codes.astype(F32) * expanded * quantum + error.astype(F32)).astype(BF16)


def kernel(nz, ny, *refs):
    inputs, refs = refs[:9], refs[9:]
    outputs, fetched, held, refs = refs[:3], refs[3:12], refs[12:14], refs[14:]
    update, (new_first, new_second) = outputs[0], held
    grad, lcodes, lscales, lerror, rcodes, rscales, rerror, first, second = fetched
    (
        turned,
        right,
        left,
        rstage,
        lstage,
        outgoing,
        slabs,
        total,
        direction,
        partial,
        halfway,
        arrived,
        home,
        back,
        result,
    ) = refs[:15]
    (
        fetch_sem,
        sib_s,
        sib_r,
        swap_s,
        swap_r,
        grad_s,
        grad_r,
        zr_s,
        zr_r,
        zl_s,
        zl_r,
        za_s,
        za_r,
        zb_s,
        zb_r,
        yr_s,
        yr_r,
        late_s,
        late_r,
        ya_s,
        ya_r,
        yb_s,
        yb_r,
        share_s,
        share_r,
        out_s,
        out_r,
        back_s,
        back_r,
        own_sem,
        ring_s,
        ring_r,
        sum_s,
        sum_r,
    ) = refs[15:]
    nq = nz * ny
    block = 32 * nq
    order = 128 * nq
    span = lcodes.shape[1]
    half = span // 2
    hb = block // 2
    wide, narrow = lax.axis_index("wide"), lax.axis_index("narrow")
    core, chip = lax.rem(wide, 2), wide // 2
    z, y = chip // ny, lax.rem(chip, ny)
    x, high = narrow // NH, lax.rem(narrow, NH)
    other = 1 - core
    pair, odd = z // 2, lax.rem(z, 2)
    place = (pair * ny + y) * 2 + odd
    side = wide // nq
    has_own = side == core
    sends_own = wide // (nq // 2) == 2 * core + odd

    fetches = [pltpu.make_async_copy(a, b, fetch_sem.at[i]) for i, (a, b) in enumerate(zip(inputs, fetched))]
    for i in (4, 5, 6, 1, 2, 3, 0, 7, 8):
        fetches[i].start()

    def wide_at(zz, yy, cc):
        return (zz * ny + yy) * 2 + cc

    def copy(src, dst, send, recv, ww, nn):
        return pltpu.make_async_remote_copy(
            src_ref=src, dst_ref=dst, send_sem=send, recv_sem=recv, device_id=(ww, nn), device_id_type=MESH
        )

    def start(copies):
        for c in copies:
            c.start()

    def landed(copies):
        for c in copies:
            c.wait_recv()

    sibling = wide + 1 - 2 * core
    y_up, y_down = lax.rem(y + 1, ny), lax.rem(y + ny - 1, ny)
    x_up, x_down = lax.rem(x + 1, NX), lax.rem(x + NX - 1, NX)
    x_far = lax.rem(x + 2, NX)
    n_up, n_down = x_up * NH + high, x_down * NH + high
    w_up, w_down = wide_at(z, y_up, core), wide_at(z, y_down, core)

    barrier = pltpu.get_barrier_semaphore()
    plane = 2 * nq * NH

    for extra in range(NH):
        nn = x * NH + lax.rem(high + extra, NH)

        def greet(i, carry):
            there = wide + i
            there = jnp.where(there >= 2 * nq, there - 2 * nq, there)
            pl.semaphore_signal(barrier, inc=1, device_id=(there, nn), device_id_type=MESH)
            return carry

        lax.fori_loop(1 if extra == 0 else 0, 2 * nq, greet, 0)
    for nn in (n_up, n_down):
        pl.semaphore_signal(barrier, inc=1, device_id=(wide, nn), device_id_type=MESH)

    rows16 = pl.ds(pl.multiple_of(core * 16, 16), 16)
    rows64 = pl.ds(pl.multiple_of(core * 64, 64), 64)
    quantum = 1.0 / (16.0 * math.sqrt(block))
    for i in (4, 5, 6):
        fetches[i].wait()
    for ref, which in ((rstage, other), (right.at[:, z, y, rows16, :], core)):
        value = dequantized(rcodes[which], rscales[which], rerror[which], quantum)
        for h in range(2):
            ref[h] = value[:, h * hb : (h + 1) * hb]
    pl.semaphore_wait(barrier, plane - 1 + 2)
    sib = [
        copy(rstage, right.at[:, z, y, rows16, :], sib_s.at[0], sib_r.at[0], sibling, narrow),
        copy(lstage, left.at[other, pair, y, odd, rows64, :], sib_s.at[1], sib_r.at[1], sibling, narrow),
    ]
    rows_g = pl.ds(pl.multiple_of(odd * 128 + core * 64, 64), 64)
    beside = wide_at(z + 1 - 2 * odd, y, core)
    own_block = grad.at[:, pl.ds(pl.multiple_of(core * block, block), block)]
    other_block = grad.at[:, pl.ds(pl.multiple_of(other * block, block), block)]
    rows_out = [
        copy(other_block, turned.at[rows_g, :], grad_s.at[0], grad_r.at[0], sibling, narrow),
        copy(own_block, turned.at[rows_g, :], grad_s.at[1], grad_r.at[1], beside, narrow),
        copy(other_block, turned.at[rows_g, :], grad_s.at[2], grad_r.at[2], beside + 1 - 2 * core, narrow),
    ]
    last = ny // 2

    def along_z(ref_for, send, recv):
        made = []
        for d in range(1, nz):
            ref = ref_for(lax.rem(z + d, nz))
            made.append(copy(ref, ref, send.at[d - 1], recv.at[d - 1], wide_at(lax.rem(z + d, nz), y, core), narrow))
        return made

    def passed(t):
        return lax.rem(y + ny - (t - 1), ny), lax.rem(y + (t - 1), ny)

    nearest = [0, 1, nz - 1][: min(nz, 3)] + list(range(2, nz - 1))
    if nz == 2:
        nearest = [0, 1]
    def rows_to_line(which, send, recv):
        made = []
        for d in range(1, nz):
            zz = lax.rem(z + d, nz)
            h = lax.rem(zz + which, 2)
            dst = right.at[h, z, y, rows16, :]
            both = ((dst, core), (rstage.at[h], other))
            made.append(
                [
                    copy(src, dst, send.at[d - 1, i], recv.at[d - 1, i], wide_at(zz, y, cc), narrow)
                    for i, (src, cc) in enumerate(both)
                ]
            )
        return made

    zr = rows_to_line(0, zr_s, zr_r)
    zlate = rows_to_line(1, zl_s, zl_r)

    sib[0].start()
    for e in nearest[1:]:
        start(zr[e - 1])
    quantum = 1.0 / (16.0 * math.sqrt(order))
    for i in (1, 2, 3):
        fetches[i].wait()
    value = dequantized(lcodes[...], lscales[...], lerror[...], quantum)
    for h in range(2):

        @pl.when(core == h)
        def _():
            left[h, pair, y, odd, rows64, :] = value[:, h * half : (h + 1) * half]

        @pl.when(core != h)
        def _():
            lstage[...] = value[:, h * half : (h + 1) * half]

    sib[1].start()

    def ring_right(t, e):
        zz = lax.rem(z + nz - e, nz)
        at = nearest.index(e)
        made = []
        for way, (yy, ww) in enumerate(zip(passed(t), (w_up, w_down))):
            if t < last or (at < nz // 2) == (way == 0):
                ref = right.at[odd, zz, yy]
                made.append(copy(ref, ref, yr_s.at[t - 1, e, way], yr_r.at[t - 1, e, way], ww, narrow))
        return made

    yr = [[ring_right(t, e) for e in nearest] for t in range(1, last + 1)]

    ra = 112
    rb = 128 - ra

    def rows_a(yy, zs=slice(None)):
        return left.at[core, :, yy, zs, pl.ds(0, ra)]

    def rows_b(yy, begin=0, size=rb):
        return left.at[core, pair, yy, odd, pl.ds(ra + begin, size)]

    own_a = left.at[core, pair, y, odd, pl.ds(0, ra)]
    za = along_z(lambda zz: own_a, za_s, za_r)
    zb = along_z(lambda zz: rows_b(pl.ds(0, ny)), zb_s, zb_r)
    ya, yb, late = [], [], []

    def both_ways(t, a, b, send, recv):
        return [
            copy(a, a, send.at[t - 1, 0], recv.at[t - 1, 0], w_up, narrow),
            copy(b, b, send.at[t - 1, 1], recv.at[t - 1, 1], w_down, narrow),
        ]

    for t in range(1, last + 1):
        up, down = passed(t)
        if t < last:
            a, b = rows_a(up), rows_a(down)
        else:
            a, b = rows_a(up, pl.ds(0, 1)), rows_a(down, pl.ds(1, 1))
        ya.append(both_ways(t, a, b, ya_s, ya_r))
        yb.append(both_ways(t, rows_b(up), rows_b(down), yb_s, yb_r)[: 2 if t < last else 1])
        zs = (pl.ds(0, nz), pl.ds(0, nz)) if t < last else (pl.ds(0, nz // 2), pl.ds(nz // 2, nz // 2))
        a, b = right.at[1 - odd, zs[0], up], right.at[1 - odd, zs[1], down]
        late.append(both_ways(t, a, b, late_s, late_r))
    shares = []

    def share(ref):
        at = len(shares)
        c = copy(ref, ref, share_s.at[at], share_r.at[at], sibling, narrow)
        c.start()
        shares.append(c)

    sib[0].wait_recv()
    start(yr[0][0])
    fetches[0].wait()
    for h in range(2):

        @pl.when(core == h)
        def _():
            turned[rows_g, :] = grad[:, h * block : (h + 1) * block]

    start(rows_out)
    sib[1].wait_recv()
    start(yb[0])
    start(za)
    for at, e in enumerate(nearest):
        if at > 0:
            landed(zr[e - 1])
            start(yr[0][at])
    for part in zlate:
        start(part)
    b_step = 1

    def next_b(t):
        landed(yb[t - 1])
        if t < last:
            start(yb[t])
        else:
            start(zb)
            share(rows_b(pl.ds(0, ny)))

    for t in range(2, last + 1):
        for at in range(nz):
            landed(yr[t - 2][at])
            start(yr[t - 1][at])
            if at % 2 == 1 and b_step <= last and t < last:
                next_b(b_step)
                b_step += 1
    while b_step <= last:
        next_b(b_step)
        b_step += 1
    landed(za)
    start(ya[0])
    share(rows_a(y))
    for at in range(nz):
        landed(yr[last - 1][at])

    landed(rows_out)
    lands = slabs.at[pl.ds(narrow * nq + place - odd, 2)]
    high_far = 1 - high
    n_far = x * NH + high_far
    first_to = (nq // 2) * (2 * core + odd)

    wide_n = min(256, hb)
    some = wide_n // 32

    def send_near(begin, t, carry):
        j = begin + lax.rem(2 * y + pair + t, some)
        to = first_to + j

        @pl.when(to != wide)
        def _():
            copy(outgoing.at[j], lands, out_s.at[0], out_r.at[0], to, narrow).start()

        @pl.when(to == wide)
        def _():
            pltpu.make_async_copy(outgoing.at[j], lands, own_sem.at[0]).start()

        return carry

    def send_far(t, carry):
        j = lax.rem(2 * y + pair + t, nq // 2)
        copy(outgoing.at[j], lands, out_s.at[1], out_r.at[1], first_to + j, n_far).start()
        return carry

    for at in range(0, hb, wide_n):
        basis = right[odd, :, :, :, at : at + wide_n].reshape(block, wide_n)
        value = jnp.dot(turned[...], basis, preferred_element_type=F32).T.astype(BF16)
        for d in range(2):
            outgoing[at // 32 : at // 32 + some, d] = value[:, d * 128 : (d + 1) * 128].reshape(some, 32, 128)
        lax.fori_loop(0, some, functools.partial(send_near, at // 32), 0)
    lax.fori_loop(0, nq // 2, send_far, 0)

    def wait_near(ref, base, send, recv, sending, some_own=has_own, own_many=1):
        def wait(many):
            there = ref.at[pl.ds(base, many)]
            c = copy(there, there, send, recv, sibling, narrow)
            if sending:
                c.wait_send()
            else:
                c.wait_recv()

        @pl.when(some_own)
        def _():
            wait(nq - own_many)

        @pl.when(jnp.logical_not(some_own))
        def _():
            wait(nq)

    def wait_far(ref, base, send, recv, sending):
        there = ref.at[pl.ds(base, nq)]
        c = copy(there, there, send, recv, sibling, narrow)
        if sending:
            c.wait_send()
        else:
            c.wait_recv()

    def next_a(t):
        landed(ya[t - 1])
        if t < last:
            start(ya[t])
            for yy in passed(t + 1):
                share(rows_a(yy))
        else:
            share(rows_a(lax.rem(y + last, ny)))

    hq = nq // 2

    def slab_at(xx, g):
        return (xx * NH + g) * nq

    def ring_x(g, at):
        own = [slabs.at[pl.ds(slab_at(x, g) + h * hq, hq)] for h in range(2)]
        from_down = slabs.at[pl.ds(slab_at(x_down, g), hq)]
        from_up = slabs.at[pl.ds(slab_at(x_up, g) + hq, hq)]
        made = [
            (own[0], n_up),
            (own[1], n_down),
            (own[1], n_up),
            (own[0], n_down),
            (from_down, n_up),
            (from_up, n_down),
        ]
        return [copy(a, a, ring_s.at[at, i], ring_r.at[at, i], wide, nn) for i, (a, nn) in enumerate(made)]

    ring_near, ring_far = ring_x(high, 0), ring_x(high_far, 1)
    next_a(1)
    wait_near(slabs, slab_at(x, high), out_s.at[0], out_r.at[0], False, sends_own, 2)

    @pl.when(sends_own)
    def _():
        pltpu.make_async_copy(outgoing.at[0], lands, own_sem.at[0]).wait()

    start(ring_near[:4])
    if last > 1:
        next_a(2)
    landed(ring_near[:2])
    start(ring_near[4:])
    if last > 2:
        next_a(3)
    wait_far(slabs, slab_at(x, high_far), out_s.at[1], out_r.at[1], False)
    start(ring_far[:4])
    for t in range(4, last + 1):
        next_a(t)
    landed(zb)
    for d in range(1, nz):
        zz = lax.rem(z + nz - d, nz)
        share(left.at[core, zz // 2, pl.ds(0, ny), lax.rem(zz, 2), pl.ds(ra, rb)])
    landed(ring_far[:2])
    start(ring_far[4:])
    for part in zlate:
        landed(part)
    start(late[0])
    landed(ring_near[2:])
    landed(shares)
    landed(ring_far[2:])

    total[...] = jnp.zeros_like(total)
    deep = 4

    def rotate(i, carry):
        at = i * deep
        zz, yy = i // (2 * ny // deep), lax.rem(i, 2 * ny // deep) * (deep // 2)
        lhs = jnp.concatenate(
            [
                jnp.concatenate([slabs[s * nq + at + d] for s in range(NX * NH)], axis=0)
                for d in range(deep)
            ],
            axis=1,
        )
        for h in range(2):
            rhs = left[h, zz, pl.ds(yy, deep // 2)].reshape(deep * 128, half)
            total[:, h * half : (h + 1) * half] += jnp.dot(lhs, rhs, preferred_element_type=F32)
        return carry

    def next_late(t):
        landed(late[t - 1])
        if t < last:
            start(late[t])

    lax.fori_loop(0, nq // deep, rotate, 0)
    fetches[7].wait()
    fetches[8].wait()

    def moments(s, carry):
        there = pl.ds(pl.multiple_of(s * 32, 32), 32)
        value = total[there, :]
        m = BETA_ONE * first[s] + (1.0 - BETA_ONE) * value
        v = BETA_TWO * second[s] + (1.0 - BETA_TWO) * value * value
        new_first[s] = m
        new_second[s] = v
        direction[there, :] = (m / (jnp.sqrt(v) + EPSILON)).astype(BF16)
        return carry

    lax.fori_loop(0, NX * NH, moments, 0)
    stores = [pltpu.make_async_copy(held[i], outputs[1 + i], fetch_sem.at[9 + i]) for i in range(2)]
    for c in stores:
        c.start()

    def rotate_back(i, carry):
        at = i * 2
        zz, yy = i // ny, lax.rem(i, ny)
        value = None
        for h in range(2):
            rhs = left[h, zz, yy].reshape(256, half)
            term = lax.dot_general(
                direction[:, h * half : (h + 1) * half],
                rhs,
                (((1,), (1,)), ((), ())),
                preferred_element_type=F32,
            )
            value = term if value is None else value + term
        value = value.astype(BF16)
        for s in range(NX * NH):
            for d in range(2):
                partial[s * nq + at + d] = value[s * 32 : (s + 1) * 32, d * 128 : (d + 1) * 128]
        return carry

    def sums_of(g, at):
        def part(xx, h):
            return partial.at[pl.ds(slab_at(xx, g) + h * hq, hq)]

        lower, upper = pl.ds(0, hq), pl.ds(hq, hq)
        made = [
            (part(x_far, 0), halfway.at[at, 0], n_up),
            (part(x_far, 1), halfway.at[at, 1], n_down),
            (part(x_down, 0), arrived.at[at, 1, lower], n_down),
            (part(x_up, 1), arrived.at[at, 0, upper], n_up),
            (part(x_up, 0), arrived.at[at, 0, lower], n_up),
            (part(x_down, 1), arrived.at[at, 1, upper], n_down),
        ]
        return [copy(a, b, sum_s.at[at, i], sum_r.at[at, i], wide, nn) for i, (a, b, nn) in enumerate(made)]

    sums_far, sums_near = sums_of(high_far, 0), sums_of(high, 1)
    few = min(8, hq)

    def pass_on(g, at):
        def some(i, carry):
            for h, base in ((0, slab_at(x_up, g)), (1, slab_at(x_down, g) + hq)):
                there = pl.ds(base + i * few, few)
                held = halfway[at, h, pl.ds(i * few, few)]
                partial[there] = (partial[there].astype(F32) + held.astype(F32)).astype(BF16)
            return carry

        lax.fori_loop(0, hq // few, some, 0)

    def add_up(g, at):
        def some(i, carry):
            there = pl.ds(i * few, few)
            value = partial[pl.ds(slab_at(x, g) + i * few, few)].astype(F32) + arrived[at, 0, there].astype(F32)
            home[pl.ds(at * nq + i * few, few)] = (value + arrived[at, 1, there].astype(F32)).astype(BF16)
            return carry

        lax.fori_loop(0, nq // few, some, 0)

    lax.fori_loop(0, nq // 4, rotate_back, 0)
    start((sums_far[0], sums_far[2]))
    lax.fori_loop(nq // 4, nq // 2, rotate_back, 0)
    start((sums_far[1], sums_far[3]))
    start(sums_near[:2])
    next_late(1)
    landed(sums_far[:2])
    pass_on(high_far, 0)
    start(sums_far[4:])
    start(sums_near[2:4])
    if last > 1:
        next_late(2)
    landed(sums_near[:2])
    pass_on(high, 1)
    start(sums_near[4:])
    for t in range(3, last):
        next_late(t)

    goes_to = high * nq + lax.rem(wide, nq)

    def owner(at):
        zz, yy = at // (2 * ny) * 2 + lax.rem(at, 2), lax.rem(at // 2, ny)
        return wide_at(zz, yy, side)

    def back_far(t, carry):
        at = lax.rem(place + t, nq)
        copy(home.at[at], back.at[goes_to], back_s.at[1], back_r.at[1], owner(at), n_far).start()
        return carry

    def back_near(t, carry):
        at = lax.rem(place + t, nq)
        to = owner(at)
        src = home.at[nq + at]

        @pl.when(to != wide)
        def _():
            copy(src, back.at[goes_to], back_s.at[0], back_r.at[0], to, narrow).start()

        @pl.when(to == wide)
        def _():
            pltpu.make_async_copy(src, back.at[goes_to], own_sem.at[1]).start()

        return carry

    landed(sums_far[2:])
    add_up(high_far, 0)
    lax.fori_loop(0, nq, back_far, 0)
    landed(sums_near[2:])
    add_up(high, 1)
    lax.fori_loop(0, nq, back_near, 0)
    if last > 2:
        next_late(last)
    wait_far(back, high_far * nq, back_s.at[1], back_r.at[1], False)
    wait_near(back, high * nq, back_s.at[0], back_r.at[0], False)

    @pl.when(has_own)
    def _():
        pltpu.make_async_copy(home.at[0], back.at[goes_to], own_sem.at[1]).wait()

    turned_back = (back[0:nq].astype(F32) + back[nq : 2 * nq].astype(F32)).astype(BF16).reshape(block, 128)
    tall = ny * 32
    swaps = []
    for zz in range(nz):
        value = sum(
            jnp.dot(
                right[h, zz].reshape(tall, hb), turned_back[h * hb : (h + 1) * hb], preferred_element_type=F32
            )
            for h in range(2)
        )
        value = value.T.astype(BF16)
        result[zz, 0] = value[0:64]
        result[zz, 1] = value[64:128]
        there = update.at[:, pl.ds(pl.multiple_of(core * block + zz * tall, tall), tall)]
        swap = copy(result.at[zz, other], there, swap_s.at[zz], swap_r.at[zz], sibling, narrow)
        swap.start()
        swaps.append(swap)
        store = pltpu.make_async_copy(result.at[zz, core], there, fetch_sem.at[11 + zz])
        store.start()
        stores.append(store)
    landed(swaps)

    sent = sib + rows_out + za + zb + [c for part in zr + zlate for c in part] + [c for step in yr for part in step for c in part]
    sent += [c for part in ya + yb + late for c in part] + shares + ring_near + ring_far + sums_near + sums_far + swaps
    for c in sent:
        c.wait_send()
    for c in stores:
        c.wait()
    wait_near(slabs, slab_at(x, high), out_s.at[0], out_r.at[0], True, sends_own, 2)
    wait_far(slabs, slab_at(x, high_far), out_s.at[1], out_r.at[1], True)
    wait_near(back, high * nq, back_s.at[0], back_r.at[0], True)
    wait_far(back, high_far * nq, back_s.at[1], back_r.at[1], True)


def solution(mesh):
    nz, ny = 4, mesh.shape["wide"] // 8

    def step(*args):
        return body(nz, ny, *args)

    placed = (
        P("wide", "narrow"),
        P("wide", "narrow"),
        P("wide", "narrow"),
        P("wide", "narrow"),
        P("narrow", "wide", None),
        P("narrow", "wide", None),
        P("narrow", "wide", None),
        P(None, "wide", "narrow"),
        P(None, "wide", "narrow"),
    )
    return jax.shard_map(
        step,
        mesh=mesh,
        in_specs=placed,
        out_specs=(P("wide", "narrow"), P(None, "wide", "narrow"), P(None, "wide", "narrow")),
        check_vma=False,
    )


def body(nz, ny, *args):
    nq = nz * ny
    block, span = 32 * nq, args[1].shape[1]
    half = span // 2
    slabs = NX * NH
    dma = pltpu.SemaphoreType.DMA
    steps = ny // 2
    anywhere = pl.BlockSpec(memory_space=pl.ANY)
    args = list(args)
    args[2] = args[2].T
    args[5] = jnp.swapaxes(args[5], 1, 2)
    return pl.pallas_call(
        functools.partial(kernel, nz, ny),
        out_shape=(
            jax.ShapeDtypeStruct(args[0].shape, BF16),
            jax.ShapeDtypeStruct(args[7].shape, F32),
            jax.ShapeDtypeStruct(args[8].shape, F32),
        ),
        in_specs=[anywhere] * 9,
        out_specs=(anywhere,) * 3,
        scratch_shapes=[pltpu.VMEM(a.shape, a.dtype) for a in args + args[7:9]]
        + [
            pltpu.VMEM((256, block), BF16),
            pltpu.VMEM((2, nz, ny, 32, block // 2), BF16),
            pltpu.VMEM((2, nz // 2, ny, 2, 128, half), BF16),
            pltpu.VMEM((2, 16, block // 2), BF16),
            pltpu.VMEM((64, half), BF16),
            pltpu.VMEM((nq // 2, 2, 32, 128), BF16),
            pltpu.VMEM((slabs * nq, 32, 128), BF16),
            pltpu.VMEM((slabs * 32, span), F32),
            pltpu.VMEM((slabs * 32, span), BF16),
            pltpu.VMEM((slabs * nq, 32, 128), BF16),
            pltpu.VMEM((NH, 2, nq // 2, 32, 128), BF16),
            pltpu.VMEM((NH, 2, nq, 32, 128), BF16),
            pltpu.VMEM((NH * nq, 32, 128), BF16),
            pltpu.VMEM((NH * nq, 32, 128), BF16),
            pltpu.VMEM((nz, 2, 64, ny * 32), BF16),
            dma((11 + nz,)),
            dma((2,)),
            dma((2,)),
            dma((nz,)),
            dma((nz,)),
            dma((3,)),
            dma((3,)),
        ]
        + [dma((nz - 1, 2))] * 4
        + [dma((nz - 1,))] * 4
        + [dma((steps, nz, 2))] * 2
        + [dma((steps, 2))] * 6
        + [dma((ny + nz,))] * 2
        + [dma((2,))] * 5
        + [dma((2, 6))] * 4,
        compiler_params=pltpu.CompilerParams(
            collective_id=0, has_side_effects=True, vmem_limit_bytes=58 * 1024 * 1024
        ),
        cost_estimate=pl.CostEstimate(flops=2_700_000_000, bytes_accessed=8_000_000, transcendentals=131072),
    )(*args)
```

```python
import functools
import math

import jax
import jax.numpy as jnp
from jax import lax
from jax.experimental import pallas as pl
from jax.experimental.pallas import tpu as pltpu
from jax.sharding import PartitionSpec as P

MESH = pl.DeviceIdType.MESH
F32, BF16 = jnp.float32, jnp.bfloat16
BETA_ONE = 0.95
BETA_TWO = 0.95
EPSILON = 1e-08
NX = 4
NH = 2


def dequantized(codes, scales, error, quantum):
    groups, columns = scales.shape[0], codes.shape[1]
    column = lax.broadcasted_iota(jnp.int32, (groups, columns), 1) // (columns // groups)
    spread = (column == lax.broadcasted_iota(jnp.int32, (groups, columns), 0)).astype(F32).astype(BF16)
    expanded = lax.dot_general(
        scales.astype(F32).astype(BF16), spread, (((0,), (0,)), ((), ())), preferred_element_type=F32
    )
    return (codes.astype(F32) * expanded * quantum + error.astype(F32)).astype(BF16)


def kernel(nz, ny, *refs):
    inputs, refs = refs[:9], refs[9:]
    outputs, fetched, held, refs = refs[:3], refs[3:12], refs[12:14], refs[14:]
    update, (new_first, new_second) = outputs[0], held
    grad, lcodes, lscales, lerror, rcodes, rscales, rerror, first, second = fetched
    (
        turned,
        right,
        left,
        rstage,
        lstage,
        outgoing,
        slabs,
        total,
        direction,
        partial,
        halfway,
        arrived,
        home,
        back,
        result,
    ) = refs[:15]
    (
        fetch_sem,
        sib_s,
        sib_r,
        swap_s,
        swap_r,
        grad_s,
        grad_r,
        zr_s,
        zr_r,
        zl_s,
        zl_r,
        za_s,
        za_r,
        zb_s,
        zb_r,
        yr_s,
        yr_r,
        late_s,
        late_r,
        ya_s,
        ya_r,
        yb_s,
        yb_r,
        share_s,
        share_r,
        out_s,
        out_r,
        back_s,
        back_r,
        own_sem,
        ring_s,
        ring_r,
        sum_s,
        sum_r,
    ) = refs[15:]
    nq = nz * ny
    block = 32 * nq
    order = 128 * nq
    span = lcodes.shape[1]
    half = span // 2
    hb = block // 2
    wide, narrow = lax.axis_index("wide"), lax.axis_index("narrow")
    core, chip = lax.rem(wide, 2), wide // 2
    z, y = chip // ny, lax.rem(chip, ny)
    x, high = narrow // NH, lax.rem(narrow, NH)
    other = 1 - core
    pair, odd = z // 2, lax.rem(z, 2)
    place = (pair * ny + y) * 2 + odd
    side = wide // nq
    has_own = side == core
    sends_own = wide // (nq // 2) == 2 * core + odd

    fetches = [pltpu.make_async_copy(a, b, fetch_sem.at[i]) for i, (a, b) in enumerate(zip(inputs, fetched))]
    for i in (4, 5, 6, 1, 2, 3, 0, 7, 8):
        fetches[i].start()

    def wide_at(zz, yy, cc):
        return (zz * ny + yy) * 2 + cc

    def copy(src, dst, send, recv, ww, nn):
        return pltpu.make_async_remote_copy(
            src_ref=src, dst_ref=dst, send_sem=send, recv_sem=recv, device_id=(ww, nn), device_id_type=MESH
        )

    def start(copies):
        for c in copies:
            c.start()

    def landed(copies):
        for c in copies:
            c.wait_recv()

    sibling = wide + 1 - 2 * core
    y_up, y_down = lax.rem(y + 1, ny), lax.rem(y + ny - 1, ny)
    x_up, x_down = lax.rem(x + 1, NX), lax.rem(x + NX - 1, NX)
    x_far = lax.rem(x + 2, NX)
    n_up, n_down = x_up * NH + high, x_down * NH + high
    w_up, w_down = wide_at(z, y_up, core), wide_at(z, y_down, core)

    barrier = pltpu.get_barrier_semaphore()
    plane = 2 * nq * NH

    for extra in range(NH):
        nn = x * NH + lax.rem(high + extra, NH)

        def greet(i, carry):
            there = wide + i
            there = jnp.where(there >= 2 * nq, there - 2 * nq, there)
            pl.semaphore_signal(barrier, inc=1, device_id=(there, nn), device_id_type=MESH)
            return carry

        lax.fori_loop(1 if extra == 0 else 0, 2 * nq, greet, 0)
    for nn in (n_up, n_down):
        pl.semaphore_signal(barrier, inc=1, device_id=(wide, nn), device_id_type=MESH)

    rows16 = pl.ds(pl.multiple_of(core * 16, 16), 16)
    rows64 = pl.ds(pl.multiple_of(core * 64, 64), 64)
    quantum = 1.0 / (16.0 * math.sqrt(block))
    for i in (4, 5, 6):
        fetches[i].wait()
    for ref, which in ((rstage, other), (right.at[:, z, y, rows16, :], core)):
        value = dequantized(rcodes[which], rscales[which], rerror[which], quantum)
        for h in range(2):
            ref[h] = value[:, h * hb : (h + 1) * hb]
    pl.semaphore_wait(barrier, plane - 1 + 2)
    sib = [
        copy(rstage, right.at[:, z, y, rows16, :], sib_s.at[0], sib_r.at[0], sibling, narrow),
        copy(lstage, left.at[other, pair, y, odd, rows64, :], sib_s.at[1], sib_r.at[1], sibling, narrow),
    ]
    rows_g = pl.ds(pl.multiple_of(odd * 128 + core * 64, 64), 64)
    beside = wide_at(z + 1 - 2 * odd, y, core)
    own_block = grad.at[:, pl.ds(pl.multiple_of(core * block, block), block)]
    other_block = grad.at[:, pl.ds(pl.multiple_of(other * block, block), block)]
    rows_out = [
        copy(other_block, turned.at[rows_g, :], grad_s.at[0], grad_r.at[0], sibling, narrow),
        copy(own_block, turned.at[rows_g, :], grad_s.at[1], grad_r.at[1], beside, narrow),
        copy(other_block, turned.at[rows_g, :], grad_s.at[2], grad_r.at[2], beside + 1 - 2 * core, narrow),
    ]
    last = ny // 2

    def along_z(ref_for, send, recv):
        made = []
        for d in range(1, nz):
            ref = ref_for(lax.rem(z + d, nz))
            made.append(copy(ref, ref, send.at[d - 1], recv.at[d - 1], wide_at(lax.rem(z + d, nz), y, core), narrow))
        return made

    def passed(t):
        return lax.rem(y + ny - (t - 1), ny), lax.rem(y + (t - 1), ny)

    nearest = [0, 1, nz - 1][: min(nz, 3)] + list(range(2, nz - 1))
    if nz == 2:
        nearest = [0, 1]
    def rows_to_line(which, send, recv):
        made = []
        for d in range(1, nz):
            zz = lax.rem(z + d, nz)
            h = lax.rem(zz + which, 2)
            dst = right.at[h, z, y, rows16, :]
            both = ((dst, core), (rstage.at[h], other))
            made.append(
                [
                    copy(src, dst, send.at[d - 1, i], recv.at[d - 1, i], wide_at(zz, y, cc), narrow)
                    for i, (src, cc) in enumerate(both)
                ]
            )
        return made

    zr = rows_to_line(0, zr_s, zr_r)
    zlate = rows_to_line(1, zl_s, zl_r)

    sib[0].start()
    for e in nearest[1:]:
        start(zr[e - 1])
    quantum = 1.0 / (16.0 * math.sqrt(order))
    for i in (1, 2, 3):
        fetches[i].wait()
    value = dequantized(lcodes[...], lscales[...], lerror[...], quantum)
    for h in range(2):

        @pl.when(core == h)
        def _():
            left[h, pair, y, odd, rows64, :] = value[:, h * half : (h + 1) * half]

        @pl.when(core != h)
        def _():
            lstage[...] = value[:, h * half : (h + 1) * half]

    sib[1].start()

    def ring_right(t, e):
        zz = lax.rem(z + nz - e, nz)
        at = nearest.index(e)
        made = []
        for way, (yy, ww) in enumerate(zip(passed(t), (w_up, w_down))):
            if t < last or (at < nz // 2) == (way == 0):
                ref = right.at[odd, zz, yy]
                made.append(copy(ref, ref, yr_s.at[t - 1, e, way], yr_r.at[t - 1, e, way], ww, narrow))
        return made

    yr = [[ring_right(t, e) for e in nearest] for t in range(1, last + 1)]

    ra = 112
    rb = 128 - ra

    def rows_a(yy, zs=slice(None)):
        return left.at[core, :, yy, zs, pl.ds(0, ra)]

    def rows_b(yy, begin=0, size=rb):
        return left.at[core, pair, yy, odd, pl.ds(ra + begin, size)]

    own_a = left.at[core, pair, y, odd, pl.ds(0, ra)]
    za = along_z(lambda zz: own_a, za_s, za_r)
    zb = along_z(lambda zz: rows_b(pl.ds(0, ny)), zb_s, zb_r)
    ya, yb, late = [], [], []

    def both_ways(t, a, b, send, recv):
        return [
            copy(a, a, send.at[t - 1, 0], recv.at[t - 1, 0], w_up, narrow),
            copy(b, b, send.at[t - 1, 1], recv.at[t - 1, 1], w_down, narrow),
        ]

    for t in range(1, last + 1):
        up, down = passed(t)
        if t < last:
            a, b = rows_a(up), rows_a(down)
        else:
            a, b = rows_a(up, pl.ds(0, 1)), rows_a(down, pl.ds(1, 1))
        ya.append(both_ways(t, a, b, ya_s, ya_r))
        yb.append(both_ways(t, rows_b(up), rows_b(down), yb_s, yb_r)[: 2 if t < last else 1])
        zs = (pl.ds(0, nz), pl.ds(0, nz)) if t < last else (pl.ds(0, nz // 2), pl.ds(nz // 2, nz // 2))
        a, b = right.at[1 - odd, zs[0], up], right.at[1 - odd, zs[1], down]
        late.append(both_ways(t, a, b, late_s, late_r))
    shares = []

    def share(ref):
        at = len(shares)
        c = copy(ref, ref, share_s.at[at], share_r.at[at], sibling, narrow)
        c.start()
        shares.append(c)

    sib[0].wait_recv()
    start(yr[0][0])
    fetches[0].wait()
    for h in range(2):

        @pl.when(core == h)
        def _():
            turned[rows_g, :] = grad[:, h * block : (h + 1) * block]

    start(rows_out)
    sib[1].wait_recv()
    start(yb[0])
    start(za)
    for at, e in enumerate(nearest):
        if at > 0:
            landed(zr[e - 1])
            start(yr[0][at])
    for part in zlate:
        start(part)
    b_step = 1

    def next_b(t):
        landed(yb[t - 1])
        if t < last:
            start(yb[t])
        else:
            start(zb)
            share(rows_b(pl.ds(0, ny)))

    for t in range(2, last + 1):
        for at in range(nz):
            landed(yr[t - 2][at])
            start(yr[t - 1][at])
            if at % 2 == 1 and b_step <= last and t < last:
                next_b(b_step)
                b_step += 1
    while b_step <= last:
        next_b(b_step)
        b_step += 1
    landed(za)
    start(ya[0])
    share(rows_a(y))
    for at in range(nz):
        landed(yr[last - 1][at])

    landed(rows_out)
    lands = slabs.at[pl.ds(narrow * nq + place - odd, 2)]
    high_far = 1 - high
    n_far = x * NH + high_far
    first_to = (nq // 2) * (2 * core + odd)

    def next_a(t):
        landed(ya[t - 1])
        if t < last:
            start(ya[t])
            for yy in passed(t + 1):
                share(rows_a(yy))
        else:
            share(rows_a(lax.rem(y + last, ny)))

    wide_n = min(256, hb)
    some = wide_n // 32

    def send_near(begin, t, carry):
        j = begin + lax.rem(2 * y + pair + t, some)
        to = first_to + j

        @pl.when(to != wide)
        def _():
            copy(outgoing.at[j], lands, out_s.at[0], out_r.at[0], to, narrow).start()

        @pl.when(to == wide)
        def _():
            pltpu.make_async_copy(outgoing.at[j], lands, own_sem.at[0]).start()

        return carry

    def send_far(t, carry):
        j = lax.rem(2 * y + pair + t, nq // 2)
        copy(outgoing.at[j], lands, out_s.at[1], out_r.at[1], first_to + j, n_far).start()
        return carry

    for at in range(0, hb, wide_n):
        basis = right[odd, :, :, :, at : at + wide_n].reshape(block, wide_n)
        value = jnp.dot(turned[...], basis, preferred_element_type=F32).T.astype(BF16)
        for d in range(2):
            outgoing[at // 32 : at // 32 + some, d] = value[:, d * 128 : (d + 1) * 128].reshape(some, 32, 128)
        lax.fori_loop(0, some, functools.partial(send_near, at // 32), 0)
        if at == 0:
            next_a(1)
    lax.fori_loop(0, nq // 2, send_far, 0)

    def wait_near(ref, base, send, recv, sending, some_own=has_own, own_many=1):
        def wait(many):
            there = ref.at[pl.ds(base, many)]
            c = copy(there, there, send, recv, sibling, narrow)
            if sending:
                c.wait_send()
            else:
                c.wait_recv()

        @pl.when(some_own)
        def _():
            wait(nq - own_many)

        @pl.when(jnp.logical_not(some_own))
        def _():
            wait(nq)

    def wait_far(ref, base, send, recv, sending):
        there = ref.at[pl.ds(base, nq)]
        c = copy(there, there, send, recv, sibling, narrow)
        if sending:
            c.wait_send()
        else:
            c.wait_recv()

    hq = nq // 2

    def slab_at(xx, g):
        return (xx * NH + g) * nq

    def ring_x(g, at):
        own = [slabs.at[pl.ds(slab_at(x, g) + h * hq, hq)] for h in range(2)]
        from_down = slabs.at[pl.ds(slab_at(x_down, g), hq)]
        from_up = slabs.at[pl.ds(slab_at(x_up, g) + hq, hq)]
        made = [
            (own[0], n_up),
            (own[1], n_down),
            (own[1], n_up),
            (own[0], n_down),
            (from_down, n_up),
            (from_up, n_down),
        ]
        return [copy(a, a, ring_s.at[at, i], ring_r.at[at, i], wide, nn) for i, (a, nn) in enumerate(made)]

    ring_near, ring_far = ring_x(high, 0), ring_x(high_far, 1)
    wait_near(slabs, slab_at(x, high), out_s.at[0], out_r.at[0], False, sends_own, 2)

    @pl.when(sends_own)
    def _():
        pltpu.make_async_copy(outgoing.at[0], lands, own_sem.at[0]).wait()

    start(ring_near[:4])
    if last > 1:
        next_a(2)
    if last > 2:
        next_a(3)
    landed(ring_near[:2])
    start(ring_near[4:])
    wait_far(slabs, slab_at(x, high_far), out_s.at[1], out_r.at[1], False)
    start(ring_far[:4])
    for t in range(4, last + 1):
        next_a(t)
    landed(zb)
    for d in range(1, nz):
        zz = lax.rem(z + nz - d, nz)
        share(left.at[core, zz // 2, pl.ds(0, ny), lax.rem(zz, 2), pl.ds(ra, rb)])
    landed(ring_far[:2])
    start(ring_far[4:])
    for part in zlate:
        landed(part)
    start(late[0])
    landed(ring_near[2:])
    landed(shares)
    landed(ring_far[2:])

    total[...] = jnp.zeros_like(total)
    deep = 4

    def rotate(i, carry):
        at = i * deep
        zz, yy = i // (2 * ny // deep), lax.rem(i, 2 * ny // deep) * (deep // 2)
        lhs = jnp.concatenate(
            [
                jnp.concatenate([slabs[s * nq + at + d] for s in range(NX * NH)], axis=0)
                for d in range(deep)
            ],
            axis=1,
        )
        for h in range(2):
            rhs = left[h, zz, pl.ds(yy, deep // 2)].reshape(deep * 128, half)
            total[:, h * half : (h + 1) * half] += jnp.dot(lhs, rhs, preferred_element_type=F32)
        return carry

    def next_late(t):
        landed(late[t - 1])
        if t < last:
            start(late[t])

    lax.fori_loop(0, nq // deep, rotate, 0)
    fetches[7].wait()
    fetches[8].wait()

    def moments(s, carry):
        there = pl.ds(pl.multiple_of(s * 32, 32), 32)
        value = total[there, :]
        m = BETA_ONE * first[s] + (1.0 - BETA_ONE) * value
        v = BETA_TWO * second[s] + (1.0 - BETA_TWO) * value * value
        new_first[s] = m
        new_second[s] = v
        direction[there, :] = (m / (jnp.sqrt(v) + EPSILON)).astype(BF16)
        return carry

    lax.fori_loop(0, NX * NH, moments, 0)
    stores = [pltpu.make_async_copy(held[i], outputs[1 + i], fetch_sem.at[9 + i]) for i in range(2)]
    for c in stores:
        c.start()

    def rotate_back(i, carry):
        at = i * 2
        zz, yy = i // ny, lax.rem(i, ny)
        value = None
        for h in range(2):
            rhs = left[h, zz, yy].reshape(256, half)
            term = lax.dot_general(
                direction[:, h * half : (h + 1) * half],
                rhs,
                (((1,), (1,)), ((), ())),
                preferred_element_type=F32,
            )
            value = term if value is None else value + term
        value = value.astype(BF16)
        for s in range(NX * NH):
            for d in range(2):
                partial[s * nq + at + d] = value[s * 32 : (s + 1) * 32, d * 128 : (d + 1) * 128]
        return carry

    def sums_of(g, at):
        def part(xx, h):
            return partial.at[pl.ds(slab_at(xx, g) + h * hq, hq)]

        lower, upper = pl.ds(0, hq), pl.ds(hq, hq)
        made = [
            (part(x_far, 0), halfway.at[at, 0], n_up),
            (part(x_far, 1), halfway.at[at, 1], n_down),
            (part(x_down, 0), arrived.at[at, 1, lower], n_down),
            (part(x_up, 1), arrived.at[at, 0, upper], n_up),
            (part(x_up, 0), arrived.at[at, 0, lower], n_up),
            (part(x_down, 1), arrived.at[at, 1, upper], n_down),
        ]
        return [copy(a, b, sum_s.at[at, i], sum_r.at[at, i], wide, nn) for i, (a, b, nn) in enumerate(made)]

    sums_far, sums_near = sums_of(high_far, 0), sums_of(high, 1)
    few = min(8, hq)

    def pass_on(g, at):
        def some(i, carry):
            for h, base in ((0, slab_at(x_up, g)), (1, slab_at(x_down, g) + hq)):
                there = pl.ds(base + i * few, few)
                held = halfway[at, h, pl.ds(i * few, few)]
                partial[there] = (partial[there].astype(F32) + held.astype(F32)).astype(BF16)
            return carry

        lax.fori_loop(0, hq // few, some, 0)

    def add_up(g, at):
        def some(i, carry):
            there = pl.ds(i * few, few)
            value = partial[pl.ds(slab_at(x, g) + i * few, few)].astype(F32) + arrived[at, 0, there].astype(F32)
            home[pl.ds(at * nq + i * few, few)] = (value + arrived[at, 1, there].astype(F32)).astype(BF16)
            return carry

        lax.fori_loop(0, nq // few, some, 0)

    lax.fori_loop(0, nq // 4, rotate_back, 0)
    start((sums_far[0], sums_far[2]))
    lax.fori_loop(nq // 4, nq // 2, rotate_back, 0)
    start((sums_far[1], sums_far[3]))
    start(sums_near[:2])
    next_late(1)
    landed(sums_far[:2])
    pass_on(high_far, 0)
    start(sums_far[4:])
    start(sums_near[2:4])
    if last > 1:
        next_late(2)
    landed(sums_near[:2])
    pass_on(high, 1)
    start(sums_near[4:])
    for t in range(3, last):
        next_late(t)

    goes_to = high * nq + lax.rem(wide, nq)

    def owner(at):
        zz, yy = at // (2 * ny) * 2 + lax.rem(at, 2), lax.rem(at // 2, ny)
        return wide_at(zz, yy, side)

    def back_far(t, carry):
        at = lax.rem(place + t, nq)
        copy(home.at[at], back.at[goes_to], back_s.at[1], back_r.at[1], owner(at), n_far).start()
        return carry

    def back_near(t, carry):
        at = lax.rem(place + t, nq)
        to = owner(at)
        src = home.at[nq + at]

        @pl.when(to != wide)
        def _():
            copy(src, back.at[goes_to], back_s.at[0], back_r.at[0], to, narrow).start()

        @pl.when(to == wide)
        def _():
            pltpu.make_async_copy(src, back.at[goes_to], own_sem.at[1]).start()

        return carry

    landed(sums_far[2:])
    add_up(high_far, 0)
    lax.fori_loop(0, nq, back_far, 0)
    landed(sums_near[2:])
    add_up(high, 1)
    lax.fori_loop(0, nq, back_near, 0)
    if last > 2:
        next_late(last)
    wait_far(back, high_far * nq, back_s.at[1], back_r.at[1], False)
    wait_near(back, high * nq, back_s.at[0], back_r.at[0], False)

    @pl.when(has_own)
    def _():
        pltpu.make_async_copy(home.at[0], back.at[goes_to], own_sem.at[1]).wait()

    turned_back = (back[0:nq].astype(F32) + back[nq : 2 * nq].astype(F32)).astype(BF16).reshape(block, 128)
    tall = ny * 32
    swaps = []
    for zz in range(nz):
        value = sum(
            jnp.dot(
                right[h, zz].reshape(tall, hb), turned_back[h * hb : (h + 1) * hb], preferred_element_type=F32
            )
            for h in range(2)
        )
        value = value.T.astype(BF16)
        result[zz, 0] = value[0:64]
        result[zz, 1] = value[64:128]
        there = update.at[:, pl.ds(pl.multiple_of(core * block + zz * tall, tall), tall)]
        swap = copy(result.at[zz, other], there, swap_s.at[zz], swap_r.at[zz], sibling, narrow)
        swap.start()
        swaps.append(swap)
        store = pltpu.make_async_copy(result.at[zz, core], there, fetch_sem.at[11 + zz])
        store.start()
        stores.append(store)
    landed(swaps)

    sent = sib + rows_out + za + zb + [c for part in zr + zlate for c in part] + [c for step in yr for part in step for c in part]
    sent += [c for part in ya + yb + late for c in part] + shares + ring_near + ring_far + sums_near + sums_far + swaps
    for c in sent:
        c.wait_send()
    for c in stores:
        c.wait()
    wait_near(slabs, slab_at(x, high), out_s.at[0], out_r.at[0], True, sends_own, 2)
    wait_far(slabs, slab_at(x, high_far), out_s.at[1], out_r.at[1], True)
    wait_near(back, high * nq, back_s.at[0], back_r.at[0], True)
    wait_far(back, high_far * nq, back_s.at[1], back_r.at[1], True)


def solution(mesh):
    nz, ny = 4, mesh.shape["wide"] // 8

    def step(*args):
        return body(nz, ny, *args)

    placed = (
        P("wide", "narrow"),
        P("wide", "narrow"),
        P("wide", "narrow"),
        P("wide", "narrow"),
        P("narrow", "wide", None),
        P("narrow", "wide", None),
        P("narrow", "wide", None),
        P(None, "wide", "narrow"),
        P(None, "wide", "narrow"),
    )
    return jax.shard_map(
        step,
        mesh=mesh,
        in_specs=placed,
        out_specs=(P("wide", "narrow"), P(None, "wide", "narrow"), P(None, "wide", "narrow")),
        check_vma=False,
    )


def body(nz, ny, *args):
    nq = nz * ny
    block, span = 32 * nq, args[1].shape[1]
    half = span // 2
    slabs = NX * NH
    dma = pltpu.SemaphoreType.DMA
    steps = ny // 2
    anywhere = pl.BlockSpec(memory_space=pl.ANY)
    args = list(args)
    args[2] = args[2].T
    args[5] = jnp.swapaxes(args[5], 1, 2)
    return pl.pallas_call(
        functools.partial(kernel, nz, ny),
        out_shape=(
            jax.ShapeDtypeStruct(args[0].shape, BF16),
            jax.ShapeDtypeStruct(args[7].shape, F32),
            jax.ShapeDtypeStruct(args[8].shape, F32),
        ),
        in_specs=[anywhere] * 9,
        out_specs=(anywhere,) * 3,
        scratch_shapes=[pltpu.VMEM(a.shape, a.dtype) for a in args + args[7:9]]
        + [
            pltpu.VMEM((256, block), BF16),
            pltpu.VMEM((2, nz, ny, 32, block // 2), BF16),
            pltpu.VMEM((2, nz // 2, ny, 2, 128, half), BF16),
            pltpu.VMEM((2, 16, block // 2), BF16),
            pltpu.VMEM((64, half), BF16),
            pltpu.VMEM((nq // 2, 2, 32, 128), BF16),
            pltpu.VMEM((slabs * nq, 32, 128), BF16),
            pltpu.VMEM((slabs * 32, span), F32),
            pltpu.VMEM((slabs * 32, span), BF16),
            pltpu.VMEM((slabs * nq, 32, 128), BF16),
            pltpu.VMEM((NH, 2, nq // 2, 32, 128), BF16),
            pltpu.VMEM((NH, 2, nq, 32, 128), BF16),
            pltpu.VMEM((NH * nq, 32, 128), BF16),
            pltpu.VMEM((NH * nq, 32, 128), BF16),
            pltpu.VMEM((nz, 2, 64, ny * 32), BF16),
            dma((11 + nz,)),
            dma((2,)),
            dma((2,)),
            dma((nz,)),
            dma((nz,)),
            dma((3,)),
            dma((3,)),
        ]
        + [dma((nz - 1, 2))] * 4
        + [dma((nz - 1,))] * 4
        + [dma((steps, nz, 2))] * 2
        + [dma((steps, 2))] * 6
        + [dma((ny + nz,))] * 2
        + [dma((2,))] * 5
        + [dma((2, 6))] * 4,
        compiler_params=pltpu.CompilerParams(
            collective_id=0, has_side_effects=True, vmem_limit_bytes=58 * 1024 * 1024
        ),
        cost_estimate=pl.CostEstimate(flops=2_700_000_000, bytes_accessed=8_000_000, transcendentals=131072),
    )(*args)
```
